32 devices in a mesh: row: 4 (over y, x), col: 8 (over z, core).
Axes of the slice: x: 2, y: 2, z: 4, core: 2. Of those that a mesh axis runs over, the one named last changes fastest.
Arguments:
- unfolding: float32 [1024, 4096], P('row', 'col'), may hold values from -40 to 40, as said below
- factor: float32 [1024, 64], replicated, may hold values from -6 to 6
Outputs:
- gram_lower: float32 [1024, 1024], P(('row', 'col'))
- new_factor: float32 [1024, 64], replicated
- core: float32 [64, 4096], P('row', 'col')
The draws below stay inside these ranges and needn't reach their ends.
Inputs may be any that keep to these rules, and one draw needn't show every extreme that they name: Entries of the unfolding are real values.
All inputs are finite; a program needn't handle non-finite values.
Results may differ from the reference program's by a relative error of at most 0.0003.
Values sent between devices are 32-bit elements; how exact they have to be, the bound alone decides.
No kernel may reach another device: no remote copies, remote signals or barrier semaphores. Data moves between devices by JAX's collectives and lax.ppermute only.
A program may use at most 64 MiB of HBM per device.

```python
import math
import jax
import jax.numpy as jnp
import numpy as np
from jax import lax

M = 1024
RANK = 64
COLS = 4096
HALF = 16
N_ROW = 4
N_COL = 8


def draw_unfolding(key, part):
    base = jax.random.fold_in(key, 11)
    keys = jax.random.split(base, 5)
    noise = jax.random.normal(keys[0], (M, COLS), jnp.float32)
    left = jax.random.normal(keys[1], (M, 16), jnp.float32)
    right = jax.random.normal(keys[2], (16, COLS), jnp.float32)
    weight_common = 0.3
    row_scale = jnp.exp(jax.random.uniform(keys[3], (M,), jnp.float32, math.log(0.5), math.log(3.0)))
    col_scale = jnp.exp(jax.random.uniform(keys[4], (COLS,), jnp.float32, math.log(0.5), math.log(2.0)))
    common = jnp.dot(left, right) * (weight_common / 4.0)
    values = row_scale[:, None] * (noise + common) * col_scale[None, :]
    return jnp.clip(values, -40.0, 40.0)


def bell_draw(key, shape, width, bound, held_as=jnp.bfloat16):
    array = width * jax.random.normal(key, shape, jnp.float32)
    return jnp.clip(array, min=-bound, max=bound).astype(held_as)


def setup_inputs(seed: int = 0) -> dict:
    seeds = jax.random.split(jax.random.key(seed), 3)
    unfolding = draw_unfolding(jax.random.fold_in(seeds[2], 71), 0)
    factor = bell_draw(seeds[1], (M, RANK), 1.0, 6.0, jnp.float32)
    return {"unfolding": unfolding, "factor": factor}


def folded_source(mode, half, devices):
    place = np.arange(mode)
    owner = place // (2 * half)
    inner = place % (2 * half)
    return np.where(inner < half, owner * half + inner, (2 * devices - 1 - owner) * half + inner - half)

def reference(unfolding, factor):
    highest = lax.Precision.HIGHEST
    devices = N_ROW * N_COL
    gram = jnp.dot(unfolding.astype(jnp.float32), unfolding.T.astype(jnp.float32), precision=highest, preferred_element_type=jnp.float32) / COLS
    source = jnp.asarray(folded_source(M, HALF, devices)).astype(jnp.int32)
    picked = gram[source]
    columns = jnp.arange(M, dtype=jnp.int32)
    gram_lower = jnp.where(columns[None, :] <= source[:, None], picked, jnp.float32(0.0))
    image = jnp.dot(gram.astype(jnp.float32), factor.astype(jnp.float32), precision=highest, preferred_element_type=jnp.float32)
    inner = jnp.dot(image.T.astype(jnp.float32), image.astype(jnp.float32), precision=highest, preferred_element_type=jnp.float32) / M
    chol = jnp.linalg.cholesky(inner)
    new_factor = jax.scipy.linalg.solve_triangular(chol, image.T, lower=True).T
    core = jnp.dot(new_factor.T.astype(jnp.float32), unfolding.astype(jnp.float32), precision=highest, preferred_element_type=jnp.float32) / math.sqrt(M)
    return (gram_lower, new_factor, core)
```

```python
import math

import jax
import jax.numpy as jnp
from jax import lax
from jax.sharding import PartitionSpec as P

HIGH = lax.Precision.HIGH
HIGHEST = lax.Precision.HIGHEST


def partner_pairs(n, s):
    if n & (n - 1) == 0:
        return [(i, i ^ s) for i in range(n)]
    return [(i, (i + s) % n) for i in range(n)]


def partner_source(me, n, s):
    if n & (n - 1) == 0:
        return me ^ s
    return (me + n - s) % n


def gather_blocks(x, axis):
    n = lax.axis_size(axis)
    return [x] + [lax.ppermute(x, axis, partner_pairs(n, s)) for s in range(1, n)]


def dot(a, b, dims, precision=HIGH):
    return lax.dot_general(a, b, (dims, ((), ())), precision=precision, preferred_element_type=jnp.float32)


def body(unfolding, factor):
    n_row = lax.axis_size("row")
    n_col = lax.axis_size("col")
    row = lax.axis_index("row")
    col = lax.axis_index("col")
    rows_here, cols_here = unfolding.shape
    mode = rows_here * n_row
    rank = factor.shape[1]
    total_cols = cols_here * n_col
    group = mode // (2 * n_row)
    half = group // n_col

    blocks = gather_blocks(unfolding, "row")
    x = jnp.zeros((mode, cols_here), jnp.float32)
    for s, block in enumerate(blocks):
        x = lax.dynamic_update_slice(x, block, (partner_source(row, n_row, s) * rows_here, 0))

    y = dot(factor, x, ((0,), (0,)))
    term = dot(y, x, ((1,), (1,))) * (1.0 / total_cols)
    pieces = term.reshape(rank, n_col, mode // n_col).transpose(1, 0, 2)
    swapped = lax.all_to_all(pieces, "col", split_axis=0, concat_axis=0, tiled=True)
    part = jnp.sum(swapped, axis=0)
    image_t = jnp.zeros((rank, mode), jnp.float32)
    for s, block in enumerate(gather_blocks(part, "col")):
        image_t = lax.dynamic_update_slice(image_t, block, (0, partner_source(col, n_col, s) * (mode // n_col)))

    inner = dot(image_t, image_t, ((1,), (1,)), HIGHEST) / mode
    chol = jnp.linalg.cholesky(inner)
    factor_t = jax.scipy.linalg.solve_triangular(chol, image_t, lower=True)
    new_factor = factor_t.T
    rank_here = rank // n_row
    mine = lax.dynamic_slice_in_dim(factor_t, row * rank_here, rank_here, 0)
    core = dot(mine, x, ((1,), (0,))) * (1.0 / math.sqrt(mode))

    low = lax.dynamic_slice_in_dim(x, row * group, group, 0)
    high_start = mode - (row + 1) * group
    high = lax.dynamic_slice_in_dim(x, high_start, group, 0)
    high = high.reshape(n_col, half, cols_here)[::-1].reshape(group, cols_here)
    both = dot(jnp.concatenate([high, low], 0), x, ((1,), (1,))) * (1.0 / total_cols)
    width = mode + group
    split = mode - row * group
    column = lax.broadcasted_iota(jnp.int32, (group, width), 1)
    wide_high = jnp.pad(both[:group], ((0, 0), (0, group)))
    doubled = jnp.concatenate([both[group:], both[group:], both[group:, :group]], 1)
    rolled = lax.dynamic_slice_in_dim(doubled, row * group, width, 1)
    packed = jnp.where(column < split, wide_high, rolled)
    received = lax.all_to_all(packed.reshape(n_col, half, width), "col", split_axis=0, concat_axis=0, tiled=True)
    return finish(received, x, new_factor, core, split, half, group, mode, n_col, col, row)


def finish(received, x, new_factor, core, split, half, group, mode, n_col, col, row):
    total = jnp.sum(received, axis=0)
    low_cols = lax.dynamic_slice_in_dim(jnp.pad(total, ((0, 0), (0, mode))), split, mode, 1)
    owner = row * n_col + col
    r = lax.broadcasted_iota(jnp.int32, (half, mode), 0)
    c = lax.broadcasted_iota(jnp.int32, (half, mode), 1)
    low_row = owner * half + r
    high_row = mode - (owner + 1) * half + r
    gram_lower = jnp.concatenate(
        [
            jnp.where(c <= low_row, low_cols, 0.0),
            jnp.where(c <= high_row, total[:, :mode], 0.0),
        ],
        0,
    )
    return gram_lower, new_factor, core


def solution(mesh):
    in_specs = (P("row", "col"), P())
    out_specs = (P(("row", "col"), None), P(), P("row", "col"))
    return jax.shard_map(body, mesh=mesh, in_specs=in_specs, out_specs=out_specs, check_vma=False)
```

```python
import math

import jax
import jax.numpy as jnp
from jax import lax
from jax.sharding import PartitionSpec as P

HIGH = lax.Precision.HIGH
HIGHEST = lax.Precision.HIGHEST
BOTH = ("row", "col")


def step(i, s, n):
    return i ^ s if n & (n - 1) == 0 else (i + s) % n


def back(i, s, n):
    return i ^ s if n & (n - 1) == 0 else (i + n - s) % n


def tree_sum(parts):
    while len(parts) > 1:
        paired = [a + b for a, b in zip(parts[::2], parts[1::2])]
        parts = paired + parts[2 * len(paired) :]
    return parts[0]


def dot(a, b, dims, precision=HIGH):
    return lax.dot_general(a, b, (dims, ((), ())), precision=precision, preferred_element_type=jnp.float32)


def body(unfolding, factor):
    n_row = lax.axis_size("row")
    n_col = lax.axis_size("col")
    n_z = n_col // 2
    row = lax.axis_index("row")
    col = lax.axis_index("col")
    z, core = col // 2, col % 2
    rows_here, cols_here = unfolding.shape
    mode = rows_here * n_row
    rank = factor.shape[1]
    hr = rank // 2
    total_cols = cols_here * n_col
    group = mode // (2 * n_row)
    half = group // n_col

    row_pairs = [[(i, step(i, s, n_row)) for i in range(n_row)] for s in range(n_row)]
    core_pairs = [(i, i ^ 1) for i in range(n_col)]
    z_pairs = [[(i, 2 * step(i // 2, s, n_z) + i % 2) for i in range(n_col)] for s in range(n_z)]

    factor_here = lax.dynamic_slice_in_dim(factor, row * rows_here, rows_here, 0)
    y_part = dot(factor_here, unfolding, ((0,), (0,)))
    y = tree_sum([y_part] + [lax.ppermute(y_part, "row", row_pairs[s]) for s in range(1, n_row)])

    x = jnp.zeros((mode, cols_here), jnp.float32)
    blocks = [unfolding] + [lax.ppermute(unfolding, "row", row_pairs[s]) for s in range(1, n_row)]
    for s, block in enumerate(blocks):
        x = lax.dynamic_update_slice(x, block, (back(row, s, n_row) * rows_here, 0))

    term = dot(y, unfolding, ((1,), (1,))) * (1.0 / total_cols)
    kept = lax.dynamic_slice_in_dim(term, core * hr, hr, 0)
    given = lax.dynamic_slice_in_dim(term, (1 - core) * hr, hr, 0)
    pair = kept + lax.ppermute(given, "col", core_pairs)
    part = tree_sum([pair] + [lax.ppermute(pair, "col", z_pairs[s]) for s in range(1, n_z)])

    image_t = jnp.zeros((rank, mode), jnp.float32)
    for s in range(n_row):
        for t in range(2):
            pairs = [
                (i, step(i // n_col, s, n_row) * n_col + ((i % n_col) ^ t)) for i in range(n_row * n_col)
            ]
            block = part if s + t == 0 else lax.ppermute(part, BOTH, pairs)
            image_t = lax.dynamic_update_slice(
                image_t, block, ((core ^ t) * hr, back(row, s, n_row) * rows_here)
            )

    inner = dot(image_t, image_t, ((1,), (1,)), HIGHEST) / mode
    chol = jnp.linalg.cholesky(inner)
    factor_t = jax.scipy.linalg.solve_triangular(chol, image_t, lower=True)
    new_factor = factor_t.T
    rank_here = rank // n_row
    mine = lax.dynamic_slice_in_dim(factor_t, row * rank_here, rank_here, 0)
    core_out = dot(mine, x, ((1,), (0,))) * (1.0 / math.sqrt(mode))

    low = lax.dynamic_slice_in_dim(x, row * group, group, 0)
    high = lax.dynamic_slice_in_dim(x, mode - (row + 1) * group, group, 0)
    low = low.reshape(n_z, 2, half, cols_here).transpose(1, 0, 2, 3).reshape(group, cols_here)
    high = high.reshape(n_col, half, cols_here)[::-1]
    high = high.reshape(n_z, 2, half, cols_here).transpose(1, 0, 2, 3).reshape(group, cols_here)
    both = dot(jnp.concatenate([high, low], 0), x, ((1,), (1,))) * (1.0 / total_cols)
    width = mode + group
    split = mode - row * group
    column = lax.broadcasted_iota(jnp.int32, (group, width), 1)
    wide_high = jnp.pad(both[:group], ((0, 0), (0, group)))
    doubled = jnp.concatenate([both[group:], both[group:], both[group:, :group]], 1)
    rolled = lax.dynamic_slice_in_dim(doubled, row * group, width, 1)
    packed = jnp.where(column < split, wide_high, rolled)
    kept = lax.dynamic_slice_in_dim(packed, core * n_z * half, n_z * half, 0)
    given = lax.dynamic_slice_in_dim(packed, (1 - core) * n_z * half, n_z * half, 0)
    pair = kept + lax.ppermute(given, "col", core_pairs)
    pieces = []
    for s in range(n_z):
        piece = lax.dynamic_slice_in_dim(pair, step(z, s, n_z) * half, half, 0)
        pieces.append(piece if s == 0 else lax.ppermute(piece, "col", z_pairs[s]))
    total = tree_sum(pieces)

    low_cols = lax.dynamic_slice_in_dim(jnp.pad(total, ((0, 0), (0, mode))), split, mode, 1)
    owner = row * n_col + col
    r = lax.broadcasted_iota(jnp.int32, (half, mode), 0)
    c = lax.broadcasted_iota(jnp.int32, (half, mode), 1)
    gram_lower = jnp.concatenate(
        [
            jnp.where(c <= owner * half + r, low_cols, 0.0),
            jnp.where(c <= mode - (owner + 1) * half + r, total[:, :mode], 0.0),
        ],
        0,
    )
    return gram_lower, new_factor, core_out


def solution(mesh):
    in_specs = (P("row", "col"), P())
    out_specs = (P(("row", "col"), None), P(), P("row", "col"))
    return jax.shard_map(body, mesh=mesh, in_specs=in_specs, out_specs=out_specs, check_vma=False)
```

```python
import functools
import math

import jax
import jax.numpy as jnp
from jax import lax
from jax.experimental import pallas as pl
from jax.experimental.pallas import tpu as pltpu
from jax.sharding import PartitionSpec as P

F32 = jnp.float32
BF16 = jnp.bfloat16
NN = ((1,), (0,))
NT = ((1,), (1,))


def step(i, s, n):
    return i ^ s if n & (n - 1) == 0 else (i + s) % n


def back(i, s, n):
    return i ^ s if n & (n - 1) == 0 else (i + n - s) % n


def tree_sum(parts):
    while len(parts) > 1:
        paired = [a + b for a, b in zip(parts[::2], parts[1::2])]
        parts = paired + parts[2 * len(paired) :]
    return parts[0]


def split2(a):
    hi = a.astype(BF16)
    return hi, (a - hi.astype(F32)).astype(BF16)


def split3(a):
    hi = a.astype(BF16)
    rest = a - hi.astype(F32)
    mid = rest.astype(BF16)
    return hi, mid, (rest - mid.astype(F32)).astype(BF16)


def mm(a, b, dims):
    return lax.dot_general(a, b, (dims, ((), ())), preferred_element_type=F32)


def mm3(a, b, dims):
    return mm(a[1], b[0], dims) + mm(a[0], b[1], dims) + mm(a[0], b[0], dims)


def mm6(a, b, dims):
    low = mm(a[1], b[1], dims) + (mm(a[2], b[0], dims) + mm(a[0], b[2], dims))
    return (low + (mm(a[1], b[0], dims) + mm(a[0], b[1], dims))) + mm(a[0], b[0], dims)


def call(kernel, out_shape, *args, scratch=(), work=1000, name=None):
    return pl.pallas_call(
        kernel,
        out_shape=out_shape,
        in_specs=[pl.BlockSpec(memory_space=pltpu.VMEM)] * len(args),
        out_specs=jax.tree.map(lambda _: pl.BlockSpec(memory_space=pltpu.VMEM), out_shape),
        scratch_shapes=list(scratch),
        compiler_params=pltpu.CompilerParams(vmem_limit_bytes=48 * 2**20),
        cost_estimate=pl.CostEstimate(flops=work, bytes_accessed=work, transcendentals=0),
        name=name,
    )(*args)


def project_kernel(rows_here, factor_ref, x_ref, y_ref):
    row = lax.axis_index("row")
    n_row = factor_ref.shape[1] // rows_here
    mine = factor_ref[:, :rows_here]
    for r in range(1, n_row):
        mine = jnp.where(row == r, factor_ref[:, r * rows_here : (r + 1) * rows_here], mine)
    y_ref[...] = mm3(split2(mine), split2(x_ref[...]), NN)


def term_kernel(scale, x_ref, *refs):
    y = tree_sum([r[...] for r in refs[:-1]])
    refs[-1][...] = mm3(split2(y), split2(x_ref[...]), NT) * scale


def add_kernel(*refs):
    refs[-1][...] = tree_sum([r[...] for r in refs[:-1]])


def inverse_factor(inner):
    n = inner.shape[0]
    wide = -(-2 * n // 128) * 128
    r = lax.broadcasted_iota(jnp.int32, (n, wide), 0)
    c = lax.broadcasted_iota(jnp.int32, (n, wide), 1)
    w = jnp.where(c == r + n, F32(1.0), F32(0.0))
    w = w + jnp.concatenate([inner, jnp.zeros((n, wide - n), F32)], 1)
    w = [w[8 * i : 8 * i + 8] for i in range(n // 8)]
    sub = lax.broadcasted_iota(jnp.int32, (8, wide), 0)
    done = []
    for b in range(n // 8):
        cols = {
            j: [jnp.broadcast_to(w[i][:, 8 * b + j : 8 * b + j + 1], (8, wide)) for i in range(b, n // 8)]
            for j in range(8)
        }
        for k in range(8):
            pivot = jnp.broadcast_to(cols[k][0][k : k + 1], (8, wide))
            rs = lax.rsqrt(pivot)
            rs = rs * (1.5 - 0.5 * pivot * rs * rs)
            inv = rs * rs
            row = jnp.broadcast_to(w[b][k : k + 1], (8, wide))
            done.append(row[:1] * rs[:1])
            m = [a * inv for a in cols[k]]
            m[0] = jnp.where(sub > k, m[0], F32(0.0))
            for i in range(b, n // 8):
                w[i] = w[i] - m[i - b] * row
            for j in range(k + 1, 8):
                at = jnp.broadcast_to(cols[j][0][k : k + 1], (8, wide))
                cols[j] = [a - f * at for a, f in zip(cols[j], m)]
    return jnp.concatenate(done, 0)[:, n : 2 * n]


def finish_kernel(n_row, counts, *refs):
    images, refs = refs[:n_row], refs[n_row:]
    total = sum(counts)
    pieces, (nf_ref, core_ref, rows_ref) = refs[:total], refs[total:]
    row = lax.axis_index("row")
    rank, rows_here = images[0].shape
    mode = rows_here * n_row
    blocks = [r[...] for r in images]
    split = [split3(b) for b in blocks]
    inner = tree_sum([mm6(s, s, NT) for s in split]) * (1.0 / mode)
    inv = inverse_factor(inner)
    z, at = [], 0
    for s in range(n_row):
        start = 0
        for _ in range(counts[s]):
            x = pieces[at][...]
            hi, lo = split[s][0], split[s][1]
            stop = start + x.shape[0]
            z.append(mm3((hi[:, start:stop], lo[:, start:stop]), split2(x), NN))
            start, at = stop, at + 1
    z = tree_sum(z)
    rank_here = rank // n_row
    for i in range(n_row):
        rows_ref[i] = inv[i * rank_here : (i + 1) * rank_here]
    core_ref[...] = mm6(split3(rows_ref[row]), split3(z), NN) * (1.0 / math.sqrt(mode))
    inv3 = split3(inv)
    for s in range(n_row):
        nf_ref[back(row, s, n_row)] = mm6(inv3, split[s], NN)


def gram_kernel(n_row, n_col, scale, counts, *refs):
    total = sum(counts)
    pieces, (given_ref, kept_ref, hi_ref, lo_ref, part_ref) = refs[:total], refs[total:]
    row = lax.axis_index("row")
    core = lax.axis_index("col") % 2
    n_z = n_col // 2
    rows_here = hi_ref.shape[1] * 2
    group = rows_here // 2
    half = group // n_col
    at = 0
    for s in range(n_row):
        hi, lo = [], []
        for _ in range(counts[s]):
            h, l = split2(pieces[at][...])
            hi.append(h)
            lo.append(l)
            at += 1
        hi, lo = jnp.concatenate(hi, 0), jnp.concatenate(lo, 0)
        owner = back(row, s, n_row)
        for i in range(2):
            hi_ref[2 * owner + i] = hi[i * group : (i + 1) * group]
            lo_ref[2 * owner + i] = lo[i * group : (i + 1) * group]
    high = 2 * n_row - 1 - row
    left = (
        jnp.concatenate([hi_ref[high], hi_ref[row]], 0),
        jnp.concatenate([lo_ref[high], lo_ref[row]], 0),
    )
    for r in range(n_row):
        right = (
            jnp.concatenate([hi_ref[2 * r], hi_ref[2 * r + 1]], 0),
            jnp.concatenate([lo_ref[2 * r], lo_ref[2 * r + 1]], 0),
        )
        g = mm3(left, right, NT) * scale
        for i in range(2):
            for h in range(2):
                for p in range(n_col):
                    start = h * group + p * half
                    part_ref[h, 2 * r + i, p] = g[start : start + half, i * group : (i + 1) * group]
    n_high = 2 * n_row - row
    for b in range(2 * n_row + 1):
        is_low = (b >= n_high).astype(jnp.int32)
        block = b - is_low * n_high
        for zz in range(n_z):
            for ref, k in ((given_ref, 1 - core), (kept_ref, core)):
                owner = 2 * zz + k
                piece = jnp.where(is_low == 1, owner, n_col - 1 - owner)
                ref[zz, :, b * group : (b + 1) * group] = part_ref[is_low, block, piece]


def pieces_kernel(n_z, kept_ref, got_ref, *outs):
    z = lax.axis_index("col") // 2
    for s in range(n_z):
        at = step(z, s, n_z)
        outs[s][...] = kept_ref[at] + got_ref[at]


def unpack_kernel(n_row, n_col, *refs):
    out_ref = refs[-1]
    row = lax.axis_index("row")
    owner = row * n_col + lax.axis_index("col")
    total = tree_sum([r[...] for r in refs[:-1]])
    half, width = total.shape
    mode = out_ref.shape[1]
    group = width - mode
    r = lax.broadcasted_iota(jnp.int32, (half, mode), 0)
    c = lax.broadcasted_iota(jnp.int32, (half, mode), 1)
    out_ref[half:, :] = jnp.where(c <= mode - (owner + 1) * half + r, total[:, :mode], F32(0.0))
    out_ref[:half, :] = jnp.zeros((half, mode), F32)
    for k in range(n_row):

        @pl.when(row == k)
        def _():
            start, stop = mode - k * group, mode + group
            keep = c[:, : stop - start] <= owner * half + r[:, : stop - start]
            out_ref[:half, : stop - start] = jnp.where(keep, total[:, start:stop], F32(0.0))


def body(unfolding, factor):
    n_row = lax.axis_size("row")
    n_col = lax.axis_size("col")
    n_z = n_col // 2
    rows_here, cols_here = unfolding.shape
    mode = rows_here * n_row
    rank = factor.shape[1]
    scale = 1.0 / (cols_here * n_col)
    group = rows_here // 2
    half = group // n_col
    width = mode + group

    row_pairs = [[(i, step(i, s, n_row)) for i in range(n_row)] for s in range(n_row)]
    core_pairs = [(i, i ^ 1) for i in range(n_col)]
    z_pairs = [[(i, 2 * step(i // 2, s, n_z) + i % 2) for i in range(n_col)] for s in range(n_z)]

    def over(x, axis, pairs):
        return lax.ppermute(x, axis, pairs)

    y_part = call(
        functools.partial(project_kernel, rows_here),
        jax.ShapeDtypeStruct((rank, cols_here), F32),
        factor.T,
        unfolding,
        name="project",
    )
    ys = [y_part] + [over(y_part, "row", row_pairs[s]) for s in range(1, n_row)]

    if n_row == 4:
        one = over(unfolding, "row", row_pairs[1])
        two = over(unfolding, "row", row_pairs[2])
        top = over(one[:group], "row", row_pairs[2])
        bottom = over(two[group:], "row", row_pairs[1])
        blocks = [[unfolding], [one], [two], [top, bottom]]
    else:
        blocks = [[unfolding]] + [[over(unfolding, "row", row_pairs[s])] for s in range(1, n_row)]
    counts = tuple(len(b) for b in blocks)
    blocks = [p for b in blocks for p in b]

    term = call(
        functools.partial(term_kernel, scale),
        jax.ShapeDtypeStruct((rank, rows_here), F32),
        unfolding,
        *ys,
        name="term",
    )
    pair = term + over(term, "col", core_pairs)
    image = tree_sum([pair] + [over(pair, "col", z_pairs[s]) for s in range(1, n_z)])
    images = [image] + [over(image, "row", row_pairs[s]) for s in range(1, n_row)]

    rank_here = rank // n_row
    nf, core_out = call(
        functools.partial(finish_kernel, n_row, counts),
        (
            jax.ShapeDtypeStruct((n_row, rank, rows_here), F32),
            jax.ShapeDtypeStruct((rank_here, cols_here), F32),
        ),
        *images,
        *blocks,
        scratch=[pltpu.VMEM((n_row, rank_here, rank), F32)],
        name="finish",
    )
    new_factor = nf.transpose(0, 2, 1).reshape(mode, rank)

    given, kept = call(
        functools.partial(gram_kernel, n_row, n_col, scale, counts),
        (jax.ShapeDtypeStruct((n_z, half, width), F32),) * 2,
        *blocks,
        scratch=[
            pltpu.VMEM((2 * n_row, group, cols_here), BF16),
            pltpu.VMEM((2 * n_row, group, cols_here), BF16),
            pltpu.VMEM((2, 2 * n_row, n_col, half, group), F32),
        ],
        name="gram",
    )
    got = over(given, "col", core_pairs)
    parts = call(
        functools.partial(pieces_kernel, n_z),
        (jax.ShapeDtypeStruct((half, width), F32),) * n_z,
        kept,
        got,
        name="pieces",
    )
    parts = [parts[0]] + [over(parts[s], "col", z_pairs[s]) for s in range(1, n_z)]
    gram_lower = call(
        functools.partial(unpack_kernel, n_row, n_col),
        jax.ShapeDtypeStruct((2 * half, mode), F32),
        *parts,
        name="unpack",
    )
    return gram_lower, new_factor, core_out


def solution(mesh):
    in_specs = (P("row", "col"), P())
    out_specs = (P(("row", "col"), None), P(), P("row", "col"))
    return jax.shard_map(body, mesh=mesh, in_specs=in_specs, out_specs=out_specs, check_vma=False)
```

```python
import functools
import math

import jax
import jax.numpy as jnp
from jax import lax
from jax.experimental import pallas as pl
from jax.experimental.pallas import tpu as pltpu
from jax.sharding import PartitionSpec as P

F32 = jnp.float32
BF16 = jnp.bfloat16
NN = ((1,), (0,))
NT = ((1,), (1,))


COST = dict(project=10**6, term=10**10, finish=10**6, gram=10**6, pieces=10**6, unpack=10**6)


def tree_sum(parts):
    while len(parts) > 1:
        paired = [a + b for a, b in zip(parts[::2], parts[1::2])]
        parts = paired + parts[2 * len(paired) :]
    return parts[0]


def split2(a):
    hi = a.astype(BF16)
    return hi, (a - hi.astype(F32)).astype(BF16)


def split3(a):
    hi = a.astype(BF16)
    rest = a - hi.astype(F32)
    mid = rest.astype(BF16)
    return hi, mid, (rest - mid.astype(F32)).astype(BF16)


def mm(a, b, dims):
    return lax.dot_general(a, b, (dims, ((), ())), preferred_element_type=F32)


def mm3(a, b, dims):
    return mm(a[1], b[0], dims) + mm(a[0], b[1], dims) + mm(a[0], b[0], dims)


def mm6(a, b, dims):
    low = mm(a[1], b[1], dims) + (mm(a[2], b[0], dims) + mm(a[0], b[2], dims))
    return (low + (mm(a[1], b[0], dims) + mm(a[0], b[1], dims))) + mm(a[0], b[0], dims)


def call(kernel, out_shape, *args, scratch=(), work=1000, name=None):
    return pl.pallas_call(
        kernel,
        out_shape=out_shape,
        in_specs=[pl.BlockSpec(memory_space=pltpu.VMEM)] * len(args),
        out_specs=jax.tree.map(lambda _: pl.BlockSpec(memory_space=pltpu.VMEM), out_shape),
        scratch_shapes=list(scratch),
        compiler_params=pltpu.CompilerParams(vmem_limit_bytes=48 * 2**20),
        cost_estimate=pl.CostEstimate(flops=work, bytes_accessed=0, transcendentals=0),
        name=name,
    )(*args)


def project_kernel(rows_here, factor_ref, x_ref, y_ref):
    row = lax.axis_index("row")
    n_row = factor_ref.shape[1] // rows_here
    mine = factor_ref[:, :rows_here]
    for r in range(1, n_row):
        mine = jnp.where(row == r, factor_ref[:, r * rows_here : (r + 1) * rows_here], mine)
    y_ref[...] = mm3(split2(mine), split2(x_ref[...]), NN)


def term_kernel(scale, x_ref, mine_ref, got_ref, kept_ref, given_ref):
    core = lax.axis_index("col") % 2
    y = mine_ref[...] + got_ref[...]
    term = mm3(split2(y), split2(x_ref[...]), NT) * scale
    hr = term.shape[0] // 2
    kept_ref[...] = jnp.where(core == 0, term[:hr], term[hr:])
    given_ref[...] = jnp.where(core == 0, term[hr:], term[:hr])


def inverse_factor(inner):
    n = inner.shape[0]
    wide = -(-2 * n // 128) * 128
    r = lax.broadcasted_iota(jnp.int32, (n, wide), 0)
    c = lax.broadcasted_iota(jnp.int32, (n, wide), 1)
    w = jnp.where(c == r + n, F32(1.0), F32(0.0))
    w = w + jnp.concatenate([inner, jnp.zeros((n, wide - n), F32)], 1)
    w = [w[8 * i : 8 * i + 8] for i in range(n // 8)]
    sub = lax.broadcasted_iota(jnp.int32, (8, wide), 0)
    done = []
    for b in range(n // 8):
        cols = {
            j: [jnp.broadcast_to(w[i][:, 8 * b + j : 8 * b + j + 1], (8, wide)) for i in range(b, n // 8)]
            for j in range(8)
        }
        for k in range(8):
            pivot = jnp.broadcast_to(cols[k][0][k : k + 1], (8, wide))
            rs = lax.rsqrt(pivot)
            rs = rs * (1.5 - 0.5 * pivot * rs * rs)
            inv = rs * rs
            row = jnp.broadcast_to(w[b][k : k + 1], (8, wide))
            done.append(row[:1] * rs[:1])
            m = [a * inv for a in cols[k]]
            m[0] = jnp.where(sub > k, m[0], F32(0.0))
            for i in range(b, n // 8):
                w[i] = w[i] - m[i - b] * row
            for j in range(k + 1, 8):
                at = jnp.broadcast_to(cols[j][0][k : k + 1], (8, wide))
                cols[j] = [a - f * at for a, f in zip(cols[j], m)]
    return jnp.concatenate(done, 0)[:, n : 2 * n]


def finish_kernel(n_row, counts, mine_ref, other_ref, *refs):
    total = sum(counts)
    pieces, (nf_ref, core_ref, rows_ref) = refs[:total], refs[total:]
    row = lax.axis_index("row")
    core = lax.axis_index("col") % 2
    _, hr, rows_here = mine_ref.shape
    rank = 2 * hr
    mode = rows_here * n_row
    blocks = []
    for s in range(n_row):
        mine, other = mine_ref[s], other_ref[s]
        first, second = jnp.where(core == 0, mine, other), jnp.where(core == 0, other, mine)
        blocks.append(jnp.concatenate([first, second], 0))
    split = [split3(b) for b in blocks]
    inner = tree_sum([mm6(s, s, NT) for s in split]) * (1.0 / mode)
    inv = inverse_factor(inner)
    z, at = [], 0
    for s in range(n_row):
        start = 0
        for _ in range(counts[s]):
            x = pieces[at][...]
            hi, lo = split[s][0], split[s][1]
            stop = start + x.shape[0]
            z.append(mm3((hi[:, start:stop], lo[:, start:stop]), split2(x), NN))
            start, at = stop, at + 1
    z = tree_sum(z)
    rank_here = rank // n_row
    for i in range(n_row):
        rows_ref[i] = inv[i * rank_here : (i + 1) * rank_here]
    core_ref[...] = mm6(split3(rows_ref[row]), split3(z), NN) * (1.0 / math.sqrt(mode))
    inv3 = split3(inv)
    for s in range(n_row):
        block = mm6(inv3, split[s], NN)
        if len(nf_ref.shape) == 3:
            nf_ref[row ^ s] = block
        else:
            nf_ref[:, pl.ds(pl.multiple_of((row ^ s) * rows_here, rows_here), rows_here)] = block


def gram_kernel(n_row, n_col, scale, counts, *refs):
    total = sum(counts)
    pieces, (given_ref, kept_ref, hi_ref, lo_ref, part_ref) = refs[:total], refs[total:]
    row = lax.axis_index("row")
    core = lax.axis_index("col") % 2
    n_z = n_col // 2
    rows_here = hi_ref.shape[1] * 2
    group = rows_here // 2
    half = group // n_col
    at = 0
    for s in range(n_row):
        hi, lo = [], []
        for _ in range(counts[s]):
            h, l = split2(pieces[at][...])
            hi.append(h)
            lo.append(l)
            at += 1
        hi, lo = jnp.concatenate(hi, 0), jnp.concatenate(lo, 0)
        owner = row ^ s
        for i in range(2):
            hi_ref[2 * owner + i] = hi[i * group : (i + 1) * group]
            lo_ref[2 * owner + i] = lo[i * group : (i + 1) * group]
    high = 2 * n_row - 1 - row
    left = (
        jnp.concatenate([hi_ref[high], hi_ref[row]], 0),
        jnp.concatenate([lo_ref[high], lo_ref[row]], 0),
    )
    for r in range(n_row):
        right = (
            jnp.concatenate([hi_ref[2 * r], hi_ref[2 * r + 1]], 0),
            jnp.concatenate([lo_ref[2 * r], lo_ref[2 * r + 1]], 0),
        )
        g = mm3(left, right, NT) * scale
        for i in range(2):
            for h in range(2):
                for p in range(n_col):
                    start = h * group + p * half
                    part_ref[h, 2 * r + i, p] = g[start : start + half, i * group : (i + 1) * group]
    n_high = 2 * n_row - row
    for b in range(2 * n_row + 1):
        is_low = (b >= n_high).astype(jnp.int32)
        block = b - is_low * n_high
        for zz in range(n_z):
            for ref, k in ((given_ref, 1 - core), (kept_ref, core)):
                owner = 2 * zz + k
                piece = jnp.where(is_low == 1, owner, n_col - 1 - owner)
                ref[zz, :, b * group : (b + 1) * group] = part_ref[is_low, block, piece]


def pieces_kernel(n_z, kept_ref, got_ref, keep_ref, give_ref):
    z = lax.axis_index("col") // 2
    for t in range(n_z):
        ref = give_ref if t % 2 else keep_ref
        ref[t // 2] = kept_ref[z ^ t] + got_ref[z ^ t]


def unpack_kernel(n_row, n_col, *refs):
    out_ref = refs[-1]
    row = lax.axis_index("row")
    owner = row * n_col + lax.axis_index("col")
    total = tree_sum([r[0] for r in refs[:-1]])
    half, width = total.shape
    mode = out_ref.shape[1]
    group = width - mode
    r = lax.broadcasted_iota(jnp.int32, (half, mode), 0)
    c = lax.broadcasted_iota(jnp.int32, (half, mode), 1)
    out_ref[half:, :] = jnp.where(c <= mode - (owner + 1) * half + r, total[:, :mode], F32(0.0))
    out_ref[:half, :] = jnp.zeros((half, mode), F32)
    for k in range(n_row):

        @pl.when(row == k)
        def _():
            start, stop = mode - k * group, mode + group
            keep = c[:, : stop - start] <= owner * half + r[:, : stop - start]
            out_ref[:half, : stop - start] = jnp.where(keep, total[:, start:stop], F32(0.0))


def body(unfolding, factor):
    n_row = lax.axis_size("row")
    n_col = lax.axis_size("col")
    n_z = n_col // 2
    rows_here, cols_here = unfolding.shape
    mode = rows_here * n_row
    rank = factor.shape[1]
    hr = rank // 2
    scale = 1.0 / (cols_here * n_col)
    group = rows_here // 2
    half = group // n_col
    width = mode + group

    def over_row(x, s):
        return lax.ppermute(x, "row", [(i, i ^ s) for i in range(n_row)])

    def over_col(x, s):
        return lax.ppermute(x, "col", [(i, i ^ s) for i in range(n_col)])

    def steps(n):
        return [1 << k for k in range(n.bit_length() - 1)]

    y = call(
        functools.partial(project_kernel, rows_here),
        jax.ShapeDtypeStruct((rank, cols_here), F32),
        factor.T,
        unfolding,
        work=COST["project"],
        name="project",
    )
    for s in steps(n_row)[:-1]:
        y = y + over_row(y, s)
    y_got = over_row(y, n_row // 2)

    if n_row == 4:
        one = over_row(unfolding, 1)
        two = over_row(unfolding, 2)
        top = over_row(one[:group], 2)
        bottom = over_row(two[group:], 1)
        blocks = [[unfolding], [one], [two], [top, bottom]]
    else:
        blocks = [[unfolding]] + [[over_row(unfolding, s)] for s in range(1, n_row)]
    counts = tuple(len(b) for b in blocks)
    blocks = [p for b in blocks for p in b]

    kept, given = call(
        functools.partial(term_kernel, scale),
        (jax.ShapeDtypeStruct((hr, rows_here), F32),) * 2,
        unfolding,
        y,
        y_got,
        work=COST["term"],
        name="term",
    )
    image = kept + over_col(given, 1)
    for s in steps(n_z):
        image = image + over_col(image, 2 * s)
    mine = image[None]
    for s in steps(n_row):
        mine = jnp.concatenate([mine, over_row(mine, s)], 0)
    other = over_col(mine, 1)

    rank_here = rank // n_row
    whole = rows_here % 128 == 0
    nf, core_out = call(
        functools.partial(finish_kernel, n_row, counts),
        (
            jax.ShapeDtypeStruct((rank, mode) if whole else (n_row, rank, rows_here), F32),
            jax.ShapeDtypeStruct((rank_here, cols_here), F32),
        ),
        mine,
        other,
        *blocks,
        scratch=[pltpu.VMEM((n_row, rank_here, rank), F32)],
        work=COST["finish"],
        name="finish",
    )
    new_factor = nf.T if whole else nf.transpose(0, 2, 1).reshape(mode, rank)

    given, kept = call(
        functools.partial(gram_kernel, n_row, n_col, scale, counts),
        (jax.ShapeDtypeStruct((n_z, half, width), F32),) * 2,
        *blocks,
        scratch=[
            pltpu.VMEM((2 * n_row, group, cols_here), BF16),
            pltpu.VMEM((2 * n_row, group, cols_here), BF16),
            pltpu.VMEM((2, 2 * n_row, n_col, half, group), F32),
        ],
        work=COST["gram"],
        name="gram",
    )
    keep, give = call(
        functools.partial(pieces_kernel, n_z),
        (jax.ShapeDtypeStruct((n_z // 2, half, width), F32),) * 2,
        kept,
        over_col(given, 1),
        work=COST["pieces"],
        name="pieces",
    )
    got = over_col(give, 2)
    for s in steps(n_z)[1:]:
        keep, give = keep[0::2] + got[0::2], keep[1::2] + got[1::2]
        got = over_col(give, 2 * s)
    gram_lower = call(
        functools.partial(unpack_kernel, n_row, n_col),
        jax.ShapeDtypeStruct((2 * half, mode), F32),
        keep,
        got,
        work=COST["unpack"],
        name="unpack",
    )
    return gram_lower, new_factor, core_out


def solution(mesh):
    in_specs = (P("row", "col"), P())
    out_specs = (P(("row", "col"), None), P(), P("row", "col"))
    return jax.shard_map(body, mesh=mesh, in_specs=in_specs, out_specs=out_specs, check_vma=False)
```

```python
import functools
import math

import jax
import jax.numpy as jnp
from jax import lax
from jax.experimental import pallas as pl
from jax.experimental.pallas import tpu as pltpu
from jax.sharding import PartitionSpec as P

F32 = jnp.float32
BF16 = jnp.bfloat16
NN = ((1,), (0,))
NT = ((1,), (1,))


COST = dict(project=10**6, join=10**6, term=10**10, finish=10**6, gram=10**6, pieces=10**6, unpack=10**6)


def tree_sum(parts):
    while len(parts) > 1:
        paired = [a + b for a, b in zip(parts[::2], parts[1::2])]
        parts = paired + parts[2 * len(paired) :]
    return parts[0]


def split2(a):
    hi = a.astype(BF16)
    return hi, (a - hi.astype(F32)).astype(BF16)


def split3(a):
    hi = a.astype(BF16)
    rest = a - hi.astype(F32)
    mid = rest.astype(BF16)
    return hi, mid, (rest - mid.astype(F32)).astype(BF16)


def mm(a, b, dims):
    return lax.dot_general(a, b, (dims, ((), ())), preferred_element_type=F32)


def mm3(a, b, dims):
    return mm(a[1], b[0], dims) + mm(a[0], b[1], dims) + mm(a[0], b[0], dims)


def mm6(a, b, dims):
    low = mm(a[1], b[1], dims) + (mm(a[2], b[0], dims) + mm(a[0], b[2], dims))
    return (low + (mm(a[1], b[0], dims) + mm(a[0], b[1], dims))) + mm(a[0], b[0], dims)


def call(kernel, out_shape, *args, after=(), scratch=(), work=1000, name=None):
    n = len(args)

    def run(*refs):
        kernel(*refs[:n], *refs[n + len(after) :])

    return pl.pallas_call(
        run,
        out_shape=out_shape,
        in_specs=[pl.BlockSpec(memory_space=pltpu.VMEM)] * n + [pl.BlockSpec(memory_space=pl.ANY)] * len(after),
        out_specs=jax.tree.map(lambda _: pl.BlockSpec(memory_space=pltpu.VMEM), out_shape),
        scratch_shapes=list(scratch),
        compiler_params=pltpu.CompilerParams(vmem_limit_bytes=48 * 2**20),
        cost_estimate=pl.CostEstimate(flops=work, bytes_accessed=0, transcendentals=0),
        name=name,
    )(*args, *after)


def project_kernel(rows_here, factor_ref, x_ref, y_ref, *copies):
    row = lax.axis_index("row")
    n_row = factor_ref.shape[1] // rows_here
    mine = factor_ref[:, :rows_here]
    for r in range(1, n_row):
        mine = jnp.where(row == r, factor_ref[:, r * rows_here : (r + 1) * rows_here], mine)
    y_ref[...] = mm3(split2(mine), split2(x_ref[...]), NN)
    for i, ref in enumerate(copies):
        ref[...] = x_ref[i * ref.shape[0] : (i + 1) * ref.shape[0], :]


def join_kernel(mine_ref, got_ref, x_ref, y_ref, copy_ref):
    y_ref[...] = mine_ref[...] + got_ref[...]
    copy_ref[...] = x_ref[...]


def term_kernel(scale, x_ref, mine_ref, got_ref, kept_ref, given_ref):
    core = lax.axis_index("col") % 2
    y = mine_ref[...] + got_ref[...]
    term = mm3(split2(y), split2(x_ref[...]), NT) * scale
    hr = term.shape[0] // 2
    kept_ref[...] = jnp.where(core == 0, term[:hr], term[hr:])
    given_ref[...] = jnp.where(core == 0, term[hr:], term[:hr])


def inverse_factor(inner):
    n = inner.shape[0]
    wide = -(-2 * n // 128) * 128
    r = lax.broadcasted_iota(jnp.int32, (n, wide), 0)
    c = lax.broadcasted_iota(jnp.int32, (n, wide), 1)
    w = jnp.where(c == r + n, F32(1.0), F32(0.0))
    w = w + jnp.concatenate([inner, jnp.zeros((n, wide - n), F32)], 1)
    w = [w[8 * i : 8 * i + 8] for i in range(n // 8)]
    sub = lax.broadcasted_iota(jnp.int32, (8, wide), 0)
    done = []
    for b in range(n // 8):
        cols = {
            j: [jnp.broadcast_to(w[i][:, 8 * b + j : 8 * b + j + 1], (8, wide)) for i in range(b, n // 8)]
            for j in range(8)
        }
        for k in range(8):
            pivot = jnp.broadcast_to(cols[k][0][k : k + 1], (8, wide))
            rs = lax.rsqrt(pivot)
            rs = rs * (1.5 - 0.5 * pivot * rs * rs)
            inv = rs * rs
            row = jnp.broadcast_to(w[b][k : k + 1], (8, wide))
            done.append(row[:1] * rs[:1])
            m = [a * inv for a in cols[k]]
            m[0] = jnp.where(sub > k, m[0], F32(0.0))
            for i in range(b, n // 8):
                w[i] = w[i] - m[i - b] * row
            for j in range(k + 1, 8):
                at = jnp.broadcast_to(cols[j][0][k : k + 1], (8, wide))
                cols[j] = [a - f * at for a, f in zip(cols[j], m)]
    return jnp.concatenate(done, 0)[:, n : 2 * n]


def finish_kernel(n_row, counts, mine_ref, other_ref, *refs):
    total = sum(counts)
    pieces, (nf_ref, core_ref, rows_ref) = refs[:total], refs[total:]
    row = lax.axis_index("row")
    core = lax.axis_index("col") % 2
    _, hr, rows_here = mine_ref.shape
    rank = 2 * hr
    mode = rows_here * n_row
    blocks = []
    for s in range(n_row):
        mine, other = mine_ref[s], other_ref[s]
        first, second = jnp.where(core == 0, mine, other), jnp.where(core == 0, other, mine)
        blocks.append(jnp.concatenate([first, second], 0))
    split = [split3(b) for b in blocks]
    inner = tree_sum([mm6(s, s, NT) for s in split]) * (1.0 / mode)
    inv = inverse_factor(inner)
    z, at = [], 0
    for s in range(n_row):
        start = 0
        for _ in range(counts[s]):
            x = pieces[at][...]
            hi, lo = split[s][0], split[s][1]
            stop = start + x.shape[0]
            z.append(mm3((hi[:, start:stop], lo[:, start:stop]), split2(x), NN))
            start, at = stop, at + 1
    z = tree_sum(z)
    rank_here = rank // n_row
    for i in range(n_row):
        rows_ref[i] = inv[i * rank_here : (i + 1) * rank_here]
    core_ref[...] = mm6(split3(rows_ref[row]), split3(z), NN) * (1.0 / math.sqrt(mode))
    inv3 = split3(inv)
    for s in range(n_row):
        block = mm6(inv3, split[s], NN)
        if len(nf_ref.shape) == 3:
            nf_ref[row ^ s] = block
        else:
            nf_ref[:, pl.ds(pl.multiple_of((row ^ s) * rows_here, rows_here), rows_here)] = block


def gram_kernel(n_row, n_col, scale, counts, *refs):
    total = sum(counts)
    pieces, (given_ref, kept_ref, hi_ref, lo_ref, part_ref) = refs[:total], refs[total:]
    row = lax.axis_index("row")
    core = lax.axis_index("col") % 2
    n_z = n_col // 2
    rows_here = hi_ref.shape[1] * 2
    group = rows_here // 2
    half = group // n_col
    at = 0
    for s in range(n_row):
        hi, lo = [], []
        for _ in range(counts[s]):
            h, l = split2(pieces[at][...])
            hi.append(h)
            lo.append(l)
            at += 1
        hi, lo = jnp.concatenate(hi, 0), jnp.concatenate(lo, 0)
        owner = row ^ s
        for i in range(2):
            hi_ref[2 * owner + i] = hi[i * group : (i + 1) * group]
            lo_ref[2 * owner + i] = lo[i * group : (i + 1) * group]
    high = 2 * n_row - 1 - row
    left = (
        jnp.concatenate([hi_ref[high], hi_ref[row]], 0),
        jnp.concatenate([lo_ref[high], lo_ref[row]], 0),
    )
    for r in range(n_row):
        right = (
            jnp.concatenate([hi_ref[2 * r], hi_ref[2 * r + 1]], 0),
            jnp.concatenate([lo_ref[2 * r], lo_ref[2 * r + 1]], 0),
        )
        g = mm3(left, right, NT) * scale
        for i in range(2):
            for h in range(2):
                for p in range(n_col):
                    start = h * group + p * half
                    part_ref[h, 2 * r + i, p] = g[start : start + half, i * group : (i + 1) * group]
    n_high = 2 * n_row - row
    for b in range(2 * n_row + 1):
        is_low = (b >= n_high).astype(jnp.int32)
        block = b - is_low * n_high
        for zz in range(n_z):
            for ref, k in ((given_ref, 1 - core), (kept_ref, core)):
                owner = 2 * zz + k
                piece = jnp.where(is_low == 1, owner, n_col - 1 - owner)
                ref[zz, :, b * group : (b + 1) * group] = part_ref[is_low, block, piece]


def pieces_kernel(n_z, kept_ref, got_ref, keep_ref, give_ref):
    z = lax.axis_index("col") // 2
    for t in range(n_z):
        ref = give_ref if t % 2 else keep_ref
        ref[t // 2] = kept_ref[z ^ t] + got_ref[z ^ t]


def unpack_kernel(n_row, n_col, *refs):
    out_ref = refs[-1]
    row = lax.axis_index("row")
    owner = row * n_col + lax.axis_index("col")
    total = tree_sum([r[0] for r in refs[:-1]])
    half, width = total.shape
    mode = out_ref.shape[1]
    group = width - mode
    r = lax.broadcasted_iota(jnp.int32, (half, mode), 0)
    c = lax.broadcasted_iota(jnp.int32, (half, mode), 1)
    out_ref[half:, :] = jnp.where(c <= mode - (owner + 1) * half + r, total[:, :mode], F32(0.0))
    out_ref[:half, :] = jnp.zeros((half, mode), F32)
    for k in range(n_row):

        @pl.when(row == k)
        def _():
            start, stop = mode - k * group, mode + group
            keep = c[:, : stop - start] <= owner * half + r[:, : stop - start]
            out_ref[:half, : stop - start] = jnp.where(keep, total[:, start:stop], F32(0.0))


def body(unfolding, factor):
    n_row = lax.axis_size("row")
    n_col = lax.axis_size("col")
    n_z = n_col // 2
    rows_here, cols_here = unfolding.shape
    mode = rows_here * n_row
    rank = factor.shape[1]
    hr = rank // 2
    scale = 1.0 / (cols_here * n_col)
    group = rows_here // 2
    half = group // n_col
    width = mode + group

    def over_row(x, s):
        return lax.ppermute(x, "row", [(i, i ^ s) for i in range(n_row)])

    def over_col(x, s):
        return lax.ppermute(x, "col", [(i, i ^ s) for i in range(n_col)])

    def steps(n):
        return [1 << k for k in range(n.bit_length() - 1)]

    y_shape = jax.ShapeDtypeStruct((rank, cols_here), F32)
    part_shape = jax.ShapeDtypeStruct((group, cols_here), F32)
    project = functools.partial(project_kernel, rows_here)
    if n_row == 4:
        two_low = over_row(unfolding[group:], 2)
        y, upper, lower = call(
            project,
            (y_shape, part_shape, part_shape),
            factor.T,
            unfolding,
            work=COST["project"],
            name="project",
        )
        got = over_row(y, 1)
        one_up = over_row(upper, 1)
        one_low = over_row(lower, 1)
        y, upper = call(
            join_kernel, (y_shape, part_shape), y, got, upper, work=COST["join"], name="join"
        )
        y_got = over_row(y, 2)
        two_up = over_row(upper, 2)
        three = [over_row(one_up, 2), over_row(two_low, 1)]
        blocks = [[unfolding], [one_up, one_low], [two_up, two_low], three]
    else:
        (y,) = call(project, (y_shape,), factor.T, unfolding, work=COST["project"], name="project")
        for s in steps(n_row)[:-1]:
            y = y + over_row(y, s)
        y_got = over_row(y, n_row // 2)
        blocks = [[unfolding]] + [[over_row(unfolding, s)] for s in range(1, n_row)]
    counts = tuple(len(b) for b in blocks)
    blocks = [p for b in blocks for p in b]

    kept, given = call(
        functools.partial(term_kernel, scale),
        (jax.ShapeDtypeStruct((hr, rows_here), F32),) * 2,
        unfolding,
        y,
        y_got,
        work=COST["term"],
        name="term",
    )
    image = kept + over_col(given, 1)
    for s in steps(n_z):
        image = image + over_col(image, 2 * s)
    mine = image[None]
    for s in steps(n_row):
        mine = jnp.concatenate([mine, over_row(mine, s)], 0)
    other = over_col(mine, 1)

    rank_here = rank // n_row
    whole = rows_here % 128 == 0
    nf, core_out = call(
        functools.partial(finish_kernel, n_row, counts),
        (
            jax.ShapeDtypeStruct((rank, mode) if whole else (n_row, rank, rows_here), F32),
            jax.ShapeDtypeStruct((rank_here, cols_here), F32),
        ),
        mine,
        other,
        *blocks,
        scratch=[pltpu.VMEM((n_row, rank_here, rank), F32)],
        work=COST["finish"],
        name="finish",
    )
    new_factor = nf.T if whole else nf.transpose(0, 2, 1).reshape(mode, rank)

    given, kept = call(
        functools.partial(gram_kernel, n_row, n_col, scale, counts),
        (jax.ShapeDtypeStruct((n_z, half, width), F32),) * 2,
        *blocks,
        scratch=[
            pltpu.VMEM((2 * n_row, group, cols_here), BF16),
            pltpu.VMEM((2 * n_row, group, cols_here), BF16),
            pltpu.VMEM((2, 2 * n_row, n_col, half, group), F32),
        ],
        after=[image],
        work=COST["gram"],
        name="gram",
    )
    keep, give = call(
        functools.partial(pieces_kernel, n_z),
        (jax.ShapeDtypeStruct((n_z // 2, half, width), F32),) * 2,
        kept,
        over_col(given, 1),
        work=COST["pieces"],
        name="pieces",
    )
    got = over_col(give, 2)
    for s in steps(n_z)[1:]:
        keep, give = keep[0::2] + got[0::2], keep[1::2] + got[1::2]
        got = over_col(give, 2 * s)
    gram_lower = call(
        functools.partial(unpack_kernel, n_row, n_col),
        jax.ShapeDtypeStruct((2 * half, mode), F32),
        keep,
        got,
        work=COST["unpack"],
        name="unpack",
    )
    return gram_lower, new_factor, core_out


def solution(mesh):
    in_specs = (P("row", "col"), P())
    out_specs = (P(("row", "col"), None), P(), P("row", "col"))
    return jax.shard_map(body, mesh=mesh, in_specs=in_specs, out_specs=out_specs, check_vma=False)
```

```python
import functools
import math

import jax
import jax.numpy as jnp
from jax import lax
from jax.experimental import pallas as pl
from jax.experimental.pallas import tpu as pltpu
from jax.sharding import PartitionSpec as P

F32 = jnp.float32
BF16 = jnp.bfloat16
NN = ((1,), (0,))
NT = ((1,), (1,))


COST = dict(stack=3 * 10**9, sum=7 * 10**8, project=10**6, term=10**6, relay=10**6, finish=10**10, gram=10**6, pieces=10**6, unpack=10**6)


def tree_sum(parts):
    while len(parts) > 1:
        paired = [a + b for a, b in zip(parts[::2], parts[1::2])]
        parts = paired + parts[2 * len(paired) :]
    return parts[0]


def split2(a):
    hi = a.astype(BF16)
    return hi, (a - hi.astype(F32)).astype(BF16)


def split3(a):
    hi = a.astype(BF16)
    rest = a - hi.astype(F32)
    mid = rest.astype(BF16)
    return hi, mid, (rest - mid.astype(F32)).astype(BF16)


def mm(a, b, dims):
    return lax.dot_general(a, b, (dims, ((), ())), preferred_element_type=F32)


def mm3(a, b, dims):
    return mm(a[1], b[0], dims) + mm(a[0], b[1], dims) + mm(a[0], b[0], dims)


def mm6(a, b, dims):
    low = mm(a[1], b[1], dims) + (mm(a[2], b[0], dims) + mm(a[0], b[2], dims))
    return (low + (mm(a[1], b[0], dims) + mm(a[0], b[1], dims))) + mm(a[0], b[0], dims)


def call(kernel, out_shape, *args, after=(), scratch=(), work=1000, name=None, space=pltpu.VMEM, vmem=48):
    n = len(args)

    def run(*refs):
        kernel(*refs[:n], *refs[n + len(after) :])

    return pl.pallas_call(
        run,
        out_shape=out_shape,
        in_specs=[pl.BlockSpec(memory_space=space)] * n + [pl.BlockSpec(memory_space=pl.ANY)] * len(after),
        out_specs=jax.tree.map(lambda _: pl.BlockSpec(memory_space=pltpu.VMEM), out_shape),
        scratch_shapes=list(scratch),
        compiler_params=pltpu.CompilerParams(vmem_limit_bytes=vmem * 2**20),
        cost_estimate=pl.CostEstimate(flops=work, bytes_accessed=0, transcendentals=0),
        name=name,
    )(*args, *after)


def project_kernel(n_copies, factor_ref, x_ref, y_ref, *refs):
    copies, (factor_here, x_here, sems) = refs[:n_copies], refs[n_copies:]
    row = lax.axis_index("row")
    get_x = pltpu.make_async_copy(x_ref, x_here, sems.at[0])
    get_factor = pltpu.make_async_copy(factor_ref, factor_here, sems.at[1])
    get_x.start()
    get_factor.start()
    get_x.wait()
    get_factor.wait()
    rows_here = x_here.shape[0]
    n_row = factor_here.shape[1] // rows_here
    mine = factor_here[:, :rows_here]
    for r in range(1, n_row):
        mine = jnp.where(row == r, factor_here[:, r * rows_here : (r + 1) * rows_here], mine)
    y_ref[...] = mm3(split2(mine), split2(x_here[...]), NN)
    for i, ref in enumerate(copies):
        ref[...] = x_here[i * ref.shape[0] : (i + 1) * ref.shape[0], :]


def term_kernel(scale, x_ref, mine_ref, got_ref, kept_ref, given_ref):
    core = lax.axis_index("col") % 2
    y = mine_ref[...] + got_ref[...]
    term = mm3(split2(y), split2(x_ref[...]), NT) * scale
    hr = term.shape[0] // 2
    kept_ref[...] = jnp.where(core == 0, term[:hr], term[hr:])
    given_ref[...] = jnp.where(core == 0, term[hr:], term[:hr])


def relay_kernel(kept_ref, got_ref, *refs):
    n = len(refs) // 2
    refs[n][...] = kept_ref[...] + got_ref[...]
    for source, target in zip(refs[:n], refs[n + 1 :]):
        target[...] = source[...]


def sum_kernel(mine_ref, got_ref, out_ref):
    out_ref[...] = mine_ref[...] + got_ref[...]


def stack_kernel(mine_ref, got_ref, both_ref):
    n = mine_ref.shape[0]
    both_ref[:n] = mine_ref[...]
    both_ref[n:] = got_ref[...]


def inverse_factor(inner):
    n = inner.shape[0]
    wide = -(-2 * n // 128) * 128
    r = lax.broadcasted_iota(jnp.int32, (n, wide), 0)
    c = lax.broadcasted_iota(jnp.int32, (n, wide), 1)
    w = jnp.where(c == r + n, F32(1.0), F32(0.0))
    w = w + jnp.concatenate([inner, jnp.zeros((n, wide - n), F32)], 1)
    w = [w[8 * i : 8 * i + 8] for i in range(n // 8)]
    sub = lax.broadcasted_iota(jnp.int32, (8, wide), 0)
    done = []
    for b in range(n // 8):
        cols = {
            j: [jnp.broadcast_to(w[i][:, 8 * b + j : 8 * b + j + 1], (8, wide)) for i in range(b, n // 8)]
            for j in range(8)
        }
        for k in range(8):
            pivot = jnp.broadcast_to(cols[k][0][k : k + 1], (8, wide))
            rs = lax.rsqrt(pivot)
            rs = rs * (1.5 - 0.5 * pivot * rs * rs)
            inv = rs * rs
            row = jnp.broadcast_to(w[b][k : k + 1], (8, wide))
            done.append(row[:1] * rs[:1])
            m = [a * inv for a in cols[k]]
            m[0] = jnp.where(sub > k, m[0], F32(0.0))
            for i in range(b, n // 8):
                w[i] = w[i] - m[i - b] * row
            for j in range(k + 1, 8):
                at = jnp.broadcast_to(cols[j][0][k : k + 1], (8, wide))
                cols[j] = [a - f * at for a, f in zip(cols[j], m)]
    return jnp.concatenate(done, 0)[:, n : 2 * n]


def finish_kernel(n_row, counts, mine_ref, other_ref, *refs):
    total = sum(counts)
    pieces, (nf_ref, core_ref, rows_ref) = refs[:total], refs[total:]
    row = lax.axis_index("row")
    core = lax.axis_index("col") % 2
    _, hr, rows_here = mine_ref.shape
    rank = 2 * hr
    mode = rows_here * n_row
    blocks = []
    for s in range(n_row):
        mine, other = mine_ref[s], other_ref[s]
        first, second = jnp.where(core == 0, mine, other), jnp.where(core == 0, other, mine)
        blocks.append(jnp.concatenate([first, second], 0))
    split = [split3(b) for b in blocks]
    inner = tree_sum([mm6(s, s, NT) for s in split]) * (1.0 / mode)
    inv = inverse_factor(inner)
    z, at = [], 0
    for s in range(n_row):
        start = 0
        for _ in range(counts[s]):
            x = pieces[at][...]
            hi, lo = split[s][0], split[s][1]
            stop = start + x.shape[0]
            z.append(mm3((hi[:, start:stop], lo[:, start:stop]), split2(x), NN))
            start, at = stop, at + 1
    z = tree_sum(z)
    rank_here = rank // n_row
    for i in range(n_row):
        rows_ref[i] = inv[i * rank_here : (i + 1) * rank_here]
    core_ref[...] = mm6(split3(rows_ref[row]), split3(z), NN) * (1.0 / math.sqrt(mode))
    inv3 = split3(inv)
    for s in range(n_row):
        block = mm6(inv3, split[s], NN)
        if len(nf_ref.shape) == 3:
            nf_ref[row ^ s] = block
        else:
            nf_ref[:, pl.ds(pl.multiple_of((row ^ s) * rows_here, rows_here), rows_here)] = block


def gram_kernel(n_row, n_col, scale, counts, *refs):
    total = sum(counts)
    pieces, (given_ref, kept_ref, hi_ref, lo_ref, part_ref) = refs[:total], refs[total:]
    row = lax.axis_index("row")
    core = lax.axis_index("col") % 2
    n_z = n_col // 2
    rows_here = hi_ref.shape[1] * 2
    group = rows_here // 2
    half = group // n_col
    at = 0
    for s in range(n_row):
        hi, lo = [], []
        for _ in range(counts[s]):
            h, l = split2(pieces[at][...])
            hi.append(h)
            lo.append(l)
            at += 1
        hi, lo = jnp.concatenate(hi, 0), jnp.concatenate(lo, 0)
        owner = row ^ s
        for i in range(2):
            hi_ref[2 * owner + i] = hi[i * group : (i + 1) * group]
            lo_ref[2 * owner + i] = lo[i * group : (i + 1) * group]
    high = 2 * n_row - 1 - row
    left = (
        jnp.concatenate([hi_ref[high], hi_ref[row]], 0),
        jnp.concatenate([lo_ref[high], lo_ref[row]], 0),
    )
    for r in range(n_row):
        right = (
            jnp.concatenate([hi_ref[2 * r], hi_ref[2 * r + 1]], 0),
            jnp.concatenate([lo_ref[2 * r], lo_ref[2 * r + 1]], 0),
        )
        g = mm3(left, right, NT) * scale
        for i in range(2):
            for h in range(2):
                for p in range(n_col):
                    start = h * group + p * half
                    part_ref[h, 2 * r + i, p] = g[start : start + half, i * group : (i + 1) * group]
    n_high = 2 * n_row - row
    for b in range(2 * n_row + 1):
        is_low = (b >= n_high).astype(jnp.int32)
        block = b - is_low * n_high
        for zz in range(n_z):
            for ref, k in ((given_ref, 1 - core), (kept_ref, core)):
                owner = 2 * zz + k
                piece = jnp.where(is_low == 1, owner, n_col - 1 - owner)
                ref[zz, :, b * group : (b + 1) * group] = part_ref[is_low, block, piece]


def pieces_kernel(n_z, kept_ref, got_ref, keep_ref, give_ref):
    z = lax.axis_index("col") // 2
    for t in range(n_z):
        ref = give_ref if t % 2 else keep_ref
        ref[t // 2] = kept_ref[z ^ t] + got_ref[z ^ t]


def unpack_kernel(n_row, n_col, *refs):
    out_ref = refs[-1]
    row = lax.axis_index("row")
    owner = row * n_col + lax.axis_index("col")
    total = tree_sum([r[0] for r in refs[:-1]])
    half, width = total.shape
    mode = out_ref.shape[1]
    group = width - mode
    r = lax.broadcasted_iota(jnp.int32, (half, mode), 0)
    c = lax.broadcasted_iota(jnp.int32, (half, mode), 1)
    out_ref[half:, :] = jnp.where(c <= mode - (owner + 1) * half + r, total[:, :mode], F32(0.0))
    out_ref[:half, :] = jnp.zeros((half, mode), F32)
    for k in range(n_row):

        @pl.when(row == k)
        def _():
            start, stop = mode - k * group, mode + group
            keep = c[:, : stop - start] <= owner * half + r[:, : stop - start]
            out_ref[:half, : stop - start] = jnp.where(keep, total[:, start:stop], F32(0.0))


def body(unfolding, factor):
    n_row = lax.axis_size("row")
    n_col = lax.axis_size("col")
    n_z = n_col // 2
    rows_here, cols_here = unfolding.shape
    mode = rows_here * n_row
    rank = factor.shape[1]
    hr = rank // 2
    scale = 1.0 / (cols_here * n_col)
    group = rows_here // 2
    half = group // n_col
    width = mode + group

    def over_row(x, s):
        return lax.ppermute(x, "row", [(i, i ^ s) for i in range(n_row)])

    def over_col(x, s):
        return lax.ppermute(x, "col", [(i, i ^ s) for i in range(n_col)])

    def steps(n):
        return [1 << k for k in range(n.bit_length() - 1)]

    y_shape = jax.ShapeDtypeStruct((rank, cols_here), F32)
    part_shape = jax.ShapeDtypeStruct((group, cols_here), F32)
    y, *halves = call(
        functools.partial(project_kernel, 2 if n_row == 4 else 0),
        (y_shape, part_shape, part_shape) if n_row == 4 else (y_shape,),
        factor.T,
        unfolding,
        scratch=[
            pltpu.VMEM((rank, mode), F32),
            pltpu.VMEM((rows_here, cols_here), F32),
            pltpu.SemaphoreType.DMA((2,)),
        ],
        work=COST["project"],
        name="project",
        space=pltpu.HBM,
        vmem=62,
    )
    if n_row == 4:
        upper, lower = halves
        got = over_row(y, 1)
        one_up = over_row(upper, 1)
        two_low = over_row(lower, 2)
        one_low = over_row(lower, 1)
        y = y + got
        y_got = over_row(y, 2)
        two_up = over_row(upper, 2)
        forward = [one_up, two_low]
        blocks = [[unfolding], [one_up, one_low], [two_up, two_low]]
    else:
        for s in steps(n_row)[:-1]:
            y = y + over_row(y, s)
        y_got = over_row(y, n_row // 2)
        forward = []
        blocks = [[unfolding]] + [[over_row(unfolding, s)] for s in range(1, n_row)]

    kept, given = call(
        functools.partial(term_kernel, scale),
        (jax.ShapeDtypeStruct((hr, rows_here), F32),) * 2,
        unfolding,
        y,
        y_got,
        work=COST["term"],
        name="term",
    )
    image, *forward = call(
        relay_kernel,
        (jax.ShapeDtypeStruct((hr, rows_here), F32), *[part_shape] * len(forward)),
        kept,
        over_col(given, 1),
        *forward,
        work=COST["relay"],
        name="relay",
    )
    if forward:
        blocks.append([over_row(forward[0], 2), over_row(forward[1], 1)])
    counts = tuple(len(b) for b in blocks)
    blocks = [p for b in blocks for p in b]
    for s in steps(n_z):
        image = call(
            sum_kernel,
            jax.ShapeDtypeStruct((hr, rows_here), F32),
            image,
            over_col(image, 2 * s),
            work=COST["sum"],
            name="z_sum",
        )
    given, kept = call(
        functools.partial(gram_kernel, n_row, n_col, scale, counts),
        (jax.ShapeDtypeStruct((n_z, half, width), F32),) * 2,
        *blocks,
        scratch=[
            pltpu.VMEM((2 * n_row, group, cols_here), BF16),
            pltpu.VMEM((2 * n_row, group, cols_here), BF16),
            pltpu.VMEM((2, 2 * n_row, n_col, half, group), F32),
        ],
        after=[image],
        work=COST["gram"],
        name="gram",
    )
    mine = image[None]
    for s in steps(n_row):
        mine = call(
            stack_kernel,
            jax.ShapeDtypeStruct((2 * s, hr, rows_here), F32),
            mine,
            over_row(mine, s),
            after=[given] if s == 1 else [],
            work=COST["stack"],
            name="stack",
        )
    other = over_col(mine, 1)

    rank_here = rank // n_row
    whole = rows_here % 128 == 0
    nf, core_out = call(
        functools.partial(finish_kernel, n_row, counts),
        (
            jax.ShapeDtypeStruct((rank, mode) if whole else (n_row, rank, rows_here), F32),
            jax.ShapeDtypeStruct((rank_here, cols_here), F32),
        ),
        mine,
        other,
        *blocks,
        scratch=[pltpu.VMEM((n_row, rank_here, rank), F32)],
        work=COST["finish"],
        name="finish",
    )
    new_factor = nf.T if whole else nf.transpose(0, 2, 1).reshape(mode, rank)

    keep, give = call(
        functools.partial(pieces_kernel, n_z),
        (jax.ShapeDtypeStruct((n_z // 2, half, width), F32),) * 2,
        kept,
        over_col(given, 1),
        work=COST["pieces"],
        name="pieces",
    )
    got = over_col(give, 2)
    for s in steps(n_z)[1:]:
        keep, give = keep[0::2] + got[0::2], keep[1::2] + got[1::2]
        got = over_col(give, 2 * s)
    gram_lower = call(
        functools.partial(unpack_kernel, n_row, n_col),
        jax.ShapeDtypeStruct((2 * half, mode), F32),
        keep,
        got,
        work=COST["unpack"],
        name="unpack",
    )
    return gram_lower, new_factor, core_out


def solution(mesh):
    in_specs = (P("row", "col"), P())
    out_specs = (P(("row", "col"), None), P(), P("row", "col"))
    return jax.shard_map(body, mesh=mesh, in_specs=in_specs, out_specs=out_specs, check_vma=False)
```

```python
import functools
import math

import jax
import jax.numpy as jnp
from jax import lax
from jax.experimental import pallas as pl
from jax.experimental.pallas import tpu as pltpu
from jax.sharding import PartitionSpec as P

F32 = jnp.float32
BF16 = jnp.bfloat16
NN = ((1,), (0,))
NT = ((1,), (1,))


COST = dict(project=10**6, join=10**6, term=10**10, core_sum=10**6, sum=10**6, stack=3 * 10**9, finish=10**10, gram=10**6, pieces=10**6, unpack=10**6)


def tree_sum(parts):
    while len(parts) > 1:
        paired = [a + b for a, b in zip(parts[::2], parts[1::2])]
        parts = paired + parts[2 * len(paired) :]
    return parts[0]


def split2(a):
    hi = a.astype(BF16)
    return hi, (a - hi.astype(F32)).astype(BF16)


def split3(a):
    hi = a.astype(BF16)
    rest = a - hi.astype(F32)
    mid = rest.astype(BF16)
    return hi, mid, (rest - mid.astype(F32)).astype(BF16)


def mm(a, b, dims):
    return lax.dot_general(a, b, (dims, ((), ())), preferred_element_type=F32)


def mm3(a, b, dims):
    return mm(a[1], b[0], dims) + mm(a[0], b[1], dims) + mm(a[0], b[0], dims)


def mm4(a, b):
    left = jnp.concatenate([a[0], a[0], a[1], a[1]], 1)
    return mm(left, jnp.concatenate([b[0], b[1], b[0], b[1]], 0), NN)


def gram6(a):
    n = a[0].shape[0]
    s = jnp.concatenate(a, 0)
    g = mm(s, s, NT)

    def at(i, j):
        return g[i * n : (i + 1) * n, j * n : (j + 1) * n]

    return at(0, 0) + ((at(0, 1) + at(1, 0)) + (at(1, 1) + (at(0, 2) + at(2, 0))))


COST = dict(project=10**6, join=10**6, term=10**10, core_sum=10**6, sum=10**6, stack=3 * 10**9, finish=10**10, gram=10**6, pieces=10**6, unpack=10**6)


def tree_sum(parts):
    while len(parts) > 1:
        paired = [a + b for a, b in zip(parts[::2], parts[1::2])]
        parts = paired + parts[2 * len(paired) :]
    return parts[0]


def split2(a):
    hi = a.astype(BF16)
    return hi, (a - hi.astype(F32)).astype(BF16)


def split3(a):
    hi = a.astype(BF16)
    rest = a - hi.astype(F32)
    mid = rest.astype(BF16)
    return hi, mid, (rest - mid.astype(F32)).astype(BF16)


def mm(a, b, dims):
    return lax.dot_general(a, b, (dims, ((), ())), preferred_element_type=F32)


def mm3(a, b, dims):
    return mm(a[1], b[0], dims) + mm(a[0], b[1], dims) + mm(a[0], b[0], dims)


def mm6(a, b, dims):
    low = mm(a[1], b[1], dims) + (mm(a[2], b[0], dims) + mm(a[0], b[2], dims))
    return (low + (mm(a[1], b[0], dims) + mm(a[0], b[1], dims))) + mm(a[0], b[0], dims)


def call(kernel, out_shape, *args, after=(), scratch=(), work=1000, name=None):
    n = len(args)

    def run(*refs):
        kernel(*refs[:n], *refs[n + len(after) :])

    return pl.pallas_call(
        run,
        out_shape=out_shape,
        in_specs=[pl.BlockSpec(memory_space=pltpu.VMEM)] * n + [pl.BlockSpec(memory_space=pl.ANY)] * len(after),
        out_specs=jax.tree.map(lambda _: pl.BlockSpec(memory_space=pltpu.VMEM), out_shape),
        scratch_shapes=list(scratch),
        compiler_params=pltpu.CompilerParams(vmem_limit_bytes=48 * 2**20),
        cost_estimate=pl.CostEstimate(flops=work, bytes_accessed=0, transcendentals=0),
        name=name,
    )(*args, *after)


def project_kernel(rows_here, factor_ref, x_ref, y_ref, *copies):
    row = lax.axis_index("row")
    n_row = factor_ref.shape[1] // rows_here
    mine = factor_ref[:, :rows_here]
    for r in range(1, n_row):
        mine = jnp.where(row == r, factor_ref[:, r * rows_here : (r + 1) * rows_here], mine)
    y_ref[...] = mm3(split2(mine), split2(x_ref[...]), NN)
    for i, ref in enumerate(copies):
        ref[...] = x_ref[i * ref.shape[0] : (i + 1) * ref.shape[0], :]


def join_kernel(mine_ref, got_ref, x_ref, y_ref, copy_ref):
    y_ref[...] = mine_ref[...] + got_ref[...]
    copy_ref[...] = x_ref[...]


def term_kernel(scale, x_ref, mine_ref, got_ref, kept_ref, given_ref):
    core = lax.axis_index("col") % 2
    y = mine_ref[...] + got_ref[...]
    term = mm3(split2(y), split2(x_ref[...]), NT) * scale
    hr = term.shape[0] // 2
    kept_ref[...] = jnp.where(core == 0, term[:hr], term[hr:])
    given_ref[...] = jnp.where(core == 0, term[hr:], term[:hr])


def sum_kernel(mine_ref, got_ref, out_ref):
    out_ref[...] = mine_ref[...] + got_ref[...]


def stack_kernel(mine_ref, got_ref, both_ref):
    n = mine_ref.shape[0]
    both_ref[:n] = mine_ref[...]
    both_ref[n:] = got_ref[...]


def inverse_factor(inner):
    n = inner.shape[0]
    wide = -(-2 * n // 128) * 128
    r = lax.broadcasted_iota(jnp.int32, (n, wide), 0)
    c = lax.broadcasted_iota(jnp.int32, (n, wide), 1)
    w = jnp.where(c == r + n, F32(1.0), F32(0.0))
    w = w + jnp.concatenate([inner, jnp.zeros((n, wide - n), F32)], 1)
    w = [w[8 * i : 8 * i + 8] for i in range(n // 8)]
    sub = lax.broadcasted_iota(jnp.int32, (8, wide), 0)
    done = []
    for b in range(n // 8):
        cols = {
            j: [jnp.broadcast_to(w[i][:, 8 * b + j : 8 * b + j + 1], (8, wide)) for i in range(b, n // 8)]
            for j in range(8)
        }
        for k in range(8):
            pivot = jnp.broadcast_to(cols[k][0][k : k + 1], (8, wide))
            rs = lax.rsqrt(pivot)
            inv = rs * rs
            rs = rs * (1.5 - 0.5 * (pivot * inv))
            inv = inv * (2.0 - pivot * inv)
            row = jnp.broadcast_to(w[b][k : k + 1], (8, wide))
            done.append(row[:1] * rs[:1])
            below = [jnp.where(sub > k, cols[k][0], F32(0.0))] + cols[k][1:]
            m = [a * inv for a in below]
            for j in range(k + 1, 8):
                at = jnp.broadcast_to(cols[j][0][k : k + 1], (8, wide))
                if j == k + 1:
                    cols[j] = [a - (f * at) * inv for a, f in zip(cols[j], below)]
                else:
                    cols[j] = [a - f * at for a, f in zip(cols[j], m)]
            for i in range(b, n // 8):
                w[i] = w[i] - m[i - b] * row
    return jnp.concatenate(done, 0)[:, n : 2 * n]


def finish_kernel(n_row, counts, mine_ref, other_ref, *refs):
    total = sum(counts)
    pieces, (nf_ref, core_ref, rows_ref) = refs[:total], refs[total:]
    row = lax.axis_index("row")
    core = lax.axis_index("col") % 2
    _, hr, rows_here = mine_ref.shape
    rank = 2 * hr
    mode = rows_here * n_row
    blocks = []
    for s in range(n_row):
        mine, other = mine_ref[s], other_ref[s]
        first, second = jnp.where(core == 0, mine, other), jnp.where(core == 0, other, mine)
        blocks.append(jnp.concatenate([first, second], 0))
    split = [split3(b) for b in blocks]
    inner = tree_sum([gram6(s) for s in split]) * (1.0 / mode)
    inv = inverse_factor(inner)
    z, at = [], 0
    for s in range(n_row):
        start = 0
        for _ in range(counts[s]):
            x = pieces[at][...]
            hi, lo = split[s][0], split[s][1]
            stop = start + x.shape[0]
            z.append(mm3((hi[:, start:stop], lo[:, start:stop]), split2(x), NN))
            start, at = stop, at + 1
    z = tree_sum(z)
    rank_here = rank // n_row
    for i in range(n_row):
        rows_ref[i] = inv[i * rank_here : (i + 1) * rank_here]
    core_ref[...] = mm4(split2(rows_ref[row]), split2(z)) * (1.0 / math.sqrt(mode))
    inv2 = split2(inv)
    for s in range(n_row):
        block = mm4(inv2, split[s])
        if len(nf_ref.shape) == 3:
            nf_ref[row ^ s] = block
        else:
            nf_ref[:, pl.ds(pl.multiple_of((row ^ s) * rows_here, rows_here), rows_here)] = block


def gram_kernel(n_row, n_col, scale, counts, *refs):
    total = sum(counts)
    pieces, (given_ref, kept_ref, hi_ref, lo_ref, part_ref) = refs[:total], refs[total:]
    row = lax.axis_index("row")
    core = lax.axis_index("col") % 2
    n_z = n_col // 2
    rows_here = hi_ref.shape[1] * 2
    group = rows_here // 2
    half = group // n_col
    at = 0
    for s in range(n_row):
        hi, lo = [], []
        for _ in range(counts[s]):
            h, l = split2(pieces[at][...])
            hi.append(h)
            lo.append(l)
            at += 1
        hi, lo = jnp.concatenate(hi, 0), jnp.concatenate(lo, 0)
        owner = row ^ s
        for i in range(2):
            hi_ref[2 * owner + i] = hi[i * group : (i + 1) * group]
            lo_ref[2 * owner + i] = lo[i * group : (i + 1) * group]
    high = 2 * n_row - 1 - row
    left = (
        jnp.concatenate([hi_ref[high], hi_ref[row]], 0),
        jnp.concatenate([lo_ref[high], lo_ref[row]], 0),
    )
    for r in range(n_row):
        right = (
            jnp.concatenate([hi_ref[2 * r], hi_ref[2 * r + 1]], 0),
            jnp.concatenate([lo_ref[2 * r], lo_ref[2 * r + 1]], 0),
        )
        g = mm3(left, right, NT) * scale
        for i in range(2):
            for h in range(2):
                for p in range(n_col):
                    start = h * group + p * half
                    part_ref[h, 2 * r + i, p] = g[start : start + half, i * group : (i + 1) * group]
    n_high = 2 * n_row - row
    for b in range(2 * n_row + 1):
        is_low = (b >= n_high).astype(jnp.int32)
        block = b - is_low * n_high
        for zz in range(n_z):
            for ref, k in ((given_ref, 1 - core), (kept_ref, core)):
                owner = 2 * zz + k
                piece = jnp.where(is_low == 1, owner, n_col - 1 - owner)
                ref[zz, :, b * group : (b + 1) * group] = part_ref[is_low, block, piece]


def pieces_kernel(n_z, kept_ref, got_ref, keep_ref, give_ref):
    z = lax.axis_index("col") // 2
    for t in range(n_z):
        ref = give_ref if t % 2 else keep_ref
        ref[t // 2] = kept_ref[z ^ t] + got_ref[z ^ t]


def unpack_kernel(n_row, n_col, *refs):
    out_ref = refs[-1]
    row = lax.axis_index("row")
    owner = row * n_col + lax.axis_index("col")
    total = tree_sum([r[0] for r in refs[:-1]])
    half, width = total.shape
    mode = out_ref.shape[1]
    group = width - mode
    r = lax.broadcasted_iota(jnp.int32, (half, mode), 0)
    c = lax.broadcasted_iota(jnp.int32, (half, mode), 1)
    out_ref[half:, :] = jnp.where(c <= mode - (owner + 1) * half + r, total[:, :mode], F32(0.0))
    out_ref[:half, :] = jnp.zeros((half, mode), F32)
    for k in range(n_row):

        @pl.when(row == k)
        def _():
            start, stop = mode - k * group, mode + group
            keep = c[:, : stop - start] <= owner * half + r[:, : stop - start]
            out_ref[:half, : stop - start] = jnp.where(keep, total[:, start:stop], F32(0.0))


def body(unfolding, factor):
    n_row = lax.axis_size("row")
    n_col = lax.axis_size("col")
    n_z = n_col // 2
    rows_here, cols_here = unfolding.shape
    mode = rows_here * n_row
    rank = factor.shape[1]
    hr = rank // 2
    scale = 1.0 / (cols_here * n_col)
    group = rows_here // 2
    half = group // n_col
    width = mode + group

    def over_row(x, s):
        return lax.ppermute(x, "row", [(i, i ^ s) for i in range(n_row)])

    def over_col(x, s):
        return lax.ppermute(x, "col", [(i, i ^ s) for i in range(n_col)])

    def steps(n):
        return [1 << k for k in range(n.bit_length() - 1)]

    y_shape = jax.ShapeDtypeStruct((rank, cols_here), F32)
    part_shape = jax.ShapeDtypeStruct((group, cols_here), F32)
    project = functools.partial(project_kernel, rows_here)
    if n_row == 4:
        two_low = over_row(unfolding[group:], 2)
        y, upper, lower = call(
            project,
            (y_shape, part_shape, part_shape),
            factor.T,
            unfolding,
            work=COST["project"],
            name="project",
        )
        got = over_row(y, 1)
        one_up = over_row(upper, 1)
        one_low = over_row(lower, 1)
        y, upper = call(
            join_kernel, (y_shape, part_shape), y, got, upper, work=COST["join"], name="join"
        )
        y_got = over_row(y, 2)
        two_up = over_row(upper, 2)
        three = [over_row(one_up, 2), over_row(two_low, 1)]
        blocks = [[unfolding], [one_up, one_low], [two_up, two_low], three]
    else:
        (y,) = call(project, (y_shape,), factor.T, unfolding, work=COST["project"], name="project")
        for s in steps(n_row)[:-1]:
            y = y + over_row(y, s)
        y_got = over_row(y, n_row // 2)
        blocks = [[unfolding]] + [[over_row(unfolding, s)] for s in range(1, n_row)]
    counts = tuple(len(b) for b in blocks)
    blocks = [p for b in blocks for p in b]

    kept, given = call(
        functools.partial(term_kernel, scale),
        (jax.ShapeDtypeStruct((hr, rows_here), F32),) * 2,
        unfolding,
        y,
        y_got,
        work=COST["term"],
        name="term",
    )
    image = call(
        sum_kernel,
        jax.ShapeDtypeStruct((hr, rows_here), F32),
        kept,
        over_col(given, 1),
        work=COST["core_sum"],
        name="core_sum",
    )
    for s in steps(n_z):
        image = call(
            sum_kernel,
            jax.ShapeDtypeStruct((hr, rows_here), F32),
            image,
            over_col(image, 2 * s),
            work=COST["sum"],
            name="z_sum",
        )
    given, kept = call(
        functools.partial(gram_kernel, n_row, n_col, scale, counts),
        (jax.ShapeDtypeStruct((n_z, half, width), F32),) * 2,
        *blocks,
        scratch=[
            pltpu.VMEM((2 * n_row, group, cols_here), BF16),
            pltpu.VMEM((2 * n_row, group, cols_here), BF16),
            pltpu.VMEM((2, 2 * n_row, n_col, half, group), F32),
        ],
        after=[image],
        work=COST["gram"],
        name="gram",
    )
    mine = image[None]
    for s in steps(n_row):
        mine = call(
            stack_kernel,
            jax.ShapeDtypeStruct((2 * s, hr, rows_here), F32),
            mine,
            over_row(mine, s),
            after=[given] if s == 1 else [],
            work=COST["stack"],
            name="stack",
        )
    other = over_col(mine, 1)

    rank_here = rank // n_row
    whole = rows_here % 128 == 0
    nf, core_out = call(
        functools.partial(finish_kernel, n_row, counts),
        (
            jax.ShapeDtypeStruct((rank, mode) if whole else (n_row, rank, rows_here), F32),
            jax.ShapeDtypeStruct((rank_here, cols_here), F32),
        ),
        mine,
        other,
        *blocks,
        scratch=[pltpu.VMEM((n_row, rank_here, rank), F32)],
        work=COST["finish"],
        name="finish",
    )
    new_factor = nf.T if whole else nf.transpose(0, 2, 1).reshape(mode, rank)

    keep, give = call(
        functools.partial(pieces_kernel, n_z),
        (jax.ShapeDtypeStruct((n_z // 2, half, width), F32),) * 2,
        kept,
        over_col(given, 1),
        work=COST["pieces"],
        name="pieces",
    )
    got = over_col(give, 2)
    for s in steps(n_z)[1:]:
        keep, give = keep[0::2] + got[0::2], keep[1::2] + got[1::2]
        got = over_col(give, 2 * s)
    gram_lower = call(
        functools.partial(unpack_kernel, n_row, n_col),
        jax.ShapeDtypeStruct((2 * half, mode), F32),
        keep,
        got,
        work=COST["unpack"],
        name="unpack",
    )
    return gram_lower, new_factor, core_out


def solution(mesh):
    in_specs = (P("row", "col"), P())
    out_specs = (P(("row", "col"), None), P(), P("row", "col"))
    return jax.shard_map(body, mesh=mesh, in_specs=in_specs, out_specs=out_specs, check_vma=False)
```

```python
import functools
import math

import jax
import jax.numpy as jnp
from jax import lax
from jax.experimental import pallas as pl
from jax.experimental.pallas import tpu as pltpu
from jax.sharding import PartitionSpec as P

F32 = jnp.float32
BF16 = jnp.bfloat16
NN = ((1,), (0,))
NT = ((1,), (1,))


COST = dict(project=10**6, join=10**6, term=10**10, core_sum=10**6, sum=10**6, stack=3 * 10**9, finish=10**10, gram=10**6, pieces=10**6, unpack=10**6)


def tree_sum(parts):
    while len(parts) > 1:
        paired = [a + b for a, b in zip(parts[::2], parts[1::2])]
        parts = paired + parts[2 * len(paired) :]
    return parts[0]


def split2(a):
    hi = a.astype(BF16)
    return hi, (a - hi.astype(F32)).astype(BF16)


def split3(a):
    hi = a.astype(BF16)
    rest = a - hi.astype(F32)
    mid = rest.astype(BF16)
    return hi, mid, (rest - mid.astype(F32)).astype(BF16)


def mm(a, b, dims):
    return lax.dot_general(a, b, (dims, ((), ())), preferred_element_type=F32)


def mm3(a, b, dims):
    return mm(a[1], b[0], dims) + mm(a[0], b[1], dims) + mm(a[0], b[0], dims)


def mm4(a, b):
    left = jnp.concatenate([a[0], a[0], a[1], a[1]], 1)
    return mm(left, jnp.concatenate([b[0], b[1], b[0], b[1]], 0), NN)


def gram6(a):
    n = a[0].shape[0]
    s = jnp.concatenate(a, 0)
    g = mm(s, s, NT)

    def at(i, j):
        return g[i * n : (i + 1) * n, j * n : (j + 1) * n]

    return at(0, 0) + ((at(0, 1) + at(1, 0)) + (at(1, 1) + (at(0, 2) + at(2, 0))))


COST = dict(project=10**6, join=10**6, term=10**10, core_sum=10**6, sum=10**6, stack=3 * 10**9, finish=10**10, gram=10**6, pieces=10**6, unpack=10**6)


def tree_sum(parts):
    while len(parts) > 1:
        paired = [a + b for a, b in zip(parts[::2], parts[1::2])]
        parts = paired + parts[2 * len(paired) :]
    return parts[0]


def split2(a):
    hi = a.astype(BF16)
    return hi, (a - hi.astype(F32)).astype(BF16)


def split3(a):
    hi = a.astype(BF16)
    rest = a - hi.astype(F32)
    mid = rest.astype(BF16)
    return hi, mid, (rest - mid.astype(F32)).astype(BF16)


def mm(a, b, dims):
    return lax.dot_general(a, b, (dims, ((), ())), preferred_element_type=F32)


def mm3(a, b, dims):
    return mm(a[1], b[0], dims) + mm(a[0], b[1], dims) + mm(a[0], b[0], dims)


def mm6(a, b, dims):
    low = mm(a[1], b[1], dims) + (mm(a[2], b[0], dims) + mm(a[0], b[2], dims))
    return (low + (mm(a[1], b[0], dims) + mm(a[0], b[1], dims))) + mm(a[0], b[0], dims)


def call(kernel, out_shape, *args, after=(), scratch=(), work=1000, name=None):
    n = len(args)

    def run(*refs):
        kernel(*refs[:n], *refs[n + len(after) :])

    return pl.pallas_call(
        run,
        out_shape=out_shape,
        in_specs=[pl.BlockSpec(memory_space=pltpu.VMEM)] * n + [pl.BlockSpec(memory_space=pl.ANY)] * len(after),
        out_specs=jax.tree.map(lambda _: pl.BlockSpec(memory_space=pltpu.VMEM), out_shape),
        scratch_shapes=list(scratch),
        compiler_params=pltpu.CompilerParams(vmem_limit_bytes=48 * 2**20),
        cost_estimate=pl.CostEstimate(flops=work, bytes_accessed=0, transcendentals=0),
        name=name,
    )(*args, *after)


def project_kernel(rows_here, factor_ref, x_ref, y_ref, *copies):
    row = lax.axis_index("row")
    n_row = factor_ref.shape[1] // rows_here
    mine = factor_ref[:, :rows_here]
    for r in range(1, n_row):
        mine = jnp.where(row == r, factor_ref[:, r * rows_here : (r + 1) * rows_here], mine)
    y_ref[...] = mm3(split2(mine), split2(x_ref[...]), NN)
    for i, ref in enumerate(copies):
        ref[...] = x_ref[i * ref.shape[0] : (i + 1) * ref.shape[0], :]


def join_kernel(mine_ref, got_ref, x_ref, y_ref, copy_ref):
    y_ref[...] = mine_ref[...] + got_ref[...]
    copy_ref[...] = x_ref[...]


def term_kernel(scale, x_ref, mine_ref, got_ref, kept_ref, given_ref):
    core = lax.axis_index("col") % 2
    y = mine_ref[...] + got_ref[...]
    term = mm3(split2(y), split2(x_ref[...]), NT) * scale
    hr = term.shape[0] // 2
    kept_ref[...] = jnp.where(core == 0, term[:hr], term[hr:])
    given_ref[...] = jnp.where(core == 0, term[hr:], term[:hr])


def sum_kernel(mine_ref, got_ref, out_ref):
    out_ref[...] = mine_ref[...] + got_ref[...]


def stack_kernel(mine_ref, got_ref, both_ref):
    n = mine_ref.shape[0]
    both_ref[:n] = mine_ref[...]
    both_ref[n:] = got_ref[...]


def inverse_factor(inner):
    n = inner.shape[0]
    wide = -(-2 * n // 128) * 128
    r = lax.broadcasted_iota(jnp.int32, (n, wide), 0)
    c = lax.broadcasted_iota(jnp.int32, (n, wide), 1)
    w = jnp.where(c == r + n, F32(1.0), F32(0.0))
    w = w + jnp.concatenate([inner, jnp.zeros((n, wide - n), F32)], 1)
    w = [w[8 * i : 8 * i + 8] for i in range(n // 8)]
    sub = lax.broadcasted_iota(jnp.int32, (8, wide), 0)
    done = []
    for b in range(n // 8):
        cols = {
            j: [jnp.broadcast_to(w[i][:, 8 * b + j : 8 * b + j + 1], (8, wide)) for i in range(b, n // 8)]
            for j in range(8)
        }
        for k in range(8):
            pivot = jnp.broadcast_to(cols[k][0][k : k + 1], (8, wide))
            rs = lax.rsqrt(pivot)
            inv = rs * rs
            rs = rs * (1.5 - 0.5 * (pivot * inv))
            inv = inv * (2.0 - pivot * inv)
            row = jnp.broadcast_to(w[b][k : k + 1], (8, wide))
            done.append(row[:1] * rs[:1])
            below = [jnp.where(sub > k, cols[k][0], F32(0.0))] + cols[k][1:]
            m = [a * inv for a in below]
            for j in range(k + 1, 8):
                at = jnp.broadcast_to(cols[j][0][k : k + 1], (8, wide))
                if j == k + 1:
                    cols[j] = [a - (f * at) * inv for a, f in zip(cols[j], below)]
                else:
                    cols[j] = [a - f * at for a, f in zip(cols[j], m)]
            for i in range(b, n // 8):
                w[i] = w[i] - m[i - b] * row
    return jnp.concatenate(done, 0)[:, n : 2 * n]


def finish_kernel(n_row, counts, mine_ref, other_ref, *refs):
    total = sum(counts)
    pieces, (nf_ref, core_ref, rows_ref) = refs[:total], refs[total:]
    row = lax.axis_index("row")
    core = lax.axis_index("col") % 2
    _, hr, rows_here = mine_ref.shape
    rank = 2 * hr
    mode = rows_here * n_row
    blocks = []
    for s in range(n_row):
        mine, other = mine_ref[s], other_ref[s]
        first, second = jnp.where(core == 0, mine, other), jnp.where(core == 0, other, mine)
        blocks.append(jnp.concatenate([first, second], 0))
    split = [split3(b) for b in blocks]
    inner = tree_sum([gram6(s) for s in split]) * (1.0 / mode)
    inv = inverse_factor(inner)
    z, at = [], 0
    for s in range(n_row):
        start = 0
        for _ in range(counts[s]):
            x = pieces[at][...]
            hi, lo = split[s][0], split[s][1]
            stop = start + x.shape[0]
            z.append(mm3((hi[:, start:stop], lo[:, start:stop]), split2(x), NN))
            start, at = stop, at + 1
    z = tree_sum(z)
    rank_here = rank // n_row
    for i in range(n_row):
        rows_ref[i] = inv[i * rank_here : (i + 1) * rank_here]
    core_ref[...] = mm4(split2(rows_ref[row]), split2(z)) * (1.0 / math.sqrt(mode))
    inv2 = split2(inv)
    for s in range(n_row):
        block = mm4(inv2, split[s])
        if len(nf_ref.shape) == 3:
            nf_ref[row ^ s] = block
        else:
            nf_ref[:, pl.ds(pl.multiple_of((row ^ s) * rows_here, rows_here), rows_here)] = block


def gram_kernel(n_row, n_col, scale, counts, *refs):
    total = sum(counts)
    pieces, (given_ref, kept_ref, hi_ref, lo_ref, part_ref) = refs[:total], refs[total:]
    row = lax.axis_index("row")
    core = lax.axis_index("col") % 2
    n_z = n_col // 2
    rows_here = hi_ref.shape[1] * 2
    group = rows_here // 2
    half = group // n_col
    at = 0
    for s in range(n_row):
        hi, lo = [], []
        for _ in range(counts[s]):
            h, l = split2(pieces[at][...])
            hi.append(h)
            lo.append(l)
            at += 1
        hi, lo = jnp.concatenate(hi, 0), jnp.concatenate(lo, 0)
        owner = row ^ s
        for i in range(2):
            hi_ref[2 * owner + i] = hi[i * group : (i + 1) * group]
            lo_ref[2 * owner + i] = lo[i * group : (i + 1) * group]
    high = 2 * n_row - 1 - row
    left = (
        jnp.concatenate([hi_ref[high], hi_ref[row]], 0),
        jnp.concatenate([lo_ref[high], lo_ref[row]], 0),
    )
    for r in range(n_row):
        right = (
            jnp.concatenate([hi_ref[2 * r], hi_ref[2 * r + 1]], 0),
            jnp.concatenate([lo_ref[2 * r], lo_ref[2 * r + 1]], 0),
        )
        g = mm3(left, right, NT) * scale
        for i in range(2):
            for h in range(2):
                for p in range(n_col):
                    start = h * group + p * half
                    part_ref[h, 2 * r + i, p] = g[start : start + half, i * group : (i + 1) * group]
    n_high = 2 * n_row - row
    for b in range(2 * n_row + 1):
        is_low = (b >= n_high).astype(jnp.int32)
        block = b - is_low * n_high
        for zz in range(n_z):
            for ref, k in ((given_ref, 1 - core), (kept_ref, core)):
                owner = 2 * zz + k
                piece = jnp.where(is_low == 1, owner, n_col - 1 - owner)
                ref[zz, :, b * group : (b + 1) * group] = part_ref[is_low, block, piece]


def pieces_kernel(n_z, kept_ref, got_ref, keep_ref, give_ref):
    z = lax.axis_index("col") // 2
    for t in range(n_z):
        ref = give_ref if t % 2 else keep_ref
        ref[t // 2] = kept_ref[z ^ t] + got_ref[z ^ t]


def unpack_kernel(n_row, n_col, *refs):
    out_ref = refs[-1]
    row = lax.axis_index("row")
    owner = row * n_col + lax.axis_index("col")
    total = tree_sum([r[0] for r in refs[:-1]])
    half, width = total.shape
    mode = out_ref.shape[1]
    group = width - mode
    r = lax.broadcasted_iota(jnp.int32, (half, mode), 0)
    c = lax.broadcasted_iota(jnp.int32, (half, mode), 1)
    out_ref[half:, :] = jnp.where(c <= mode - (owner + 1) * half + r, total[:, :mode], F32(0.0))
    out_ref[:half, :] = jnp.zeros((half, mode), F32)
    for k in range(n_row):

        @pl.when(row == k)
        def _():
            start, stop = mode - k * group, mode + group
            keep = c[:, : stop - start] <= owner * half + r[:, : stop - start]
            out_ref[:half, : stop - start] = jnp.where(keep, total[:, start:stop], F32(0.0))


def body(unfolding, factor):
    n_row = lax.axis_size("row")
    n_col = lax.axis_size("col")
    n_z = n_col // 2
    rows_here, cols_here = unfolding.shape
    mode = rows_here * n_row
    rank = factor.shape[1]
    hr = rank // 2
    scale = 1.0 / (cols_here * n_col)
    group = rows_here // 2
    half = group // n_col
    width = mode + group

    def over_row(x, s):
        return lax.ppermute(x, "row", [(i, i ^ s) for i in range(n_row)])

    def over_col(x, s):
        return lax.ppermute(x, "col", [(i, i ^ s) for i in range(n_col)])

    def steps(n):
        return [1 << k for k in range(n.bit_length() - 1)]

    y_shape = jax.ShapeDtypeStruct((rank, cols_here), F32)
    part_shape = jax.ShapeDtypeStruct((group, cols_here), F32)
    project = functools.partial(project_kernel, rows_here)
    if n_row == 4:
        two_low = over_row(unfolding[group:], 2)
        y, upper, lower = call(
            project,
            (y_shape, part_shape, part_shape),
            factor.T,
            unfolding,
            work=COST["project"],
            name="project",
        )
        got = over_row(y, 1)
        one_up = over_row(upper, 1)
        one_low = over_row(lower, 1)
        y, upper = call(
            join_kernel, (y_shape, part_shape), y, got, upper, work=COST["join"], name="join"
        )
        y_got = over_row(y, 2)
        two_up = over_row(upper, 2)
        three = [over_row(one_up, 2), over_row(two_low, 1)]
        blocks = [[unfolding], [one_up, one_low], [two_up, two_low], three]
    else:
        (y,) = call(project, (y_shape,), factor.T, unfolding, work=COST["project"], name="project")
        for s in steps(n_row)[:-1]:
            y = y + over_row(y, s)
        y_got = over_row(y, n_row // 2)
        blocks = [[unfolding]] + [[over_row(unfolding, s)] for s in range(1, n_row)]
    counts = tuple(len(b) for b in blocks)
    blocks = [p for b in blocks for p in b]

    kept, given = call(
        functools.partial(term_kernel, scale),
        (jax.ShapeDtypeStruct((hr, rows_here), F32),) * 2,
        unfolding,
        y,
        y_got,
        work=COST["term"],
        name="term",
    )
    image = call(
        sum_kernel,
        jax.ShapeDtypeStruct((hr, rows_here), F32),
        kept,
        over_col(given, 1),
        work=COST["core_sum"],
        name="core_sum",
    )

    def z_sum(image, s, after):
        return call(
            sum_kernel,
            jax.ShapeDtypeStruct((hr, rows_here), F32),
            image,
            over_col(image, 2 * s),
            after=after,
            work=COST["sum"],
            name="z_sum",
        )

    for s in steps(n_z)[:-1]:
        image = z_sum(image, s, [])

    given, kept = call(
        functools.partial(gram_kernel, n_row, n_col, scale, counts),
        (jax.ShapeDtypeStruct((n_z, half, width), F32),) * 2,
        *blocks,
        scratch=[
            pltpu.VMEM((2 * n_row, group, cols_here), BF16),
            pltpu.VMEM((2 * n_row, group, cols_here), BF16),
            pltpu.VMEM((2, 2 * n_row, n_col, half, group), F32),
        ],
        after=[image],
        work=COST["gram"],
        name="gram",
    )
    image = z_sum(image, n_z // 2, [given])
    mine = image[None]
    for s in steps(n_row):
        mine = call(
            stack_kernel,
            jax.ShapeDtypeStruct((2 * s, hr, rows_here), F32),
            mine,
            over_row(mine, s),
            work=COST["stack"],
            name="stack",
        )
    other = over_col(mine, 1)

    rank_here = rank // n_row
    whole = rows_here % 128 == 0
    nf, core_out = call(
        functools.partial(finish_kernel, n_row, counts),
        (
            jax.ShapeDtypeStruct((rank, mode) if whole else (n_row, rank, rows_here), F32),
            jax.ShapeDtypeStruct((rank_here, cols_here), F32),
        ),
        mine,
        other,
        *blocks,
        scratch=[pltpu.VMEM((n_row, rank_here, rank), F32)],
        work=COST["finish"],
        name="finish",
    )
    new_factor = nf.T if whole else nf.transpose(0, 2, 1).reshape(mode, rank)

    keep, give = call(
        functools.partial(pieces_kernel, n_z),
        (jax.ShapeDtypeStruct((n_z // 2, half, width), F32),) * 2,
        kept,
        over_col(given, 1),
        work=COST["pieces"],
        name="pieces",
    )
    got = over_col(give, 2)
    for s in steps(n_z)[1:]:
        keep, give = keep[0::2] + got[0::2], keep[1::2] + got[1::2]
        got = over_col(give, 2 * s)
    gram_lower = call(
        functools.partial(unpack_kernel, n_row, n_col),
        jax.ShapeDtypeStruct((2 * half, mode), F32),
        keep,
        got,
        work=COST["unpack"],
        name="unpack",
    )
    return gram_lower, new_factor, core_out


def solution(mesh):
    in_specs = (P("row", "col"), P())
    out_specs = (P(("row", "col"), None), P(), P("row", "col"))
    return jax.shard_map(body, mesh=mesh, in_specs=in_specs, out_specs=out_specs, check_vma=False)
```

```python
import functools
import math

import jax
import jax.numpy as jnp
from jax import lax
from jax.experimental import pallas as pl
from jax.experimental.pallas import tpu as pltpu
from jax.sharding import PartitionSpec as P

F32 = jnp.float32
BF16 = jnp.bfloat16
NN = ((1,), (0,))
NT = ((1,), (1,))


COST = dict(project=10**6, join=10**6, term=2 * 10**9, relay=10**6, sum=10**6, stack=3 * 10**9, finish=10**10, gram=10**6, pieces=10**6, unpack=10**6)


def tree_sum(parts):
    while len(parts) > 1:
        paired = [a + b for a, b in zip(parts[::2], parts[1::2])]
        parts = paired + parts[2 * len(paired) :]
    return parts[0]


def split2(a):
    hi = a.astype(BF16)
    return hi, (a - hi.astype(F32)).astype(BF16)


def split3(a):
    hi = a.astype(BF16)
    rest = a - hi.astype(F32)
    mid = rest.astype(BF16)
    return hi, mid, (rest - mid.astype(F32)).astype(BF16)


def mm(a, b, dims):
    return lax.dot_general(a, b, (dims, ((), ())), preferred_element_type=F32)


def mm3(a, b, dims):
    return mm(a[1], b[0], dims) + mm(a[0], b[1], dims) + mm(a[0], b[0], dims)


def mm4(a, b):
    left = jnp.concatenate([a[0], a[0], a[1], a[1]], 1)
    return mm(left, jnp.concatenate([b[0], b[1], b[0], b[1]], 0), NN)


def gram6(a):
    n = a[0].shape[0]
    s = jnp.concatenate(a, 0)
    g = mm(s, s, NT)

    def at(i, j):
        return g[i * n : (i + 1) * n, j * n : (j + 1) * n]

    return at(0, 0) + ((at(0, 1) + at(1, 0)) + (at(1, 1) + (at(0, 2) + at(2, 0))))


def tree_sum(parts):
    while len(parts) > 1:
        paired = [a + b for a, b in zip(parts[::2], parts[1::2])]
        parts = paired + parts[2 * len(paired) :]
    return parts[0]


def split2(a):
    hi = a.astype(BF16)
    return hi, (a - hi.astype(F32)).astype(BF16)


def split3(a):
    hi = a.astype(BF16)
    rest = a - hi.astype(F32)
    mid = rest.astype(BF16)
    return hi, mid, (rest - mid.astype(F32)).astype(BF16)


def mm(a, b, dims):
    return lax.dot_general(a, b, (dims, ((), ())), preferred_element_type=F32)


def mm3(a, b, dims):
    return mm(a[1], b[0], dims) + mm(a[0], b[1], dims) + mm(a[0], b[0], dims)


def mm6(a, b, dims):
    low = mm(a[1], b[1], dims) + (mm(a[2], b[0], dims) + mm(a[0], b[2], dims))
    return (low + (mm(a[1], b[0], dims) + mm(a[0], b[1], dims))) + mm(a[0], b[0], dims)


def call(kernel, out_shape, *args, after=(), scratch=(), work=1000, name=None):
    n = len(args)

    def run(*refs):
        kernel(*refs[:n], *refs[n + len(after) :])

    return pl.pallas_call(
        run,
        out_shape=out_shape,
        in_specs=[pl.BlockSpec(memory_space=pltpu.VMEM)] * n + [pl.BlockSpec(memory_space=pl.ANY)] * len(after),
        out_specs=jax.tree.map(lambda _: pl.BlockSpec(memory_space=pltpu.VMEM), out_shape),
        scratch_shapes=list(scratch),
        compiler_params=pltpu.CompilerParams(vmem_limit_bytes=48 * 2**20),
        cost_estimate=pl.CostEstimate(flops=work, bytes_accessed=0, transcendentals=0),
        name=name,
    )(*args, *after)


def project_kernel(rows_here, factor_ref, x_ref, y_ref, *copies):
    row = lax.axis_index("row")
    n_row = factor_ref.shape[1] // rows_here
    mine = factor_ref[:, :rows_here]
    for r in range(1, n_row):
        mine = jnp.where(row == r, factor_ref[:, r * rows_here : (r + 1) * rows_here], mine)
    y_ref[...] = mm3(split2(mine), split2(x_ref[...]), NN)
    for i, ref in enumerate(copies):
        ref[...] = x_ref[i * ref.shape[0] : (i + 1) * ref.shape[0], :]


def join_kernel(mine_ref, got_ref, x_ref, y_ref, copy_ref):
    y_ref[...] = mine_ref[...] + got_ref[...]
    copy_ref[...] = x_ref[: copy_ref.shape[0], :]


def term_kernel(scale, x_ref, mine_ref, got_ref, kept_ref, given_ref):
    core = lax.axis_index("col") % 2
    y = mine_ref[...] + got_ref[...]
    term = mm3(split2(y), split2(x_ref[...]), NT) * scale
    hr = term.shape[0] // 2
    kept_ref[...] = jnp.where(core == 0, term[:hr], term[hr:])
    given_ref[...] = jnp.where(core == 0, term[hr:], term[:hr])


def relay_kernel(kept_ref, got_ref, *refs):
    n = len(refs) // 2
    refs[n][...] = kept_ref[...] + got_ref[...]
    for source, target in zip(refs[:n], refs[n + 1 :]):
        target[...] = source[: target.shape[0], :]


def sum_kernel(mine_ref, got_ref, out_ref):
    out_ref[...] = mine_ref[...] + got_ref[...]


def stack_kernel(mine_ref, got_ref, both_ref):
    n = mine_ref.shape[0]
    both_ref[:n] = mine_ref[...]
    both_ref[n:] = got_ref[...]


def inverse_factor(inner):
    n = inner.shape[0]
    wide = -(-2 * n // 128) * 128
    r = lax.broadcasted_iota(jnp.int32, (n, wide), 0)
    c = lax.broadcasted_iota(jnp.int32, (n, wide), 1)
    w = jnp.where(c == r + n, F32(1.0), F32(0.0))
    w = w + jnp.concatenate([inner, jnp.zeros((n, wide - n), F32)], 1)
    w = [w[8 * i : 8 * i + 8] for i in range(n // 8)]
    sub = lax.broadcasted_iota(jnp.int32, (8, wide), 0)
    done = []
    for b in range(n // 8):
        cols = {
            j: [jnp.broadcast_to(w[i][:, 8 * b + j : 8 * b + j + 1], (8, wide)) for i in range(b, n // 8)]
            for j in range(8)
        }
        for k in range(8):
            pivot = jnp.broadcast_to(cols[k][0][k : k + 1], (8, wide))
            rs = lax.rsqrt(pivot)
            inv = rs * rs
            rs = rs * (1.5 - 0.5 * (pivot * inv))
            inv = inv * (2.0 - pivot * inv)
            row = jnp.broadcast_to(w[b][k : k + 1], (8, wide))
            done.append(row[:1] * rs[:1])
            below = [jnp.where(sub > k, cols[k][0], F32(0.0))] + cols[k][1:]
            m = [a * inv for a in below]
            for j in range(k + 1, 8):
                at = jnp.broadcast_to(cols[j][0][k : k + 1], (8, wide))
                if j == k + 1:
                    cols[j] = [a - (f * at) * inv for a, f in zip(cols[j], below)]
                else:
                    cols[j] = [a - f * at for a, f in zip(cols[j], m)]
            for i in range(b, n // 8):
                w[i] = w[i] - m[i - b] * row
    return jnp.concatenate(done, 0)[:, n : 2 * n]


def finish_kernel(n_row, counts, mine_ref, other_ref, *refs):
    total = sum(counts)
    pieces, (nf_ref, core_ref, rows_ref) = refs[:total], refs[total:]
    row = lax.axis_index("row")
    core = lax.axis_index("col") % 2
    _, hr, rows_here = mine_ref.shape
    rank = 2 * hr
    mode = rows_here * n_row
    blocks = []
    for s in range(n_row):
        mine, other = mine_ref[s], other_ref[s]
        first, second = jnp.where(core == 0, mine, other), jnp.where(core == 0, other, mine)
        blocks.append(jnp.concatenate([first, second], 0))
    split = [split3(b) for b in blocks]
    inner = tree_sum([gram6(s) for s in split]) * (1.0 / mode)
    inv = inverse_factor(inner)
    z, at = [], 0
    for s in range(n_row):
        start = 0
        for _ in range(counts[s]):
            x = pieces[at][...]
            hi, lo = split[s][0], split[s][1]
            stop = start + x.shape[0]
            z.append(mm3((hi[:, start:stop], lo[:, start:stop]), split2(x), NN))
            start, at = stop, at + 1
    z = tree_sum(z)
    rank_here = rank // n_row
    for i in range(n_row):
        rows_ref[i] = inv[i * rank_here : (i + 1) * rank_here]
    core_ref[...] = mm4(split2(rows_ref[row]), split2(z)) * (1.0 / math.sqrt(mode))
    inv2 = split2(inv)
    for s in range(n_row):
        block = mm4(inv2, split[s])
        if len(nf_ref.shape) == 3:
            nf_ref[row ^ s] = block
        else:
            nf_ref[:, pl.ds(pl.multiple_of((row ^ s) * rows_here, rows_here), rows_here)] = block


def gram_kernel(n_row, n_col, scale, counts, *refs):
    total = sum(counts)
    pieces, (given_ref, kept_ref, hi_ref, lo_ref, part_ref) = refs[:total], refs[total:]
    row = lax.axis_index("row")
    core = lax.axis_index("col") % 2
    n_z = n_col // 2
    rows_here = hi_ref.shape[1] * 2
    group = rows_here // 2
    half = group // n_col
    at = 0
    for s in range(n_row):
        hi, lo = [], []
        for _ in range(counts[s]):
            h, l = split2(pieces[at][...])
            hi.append(h)
            lo.append(l)
            at += 1
        hi, lo = jnp.concatenate(hi, 0), jnp.concatenate(lo, 0)
        owner = row ^ s
        for i in range(2):
            hi_ref[2 * owner + i] = hi[i * group : (i + 1) * group]
            lo_ref[2 * owner + i] = lo[i * group : (i + 1) * group]
    high = 2 * n_row - 1 - row
    left = (
        jnp.concatenate([hi_ref[high], hi_ref[row]], 0),
        jnp.concatenate([lo_ref[high], lo_ref[row]], 0),
    )
    for r in range(n_row):
        right = (
            jnp.concatenate([hi_ref[2 * r], hi_ref[2 * r + 1]], 0),
            jnp.concatenate([lo_ref[2 * r], lo_ref[2 * r + 1]], 0),
        )
        g = mm3(left, right, NT) * scale
        for i in range(2):
            for h in range(2):
                for p in range(n_col):
                    start = h * group + p * half
                    part_ref[h, 2 * r + i, p] = g[start : start + half, i * group : (i + 1) * group]
    n_high = 2 * n_row - row
    for b in range(2 * n_row + 1):
        is_low = (b >= n_high).astype(jnp.int32)
        block = b - is_low * n_high
        for zz in range(n_z):
            for ref, k in ((given_ref, 1 - core), (kept_ref, core)):
                owner = 2 * zz + k
                piece = jnp.where(is_low == 1, owner, n_col - 1 - owner)
                ref[zz, :, b * group : (b + 1) * group] = part_ref[is_low, block, piece]


def pieces_kernel(n_z, kept_ref, got_ref, keep_ref, give_ref):
    z = lax.axis_index("col") // 2
    for t in range(n_z):
        ref = give_ref if t % 2 else keep_ref
        ref[t // 2] = kept_ref[z ^ t] + got_ref[z ^ t]


def unpack_kernel(n_row, n_col, *refs):
    out_ref = refs[-1]
    row = lax.axis_index("row")
    owner = row * n_col + lax.axis_index("col")
    total = tree_sum([r[0] for r in refs[:-1]])
    half, width = total.shape
    mode = out_ref.shape[1]
    group = width - mode
    r = lax.broadcasted_iota(jnp.int32, (half, mode), 0)
    c = lax.broadcasted_iota(jnp.int32, (half, mode), 1)
    out_ref[half:, :] = jnp.where(c <= mode - (owner + 1) * half + r, total[:, :mode], F32(0.0))
    out_ref[:half, :] = jnp.zeros((half, mode), F32)
    for k in range(n_row):

        @pl.when(row == k)
        def _():
            start, stop = mode - k * group, mode + group
            keep = c[:, : stop - start] <= owner * half + r[:, : stop - start]
            out_ref[:half, : stop - start] = jnp.where(keep, total[:, start:stop], F32(0.0))


def body(unfolding, factor):
    n_row = lax.axis_size("row")
    n_col = lax.axis_size("col")
    n_z = n_col // 2
    rows_here, cols_here = unfolding.shape
    mode = rows_here * n_row
    rank = factor.shape[1]
    hr = rank // 2
    scale = 1.0 / (cols_here * n_col)
    group = rows_here // 2
    half = group // n_col
    width = mode + group

    def over_row(x, s):
        return lax.ppermute(x, "row", [(i, i ^ s) for i in range(n_row)])

    def over_col(x, s):
        return lax.ppermute(x, "col", [(i, i ^ s) for i in range(n_col)])

    def steps(n):
        return [1 << k for k in range(n.bit_length() - 1)]

    y_shape = jax.ShapeDtypeStruct((rank, cols_here), F32)
    part_shape = jax.ShapeDtypeStruct((group, cols_here), F32)
    cut = rows_here - rows_here // 4
    if n_row == 4:
        two_low = over_row(unfolding[group:], 2)
        one_low = over_row(unfolding[cut:], 1)
        y, upper = call(
            functools.partial(project_kernel, rows_here),
            (y_shape, jax.ShapeDtypeStruct((cut, cols_here), F32)),
            factor.T,
            unfolding,
            work=COST["project"],
            name="project",
        )
        got = over_row(y, 1)
        one_up = over_row(upper, 1)
        y, upper = call(
            join_kernel,
            (y_shape, part_shape),
            y,
            got,
            upper,
            after=[two_low, one_low],
            work=COST["join"],
            name="join",
        )
        y_got = over_row(y, 2)
        two_up = over_row(upper, 2)
        forward = [one_up]
        blocks = [[unfolding], [one_up, one_low], [two_up, two_low], [over_row(two_low, 1)]]
    else:
        (y,) = call(
            functools.partial(project_kernel, rows_here),
            (y_shape,),
            factor.T,
            unfolding,
            work=COST["project"],
            name="project",
        )
        for s in steps(n_row)[:-1]:
            y = y + over_row(y, s)
        y_got = over_row(y, n_row // 2)
        forward = []
        blocks = [[unfolding]] + [[over_row(unfolding, s)] for s in range(1, n_row)]

    kept, given = call(
        functools.partial(term_kernel, scale),
        (jax.ShapeDtypeStruct((hr, rows_here), F32),) * 2,
        unfolding,
        y,
        y_got,
        work=COST["term"],
        name="term",
    )
    image, *forward = call(
        relay_kernel,
        (jax.ShapeDtypeStruct((hr, rows_here), F32), *[part_shape] * len(forward)),
        kept,
        over_col(given, 1),
        *forward,
        work=COST["relay"],
        name="relay",
    )
    if forward:
        blocks[3].insert(0, over_row(forward[0], 2))
    counts = tuple(len(b) for b in blocks)
    blocks = [p for b in blocks for p in b]

    def z_sum(image, s, after):
        return call(
            sum_kernel,
            jax.ShapeDtypeStruct((hr, rows_here), F32),
            image,
            over_col(image, 2 * s),
            after=after,
            work=COST["sum"],
            name="z_sum",
        )

    hold = [two_up] if n_row == 4 else []
    for s in steps(n_z)[:-1]:
        image = z_sum(image, s, hold)
        hold = []

    given, kept = call(
        functools.partial(gram_kernel, n_row, n_col, scale, counts),
        (jax.ShapeDtypeStruct((n_z, half, width), F32),) * 2,
        *blocks,
        scratch=[
            pltpu.VMEM((2 * n_row, group, cols_here), BF16),
            pltpu.VMEM((2 * n_row, group, cols_here), BF16),
            pltpu.VMEM((2, 2 * n_row, n_col, half, group), F32),
        ],
        after=[image],
        work=COST["gram"],
        name="gram",
    )
    image = z_sum(image, n_z // 2, [given])
    mine = image[None]
    for s in steps(n_row):
        mine = call(
            stack_kernel,
            jax.ShapeDtypeStruct((2 * s, hr, rows_here), F32),
            mine,
            over_row(mine, s),
            work=COST["stack"],
            name="stack",
        )
    other = over_col(mine, 1)

    rank_here = rank // n_row
    whole = rows_here % 128 == 0
    nf, core_out = call(
        functools.partial(finish_kernel, n_row, counts),
        (
            jax.ShapeDtypeStruct((rank, mode) if whole else (n_row, rank, rows_here), F32),
            jax.ShapeDtypeStruct((rank_here, cols_here), F32),
        ),
        mine,
        other,
        *blocks,
        scratch=[pltpu.VMEM((n_row, rank_here, rank), F32)],
        work=COST["finish"],
        name="finish",
    )
    new_factor = nf.T if whole else nf.transpose(0, 2, 1).reshape(mode, rank)

    keep, give = call(
        functools.partial(pieces_kernel, n_z),
        (jax.ShapeDtypeStruct((n_z // 2, half, width), F32),) * 2,
        kept,
        over_col(given, 1),
        work=COST["pieces"],
        name="pieces",
    )
    got = over_col(give, 2)
    for s in steps(n_z)[1:]:
        keep, give = keep[0::2] + got[0::2], keep[1::2] + got[1::2]
        got = over_col(give, 2 * s)
    gram_lower = call(
        functools.partial(unpack_kernel, n_row, n_col),
        jax.ShapeDtypeStruct((2 * half, mode), F32),
        keep,
        got,
        work=COST["unpack"],
        name="unpack",
    )
    return gram_lower, new_factor, core_out


def solution(mesh):
    in_specs = (P("row", "col"), P())
    out_specs = (P(("row", "col"), None), P(), P("row", "col"))
    return jax.shard_map(body, mesh=mesh, in_specs=in_specs, out_specs=out_specs, check_vma=False)
```

```python
import functools
import math

import jax
import jax.numpy as jnp
from jax import lax
from jax.experimental import pallas as pl
from jax.experimental.pallas import tpu as pltpu
from jax.sharding import PartitionSpec as P

F32 = jnp.float32
BF16 = jnp.bfloat16
NN = ((1,), (0,))
NT = ((1,), (1,))


COST = dict(project=10**6, join=10**6, term=10**10, core_sum=10**6, sum=10**6, stack=3 * 10**9, finish=10**10, gram=10**6, pieces=10**6, unpack=10**6)


def tree_sum(parts):
    while len(parts) > 1:
        paired = [a + b for a, b in zip(parts[::2], parts[1::2])]
        parts = paired + parts[2 * len(paired) :]
    return parts[0]


def split2(a):
    hi = a.astype(BF16)
    return hi, (a - hi.astype(F32)).astype(BF16)


def split3(a):
    hi = a.astype(BF16)
    rest = a - hi.astype(F32)
    mid = rest.astype(BF16)
    return hi, mid, (rest - mid.astype(F32)).astype(BF16)


def sided(s, n_row):
    if n_row != 4 or s in (0, 3):
        return s
    return jnp.where(lax.axis_index("col") % 2 == 1, 3 - s, s)


def mm(a, b, dims):
    return lax.dot_general(a, b, (dims, ((), ())), preferred_element_type=F32)


def mm3(a, b, dims):
    return mm(a[1], b[0], dims) + mm(a[0], b[1], dims) + mm(a[0], b[0], dims)


def mm4(a, b):
    left = jnp.concatenate([a[0], a[0], a[1], a[1]], 1)
    return mm(left, jnp.concatenate([b[0], b[1], b[0], b[1]], 0), NN)


def gram6(a):
    n = a[0].shape[0]
    s = jnp.concatenate(a, 0)
    g = mm(s, s, NT)

    def at(i, j):
        return g[i * n : (i + 1) * n, j * n : (j + 1) * n]

    return at(0, 0) + ((at(0, 1) + at(1, 0)) + (at(1, 1) + (at(0, 2) + at(2, 0))))


COST = dict(project=10**6, join=10**6, term=10**10, core_sum=10**6, sum=10**6, stack=3 * 10**9, finish=10**10, gram=10**6, pieces=10**6, unpack=10**6)


def tree_sum(parts):
    while len(parts) > 1:
        paired = [a + b for a, b in zip(parts[::2], parts[1::2])]
        parts = paired + parts[2 * len(paired) :]
    return parts[0]


def split2(a):
    hi = a.astype(BF16)
    return hi, (a - hi.astype(F32)).astype(BF16)


def split3(a):
    hi = a.astype(BF16)
    rest = a - hi.astype(F32)
    mid = rest.astype(BF16)
    return hi, mid, (rest - mid.astype(F32)).astype(BF16)


def mm(a, b, dims):
    return lax.dot_general(a, b, (dims, ((), ())), preferred_element_type=F32)


def mm3(a, b, dims):
    return mm(a[1], b[0], dims) + mm(a[0], b[1], dims) + mm(a[0], b[0], dims)


def mm6(a, b, dims):
    low = mm(a[1], b[1], dims) + (mm(a[2], b[0], dims) + mm(a[0], b[2], dims))
    return (low + (mm(a[1], b[0], dims) + mm(a[0], b[1], dims))) + mm(a[0], b[0], dims)


def call(kernel, out_shape, *args, after=(), scratch=(), work=1000, name=None):
    n = len(args)

    def run(*refs):
        kernel(*refs[:n], *refs[n + len(after) :])

    return pl.pallas_call(
        run,
        out_shape=out_shape,
        in_specs=[pl.BlockSpec(memory_space=pltpu.VMEM)] * n + [pl.BlockSpec(memory_space=pl.ANY)] * len(after),
        out_specs=jax.tree.map(lambda _: pl.BlockSpec(memory_space=pltpu.VMEM), out_shape),
        scratch_shapes=list(scratch),
        compiler_params=pltpu.CompilerParams(vmem_limit_bytes=48 * 2**20),
        cost_estimate=pl.CostEstimate(flops=work, bytes_accessed=0, transcendentals=0),
        name=name,
    )(*args, *after)


def project_kernel(rows_here, factor_ref, x_ref, y_ref, *copies):
    row = lax.axis_index("row")
    n_row = factor_ref.shape[1] // rows_here
    mine = factor_ref[:, :rows_here]
    for r in range(1, n_row):
        mine = jnp.where(row == r, factor_ref[:, r * rows_here : (r + 1) * rows_here], mine)
    y_ref[...] = mm3(split2(mine), split2(x_ref[...]), NN)
    for i, ref in enumerate(copies):
        ref[...] = x_ref[i * ref.shape[0] : (i + 1) * ref.shape[0], :]


def join_kernel(mine_ref, got_ref, x_ref, y_ref, copy_ref):
    y_ref[...] = mine_ref[...] + got_ref[...]
    copy_ref[...] = x_ref[...]


def term_kernel(scale, x_ref, mine_ref, got_ref, kept_ref, given_ref):
    core = lax.axis_index("col") % 2
    y = mine_ref[...] + got_ref[...]
    term = mm3(split2(y), split2(x_ref[...]), NT) * scale
    hr = term.shape[0] // 2
    kept_ref[...] = jnp.where(core == 0, term[:hr], term[hr:])
    given_ref[...] = jnp.where(core == 0, term[hr:], term[:hr])


def sum_kernel(mine_ref, got_ref, out_ref):
    out_ref[...] = mine_ref[...] + got_ref[...]


def stack_kernel(mine_ref, got_ref, both_ref):
    n = mine_ref.shape[0]
    both_ref[:n] = mine_ref[...]
    both_ref[n:] = got_ref[...]


def inverse_factor(inner):
    n = inner.shape[0]
    wide = -(-2 * n // 128) * 128
    r = lax.broadcasted_iota(jnp.int32, (n, wide), 0)
    c = lax.broadcasted_iota(jnp.int32, (n, wide), 1)
    w = jnp.where(c == r + n, F32(1.0), F32(0.0))
    w = w + jnp.concatenate([inner, jnp.zeros((n, wide - n), F32)], 1)
    w = [w[8 * i : 8 * i + 8] for i in range(n // 8)]
    sub = lax.broadcasted_iota(jnp.int32, (8, wide), 0)
    done = []
    for b in range(n // 8):
        cols = {
            j: [jnp.broadcast_to(w[i][:, 8 * b + j : 8 * b + j + 1], (8, wide)) for i in range(b, n // 8)]
            for j in range(8)
        }
        for k in range(8):
            pivot = jnp.broadcast_to(cols[k][0][k : k + 1], (8, wide))
            rs = lax.rsqrt(pivot)
            inv = rs * rs
            rs = rs * (1.5 - 0.5 * (pivot * inv))
            inv = inv * (2.0 - pivot * inv)
            row = jnp.broadcast_to(w[b][k : k + 1], (8, wide))
            done.append(row[:1] * rs[:1])
            below = [jnp.where(sub > k, cols[k][0], F32(0.0))] + cols[k][1:]
            m = [a * inv for a in below]
            for j in range(k + 1, 8):
                at = jnp.broadcast_to(cols[j][0][k : k + 1], (8, wide))
                if j == k + 1:
                    cols[j] = [a - (f * at) * inv for a, f in zip(cols[j], below)]
                else:
                    cols[j] = [a - f * at for a, f in zip(cols[j], m)]
            for i in range(b, n // 8):
                w[i] = w[i] - m[i - b] * row
    return jnp.concatenate(done, 0)[:, n : 2 * n]


def finish_kernel(n_row, counts, mine_ref, other_ref, *refs):
    total = sum(counts)
    pieces, (nf_ref, core_ref, rows_ref) = refs[:total], refs[total:]
    row = lax.axis_index("row")
    core = lax.axis_index("col") % 2
    _, hr, rows_here = mine_ref.shape
    rank = 2 * hr
    mode = rows_here * n_row
    blocks = []
    for s in range(n_row):
        mine, other = mine_ref[s], other_ref[s]
        first, second = jnp.where(core == 0, mine, other), jnp.where(core == 0, other, mine)
        blocks.append(jnp.concatenate([first, second], 0))
    split = [split3(b) for b in blocks]
    inner = tree_sum([gram6(s) for s in split]) * (1.0 / mode)
    inv = inverse_factor(inner)
    z, at = [], 0
    for s in range(n_row):
        start = 0
        for _ in range(counts[s]):
            x = pieces[at][...]
            hi, lo = split[s][0], split[s][1]
            if n_row == 4 and s in (1, 2):
                hi, lo = (jnp.where(core == 1, b, a) for a, b in zip((hi, lo), split[3 - s][:2]))
            stop = start + x.shape[0]
            z.append(mm3((hi[:, start:stop], lo[:, start:stop]), split2(x), NN))
            start, at = stop, at + 1
    z = tree_sum(z)
    rank_here = rank // n_row
    for i in range(n_row):
        rows_ref[i] = inv[i * rank_here : (i + 1) * rank_here]
    core_ref[...] = mm4(split2(rows_ref[row]), split2(z)) * (1.0 / math.sqrt(mode))
    inv2 = split2(inv)
    for s in range(n_row):
        block = mm4(inv2, split[s])
        if len(nf_ref.shape) == 3:
            nf_ref[row ^ s] = block
        else:
            nf_ref[:, pl.ds(pl.multiple_of((row ^ s) * rows_here, rows_here), rows_here)] = block


def gram_kernel(n_row, n_col, scale, counts, *refs):
    total = sum(counts)
    pieces, (given_ref, kept_ref, hi_ref, lo_ref, part_ref) = refs[:total], refs[total:]
    row = lax.axis_index("row")
    core = lax.axis_index("col") % 2
    n_z = n_col // 2
    rows_here = hi_ref.shape[1] * 2
    group = rows_here // 2
    half = group // n_col
    at = 0
    for s in range(n_row):
        hi, lo = [], []
        for _ in range(counts[s]):
            h, l = split2(pieces[at][...])
            hi.append(h)
            lo.append(l)
            at += 1
        hi, lo = jnp.concatenate(hi, 0), jnp.concatenate(lo, 0)
        owner = row ^ sided(s, n_row)
        for i in range(2):
            hi_ref[2 * owner + i] = hi[i * group : (i + 1) * group]
            lo_ref[2 * owner + i] = lo[i * group : (i + 1) * group]
    high = 2 * n_row - 1 - row
    left = (
        jnp.concatenate([hi_ref[high], hi_ref[row]], 0),
        jnp.concatenate([lo_ref[high], lo_ref[row]], 0),
    )
    for r in range(n_row):
        right = (
            jnp.concatenate([hi_ref[2 * r], hi_ref[2 * r + 1]], 0),
            jnp.concatenate([lo_ref[2 * r], lo_ref[2 * r + 1]], 0),
        )
        g = mm3(left, right, NT) * scale
        for i in range(2):
            for h in range(2):
                for p in range(n_col):
                    start = h * group + p * half
                    part_ref[h, 2 * r + i, p] = g[start : start + half, i * group : (i + 1) * group]
    n_high = 2 * n_row - row
    for b in range(2 * n_row + 1):
        is_low = (b >= n_high).astype(jnp.int32)
        block = b - is_low * n_high
        for zz in range(n_z):
            for ref, k in ((given_ref, 1 - core), (kept_ref, core)):
                owner = 2 * zz + k
                piece = jnp.where(is_low == 1, owner, n_col - 1 - owner)
                ref[zz, :, b * group : (b + 1) * group] = part_ref[is_low, block, piece]


def pieces_kernel(n_z, kept_ref, got_ref, keep_ref, give_ref):
    z = lax.axis_index("col") // 2
    for t in range(n_z):
        ref = give_ref if t % 2 else keep_ref
        ref[t // 2] = kept_ref[z ^ t] + got_ref[z ^ t]


def unpack_kernel(n_row, n_col, *refs):
    out_ref = refs[-1]
    row = lax.axis_index("row")
    owner = row * n_col + lax.axis_index("col")
    total = tree_sum([r[0] for r in refs[:-1]])
    half, width = total.shape
    mode = out_ref.shape[1]
    group = width - mode
    r = lax.broadcasted_iota(jnp.int32, (half, mode), 0)
    c = lax.broadcasted_iota(jnp.int32, (half, mode), 1)
    out_ref[half:, :] = jnp.where(c <= mode - (owner + 1) * half + r, total[:, :mode], F32(0.0))
    out_ref[:half, :] = jnp.zeros((half, mode), F32)
    for k in range(n_row):

        @pl.when(row == k)
        def _():
            start, stop = mode - k * group, mode + group
            keep = c[:, : stop - start] <= owner * half + r[:, : stop - start]
            out_ref[:half, : stop - start] = jnp.where(keep, total[:, start:stop], F32(0.0))


def body(unfolding, factor):
    n_row = lax.axis_size("row")
    n_col = lax.axis_size("col")
    n_z = n_col // 2
    rows_here, cols_here = unfolding.shape
    mode = rows_here * n_row
    rank = factor.shape[1]
    hr = rank // 2
    scale = 1.0 / (cols_here * n_col)
    group = rows_here // 2
    half = group // n_col
    width = mode + group

    def over_row(x, s):
        return lax.ppermute(x, "row", [(i, i ^ s) for i in range(n_row)])

    def over_side(x, s):
        pairs = [((r, c), (r ^ (3 - s if c % 2 else s), c)) for r in range(n_row) for c in range(n_col)]
        return lax.ppermute(x, ("row", "col"), [(a * n_col + b, p * n_col + q) for (a, b), (p, q) in pairs])

    def over_col(x, s):
        return lax.ppermute(x, "col", [(i, i ^ s) for i in range(n_col)])

    def steps(n):
        return [1 << k for k in range(n.bit_length() - 1)]

    y_shape = jax.ShapeDtypeStruct((rank, cols_here), F32)
    part_shape = jax.ShapeDtypeStruct((group, cols_here), F32)
    project = functools.partial(project_kernel, rows_here)
    if n_row == 4:
        two_low = over_side(unfolding[group:], 2)
        y, upper, lower = call(
            project,
            (y_shape, part_shape, part_shape),
            factor.T,
            unfolding,
            work=COST["project"],
            name="project",
        )
        got = over_side(y, 1)
        one_up = over_side(upper, 1)
        one_low = over_side(lower, 1)
        y, upper = call(
            join_kernel, (y_shape, part_shape), y, got, upper, work=COST["join"], name="join"
        )
        y_got = over_side(y, 2)
        two_up = over_side(upper, 2)
        three = [over_side(one_up, 2), over_side(two_low, 1)]
        blocks = [[unfolding], [one_up, one_low], [two_up, two_low], three]
    else:
        (y,) = call(project, (y_shape,), factor.T, unfolding, work=COST["project"], name="project")
        for s in steps(n_row)[:-1]:
            y = y + over_row(y, s)
        y_got = over_row(y, n_row // 2)
        blocks = [[unfolding]] + [[over_row(unfolding, s)] for s in range(1, n_row)]
    counts = tuple(len(b) for b in blocks)
    blocks = [p for b in blocks for p in b]

    kept, given = call(
        functools.partial(term_kernel, scale),
        (jax.ShapeDtypeStruct((hr, rows_here), F32),) * 2,
        unfolding,
        y,
        y_got,
        work=COST["term"],
        name="term",
    )
    image = call(
        sum_kernel,
        jax.ShapeDtypeStruct((hr, rows_here), F32),
        kept,
        over_col(given, 1),
        work=COST["core_sum"],
        name="core_sum",
    )

    def z_sum(image, s, after):
        return call(
            sum_kernel,
            jax.ShapeDtypeStruct((hr, rows_here), F32),
            image,
            over_col(image, 2 * s),
            after=after,
            work=COST["sum"],
            name="z_sum",
        )

    for s in steps(n_z)[:-1]:
        image = z_sum(image, s, [])

    given, kept = call(
        functools.partial(gram_kernel, n_row, n_col, scale, counts),
        (jax.ShapeDtypeStruct((n_z, half, width), F32),) * 2,
        *blocks,
        scratch=[
            pltpu.VMEM((2 * n_row, group, cols_here), BF16),
            pltpu.VMEM((2 * n_row, group, cols_here), BF16),
            pltpu.VMEM((2, 2 * n_row, n_col, half, group), F32),
        ],
        after=[image],
        work=COST["gram"],
        name="gram",
    )
    image = z_sum(image, n_z // 2, [given])
    mine = image[None]
    for s in steps(n_row):
        mine = call(
            stack_kernel,
            jax.ShapeDtypeStruct((2 * s, hr, rows_here), F32),
            mine,
            over_row(mine, s),
            work=COST["stack"],
            name="stack",
        )
    other = over_col(mine, 1)

    rank_here = rank // n_row
    whole = rows_here % 128 == 0
    nf, core_out = call(
        functools.partial(finish_kernel, n_row, counts),
        (
            jax.ShapeDtypeStruct((rank, mode) if whole else (n_row, rank, rows_here), F32),
            jax.ShapeDtypeStruct((rank_here, cols_here), F32),
        ),
        mine,
        other,
        *blocks,
        scratch=[pltpu.VMEM((n_row, rank_here, rank), F32)],
        work=COST["finish"],
        name="finish",
    )
    new_factor = nf.T if whole else nf.transpose(0, 2, 1).reshape(mode, rank)

    keep, give = call(
        functools.partial(pieces_kernel, n_z),
        (jax.ShapeDtypeStruct((n_z // 2, half, width), F32),) * 2,
        kept,
        over_col(given, 1),
        work=COST["pieces"],
        name="pieces",
    )
    got = over_col(give, 2)
    for s in steps(n_z)[1:]:
        keep, give = keep[0::2] + got[0::2], keep[1::2] + got[1::2]
        got = over_col(give, 2 * s)
    gram_lower = call(
        functools.partial(unpack_kernel, n_row, n_col),
        jax.ShapeDtypeStruct((2 * half, mode), F32),
        keep,
        got,
        work=COST["unpack"],
        name="unpack",
    )
    return gram_lower, new_factor, core_out


def solution(mesh):
    in_specs = (P("row", "col"), P())
    out_specs = (P(("row", "col"), None), P(), P("row", "col"))
    return jax.shard_map(body, mesh=mesh, in_specs=in_specs, out_specs=out_specs, check_vma=False)
```

```python
import functools
import math

import jax
import jax.numpy as jnp
from jax import lax
from jax.experimental import pallas as pl
from jax.experimental.pallas import tpu as pltpu
from jax.sharding import PartitionSpec as P

F32 = jnp.float32
BF16 = jnp.bfloat16
NN = ((1,), (0,))
NT = ((1,), (1,))


COST = dict(project=10**6, join=10**6, term=10**10, core_sum=10**6, sum=10**6, stack=3 * 10**9, finish=10**10, gram=10**6, pieces=10**6, unpack=10**6)


def tree_sum(parts):
    while len(parts) > 1:
        paired = [a + b for a, b in zip(parts[::2], parts[1::2])]
        parts = paired + parts[2 * len(paired) :]
    return parts[0]


def split2(a):
    hi = a.astype(BF16)
    return hi, (a - hi.astype(F32)).astype(BF16)


def split3(a):
    hi = a.astype(BF16)
    rest = a - hi.astype(F32)
    mid = rest.astype(BF16)
    return hi, mid, (rest - mid.astype(F32)).astype(BF16)


def sided(s, n_row):
    if n_row != 4 or s in (0, 3):
        return s
    return jnp.where(lax.axis_index("col") % 2 == 1, 3 - s, s)


def mm(a, b, dims):
    return lax.dot_general(a, b, (dims, ((), ())), preferred_element_type=F32)


def mm3(a, b, dims):
    return mm(a[1], b[0], dims) + mm(a[0], b[1], dims) + mm(a[0], b[0], dims)


def mm4(a, b):
    left = jnp.concatenate([a[0], a[0], a[1], a[1]], 1)
    return mm(left, jnp.concatenate([b[0], b[1], b[0], b[1]], 0), NN)


def gram6(a):
    n = a[0].shape[0]
    s = jnp.concatenate(a, 0)
    g = mm(s, s, NT)

    def at(i, j):
        return g[i * n : (i + 1) * n, j * n : (j + 1) * n]

    return at(0, 0) + ((at(0, 1) + at(1, 0)) + (at(1, 1) + (at(0, 2) + at(2, 0))))


COST = dict(project=10**6, join=10**6, term=10**10, core_sum=10**6, sum=10**6, stack=3 * 10**9, finish=10**10, gram=10**6, pieces=10**6, unpack=10**6)


def tree_sum(parts):
    while len(parts) > 1:
        paired = [a + b for a, b in zip(parts[::2], parts[1::2])]
        parts = paired + parts[2 * len(paired) :]
    return parts[0]


def split2(a):
    hi = a.astype(BF16)
    return hi, (a - hi.astype(F32)).astype(BF16)


def split3(a):
    hi = a.astype(BF16)
    rest = a - hi.astype(F32)
    mid = rest.astype(BF16)
    return hi, mid, (rest - mid.astype(F32)).astype(BF16)


def mm(a, b, dims):
    return lax.dot_general(a, b, (dims, ((), ())), preferred_element_type=F32)


def mm3(a, b, dims):
    return mm(a[1], b[0], dims) + mm(a[0], b[1], dims) + mm(a[0], b[0], dims)


def mm6(a, b, dims):
    low = mm(a[1], b[1], dims) + (mm(a[2], b[0], dims) + mm(a[0], b[2], dims))
    return (low + (mm(a[1], b[0], dims) + mm(a[0], b[1], dims))) + mm(a[0], b[0], dims)


def call(kernel, out_shape, *args, after=(), scratch=(), work=1000, name=None):
    n = len(args)

    def run(*refs):
        kernel(*refs[:n], *refs[n + len(after) :])

    return pl.pallas_call(
        run,
        out_shape=out_shape,
        in_specs=[pl.BlockSpec(memory_space=pltpu.VMEM)] * n + [pl.BlockSpec(memory_space=pl.ANY)] * len(after),
        out_specs=jax.tree.map(lambda _: pl.BlockSpec(memory_space=pltpu.VMEM), out_shape),
        scratch_shapes=list(scratch),
        compiler_params=pltpu.CompilerParams(vmem_limit_bytes=48 * 2**20),
        cost_estimate=pl.CostEstimate(flops=work, bytes_accessed=0, transcendentals=0),
        name=name,
    )(*args, *after)


def project_kernel(rows_here, factor_ref, x_ref, y_ref, *copies):
    row = lax.axis_index("row")
    n_row = factor_ref.shape[1] // rows_here
    mine = factor_ref[:, :rows_here]
    for r in range(1, n_row):
        mine = jnp.where(row == r, factor_ref[:, r * rows_here : (r + 1) * rows_here], mine)
    y_ref[...] = mm3(split2(mine), split2(x_ref[...]), NN)
    for i, ref in enumerate(copies):
        ref[...] = x_ref[i * ref.shape[0] : (i + 1) * ref.shape[0], :]


def join_kernel(mine_ref, got_ref, x_ref, y_ref, copy_ref):
    y_ref[...] = mine_ref[...] + got_ref[...]
    copy_ref[...] = x_ref[...]


def term_kernel(scale, x_ref, mine_ref, got_ref, term_ref):
    y = mine_ref[...] + got_ref[...]
    term_ref[...] = mm3(split2(y), split2(x_ref[...]), NT) * scale


def sum_kernel(mine_ref, got_ref, out_ref):
    out_ref[...] = mine_ref[...] + got_ref[...]


def stack_kernel(mine_ref, got_ref, both_ref):
    n = mine_ref.shape[0]
    both_ref[:n] = mine_ref[...]
    both_ref[n:] = got_ref[...]


def inverse_factor(inner):
    n = inner.shape[0]
    wide = -(-2 * n // 128) * 128
    r = lax.broadcasted_iota(jnp.int32, (n, wide), 0)
    c = lax.broadcasted_iota(jnp.int32, (n, wide), 1)
    w = jnp.where(c == r + n, F32(1.0), F32(0.0))
    w = w + jnp.concatenate([inner, jnp.zeros((n, wide - n), F32)], 1)
    w = [w[8 * i : 8 * i + 8] for i in range(n // 8)]
    sub = lax.broadcasted_iota(jnp.int32, (8, wide), 0)
    done = []
    for b in range(n // 8):
        cols = {
            j: [jnp.broadcast_to(w[i][:, 8 * b + j : 8 * b + j + 1], (8, wide)) for i in range(b, n // 8)]
            for j in range(8)
        }
        for k in range(8):
            pivot = jnp.broadcast_to(cols[k][0][k : k + 1], (8, wide))
            rs = lax.rsqrt(pivot)
            inv = rs * rs
            rs = rs * (1.5 - 0.5 * (pivot * inv))
            inv = inv * (2.0 - pivot * inv)
            row = jnp.broadcast_to(w[b][k : k + 1], (8, wide))
            done.append(row[:1] * rs[:1])
            below = [jnp.where(sub > k, cols[k][0], F32(0.0))] + cols[k][1:]
            m = [a * inv for a in below]
            for j in range(k + 1, 8):
                at = jnp.broadcast_to(cols[j][0][k : k + 1], (8, wide))
                if j == k + 1:
                    cols[j] = [a - (f * at) * inv for a, f in zip(cols[j], below)]
                else:
                    cols[j] = [a - f * at for a, f in zip(cols[j], m)]
            for i in range(b, n // 8):
                w[i] = w[i] - m[i - b] * row
    return jnp.concatenate(done, 0)[:, n : 2 * n]


def finish_kernel(n_row, counts, mine_ref, other_ref, *refs):
    total = sum(counts)
    pieces, (nf_ref, core_ref, rows_ref) = refs[:total], refs[total:]
    row = lax.axis_index("row")
    core = lax.axis_index("col") % 2
    _, rank, rows_here = mine_ref.shape
    mode = rows_here * n_row
    blocks = [jnp.where(core == 1, mine_ref[s], other_ref[s]) for s in range(n_row)]
    split = [split3(b) for b in blocks]
    inner = tree_sum([gram6(s) for s in split]) * (1.0 / mode)
    inv = inverse_factor(inner)
    z, at = [], 0
    for s in range(n_row):
        start = 0
        for _ in range(counts[s]):
            x = pieces[at][...]
            hi, lo = split[s][0], split[s][1]
            if n_row == 4 and s in (1, 2):
                hi, lo = (jnp.where(core == 1, b, a) for a, b in zip((hi, lo), split[3 - s][:2]))
            stop = start + x.shape[0]
            z.append(mm3((hi[:, start:stop], lo[:, start:stop]), split2(x), NN))
            start, at = stop, at + 1
    z = tree_sum(z)
    rank_here = rank // n_row
    for i in range(n_row):
        rows_ref[i] = inv[i * rank_here : (i + 1) * rank_here]
    core_ref[...] = mm4(split2(rows_ref[row]), split2(z)) * (1.0 / math.sqrt(mode))
    inv2 = split2(inv)
    for s in range(n_row):
        block = mm4(inv2, split[s])
        if len(nf_ref.shape) == 3:
            nf_ref[row ^ s] = block
        else:
            nf_ref[:, pl.ds(pl.multiple_of((row ^ s) * rows_here, rows_here), rows_here)] = block


def gram_kernel(n_row, n_col, scale, counts, *refs):
    total = sum(counts)
    pieces, (given_ref, kept_ref, hi_ref, lo_ref, part_ref) = refs[:total], refs[total:]
    row = lax.axis_index("row")
    core = lax.axis_index("col") % 2
    n_z = n_col // 2
    rows_here = hi_ref.shape[1] * 2
    group = rows_here // 2
    half = group // n_col
    at = 0
    for s in range(n_row):
        hi, lo = [], []
        for _ in range(counts[s]):
            h, l = split2(pieces[at][...])
            hi.append(h)
            lo.append(l)
            at += 1
        hi, lo = jnp.concatenate(hi, 0), jnp.concatenate(lo, 0)
        owner = row ^ sided(s, n_row)
        for i in range(2):
            hi_ref[2 * owner + i] = hi[i * group : (i + 1) * group]
            lo_ref[2 * owner + i] = lo[i * group : (i + 1) * group]
    high = 2 * n_row - 1 - row
    left = (
        jnp.concatenate([hi_ref[high], hi_ref[row]], 0),
        jnp.concatenate([lo_ref[high], lo_ref[row]], 0),
    )
    for r in range(n_row):
        right = (
            jnp.concatenate([hi_ref[2 * r], hi_ref[2 * r + 1]], 0),
            jnp.concatenate([lo_ref[2 * r], lo_ref[2 * r + 1]], 0),
        )
        g = mm3(left, right, NT) * scale
        for i in range(2):
            for h in range(2):
                for p in range(n_col):
                    start = h * group + p * half
                    part_ref[h, 2 * r + i, p] = g[start : start + half, i * group : (i + 1) * group]
    n_high = 2 * n_row - row
    for b in range(2 * n_row + 1):
        is_low = (b >= n_high).astype(jnp.int32)
        block = b - is_low * n_high
        for zz in range(n_z):
            for ref, k in ((given_ref, 1 - core), (kept_ref, core)):
                owner = 2 * zz + k
                piece = jnp.where(is_low == 1, owner, n_col - 1 - owner)
                ref[zz, :, b * group : (b + 1) * group] = part_ref[is_low, block, piece]


def pieces_kernel(n_z, kept_ref, got_ref, keep_ref, give_ref):
    z = lax.axis_index("col") // 2
    for t in range(n_z):
        ref = give_ref if t % 2 else keep_ref
        ref[t // 2] = kept_ref[z ^ t] + got_ref[z ^ t]


def unpack_kernel(n_row, n_col, *refs):
    out_ref = refs[-1]
    row = lax.axis_index("row")
    owner = row * n_col + lax.axis_index("col")
    total = tree_sum([r[0] for r in refs[:-1]])
    half, width = total.shape
    mode = out_ref.shape[1]
    group = width - mode
    r = lax.broadcasted_iota(jnp.int32, (half, mode), 0)
    c = lax.broadcasted_iota(jnp.int32, (half, mode), 1)
    out_ref[half:, :] = jnp.where(c <= mode - (owner + 1) * half + r, total[:, :mode], F32(0.0))
    out_ref[:half, :] = jnp.zeros((half, mode), F32)
    for k in range(n_row):

        @pl.when(row == k)
        def _():
            start, stop = mode - k * group, mode + group
            keep = c[:, : stop - start] <= owner * half + r[:, : stop - start]
            out_ref[:half, : stop - start] = jnp.where(keep, total[:, start:stop], F32(0.0))


def body(unfolding, factor):
    n_row = lax.axis_size("row")
    n_col = lax.axis_size("col")
    n_z = n_col // 2
    rows_here, cols_here = unfolding.shape
    mode = rows_here * n_row
    rank = factor.shape[1]
    scale = 1.0 / (cols_here * n_col)
    group = rows_here // 2
    half = group // n_col
    width = mode + group

    def over_row(x, s):
        return lax.ppermute(x, "row", [(i, i ^ s) for i in range(n_row)])

    def over_side(x, s):
        pairs = [((r, c), (r ^ (3 - s if c % 2 else s), c)) for r in range(n_row) for c in range(n_col)]
        return lax.ppermute(x, ("row", "col"), [(a * n_col + b, p * n_col + q) for (a, b), (p, q) in pairs])

    def over_col(x, s):
        return lax.ppermute(x, "col", [(i, i ^ s) for i in range(n_col)])

    def to_core(x, core):
        return lax.ppermute(x, "col", [(i, i ^ 1) for i in range(n_col) if i % 2 != core])

    def over_z_core_1(x, s):
        return lax.ppermute(x, "col", [(i, i ^ (2 * s)) for i in range(1, n_col, 2)])

    def over_row_core_1(x, s):
        pairs = [(r * n_col + c, (r ^ s) * n_col + c) for r in range(n_row) for c in range(1, n_col, 2)]
        return lax.ppermute(x, ("row", "col"), pairs)

    def steps(n):
        return [1 << k for k in range(n.bit_length() - 1)]

    y_shape = jax.ShapeDtypeStruct((rank, cols_here), F32)
    part_shape = jax.ShapeDtypeStruct((group, cols_here), F32)
    project = functools.partial(project_kernel, rows_here)
    if n_row == 4:
        two_low = over_side(unfolding[group:], 2)
        y, upper, lower = call(
            project,
            (y_shape, part_shape, part_shape),
            factor.T,
            unfolding,
            work=COST["project"],
            name="project",
        )
        got = over_side(y, 1)
        one_up = over_side(upper, 1)
        one_low = over_side(lower, 1)
        y, upper = call(
            join_kernel, (y_shape, part_shape), y, got, upper, after=[two_low], work=COST["join"], name="join"
        )
        y_got = over_side(y, 2)
        two_up = over_side(upper, 2)
        three = [over_side(one_up, 2), over_side(two_low, 1)]
        blocks = [[unfolding], [one_up, one_low], [two_up, two_low], three]
    else:
        (y,) = call(project, (y_shape,), factor.T, unfolding, work=COST["project"], name="project")
        for s in steps(n_row)[:-1]:
            y = y + over_row(y, s)
        y_got = over_row(y, n_row // 2)
        blocks = [[unfolding]] + [[over_row(unfolding, s)] for s in range(1, n_row)]
    counts = tuple(len(b) for b in blocks)
    blocks = [p for b in blocks for p in b]

    image_shape = jax.ShapeDtypeStruct((rank, rows_here), F32)
    term = call(
        functools.partial(term_kernel, scale),
        image_shape,
        unfolding,
        y,
        y_got,
        work=COST["term"],
        name="term",
    )
    image = call(sum_kernel, image_shape, term, to_core(term, 1), work=COST["core_sum"], name="core_sum")

    def z_sum(image, s, after):
        return call(
            sum_kernel,
            image_shape,
            image,
            over_z_core_1(image, s),
            after=after,
            work=COST["sum"],
            name="z_sum",
        )

    for s in steps(n_z)[:-1]:
        image = z_sum(image, s, [])

    given, kept = call(
        functools.partial(gram_kernel, n_row, n_col, scale, counts),
        (jax.ShapeDtypeStruct((n_z, half, width), F32),) * 2,
        *blocks,
        scratch=[
            pltpu.VMEM((2 * n_row, group, cols_here), BF16),
            pltpu.VMEM((2 * n_row, group, cols_here), BF16),
            pltpu.VMEM((2, 2 * n_row, n_col, half, group), F32),
        ],
        after=[image],
        work=COST["gram"],
        name="gram",
    )
    image = z_sum(image, n_z // 2, [given])
    mine = image[None]
    for s in steps(n_row):
        mine = call(
            stack_kernel,
            jax.ShapeDtypeStruct((2 * s, rank, rows_here), F32),
            mine,
            over_row_core_1(mine, s),
            work=COST["stack"],
            name="stack",
        )
    other = to_core(mine, 0)

    rank_here = rank // n_row
    whole = rows_here % 128 == 0
    nf, core_out = call(
        functools.partial(finish_kernel, n_row, counts),
        (
            jax.ShapeDtypeStruct((rank, mode) if whole else (n_row, rank, rows_here), F32),
            jax.ShapeDtypeStruct((rank_here, cols_here), F32),
        ),
        mine,
        other,
        *blocks,
        scratch=[pltpu.VMEM((n_row, rank_here, rank), F32)],
        work=COST["finish"],
        name="finish",
    )
    new_factor = nf.T if whole else nf.transpose(0, 2, 1).reshape(mode, rank)

    keep, give = call(
        functools.partial(pieces_kernel, n_z),
        (jax.ShapeDtypeStruct((n_z // 2, half, width), F32),) * 2,
        kept,
        over_col(given, 1),
        work=COST["pieces"],
        name="pieces",
    )
    got = over_col(give, 2)
    for s in steps(n_z)[1:]:
        keep, give = keep[0::2] + got[0::2], keep[1::2] + got[1::2]
        got = over_col(give, 2 * s)
    gram_lower = call(
        functools.partial(unpack_kernel, n_row, n_col),
        jax.ShapeDtypeStruct((2 * half, mode), F32),
        keep,
        got,
        work=COST["unpack"],
        name="unpack",
    )
    return gram_lower, new_factor, core_out


def solution(mesh):
    in_specs = (P("row", "col"), P())
    out_specs = (P(("row", "col"), None), P(), P("row", "col"))
    return jax.shard_map(body, mesh=mesh, in_specs=in_specs, out_specs=out_specs, check_vma=False)
```

```python
import functools
import math

import jax
import jax.numpy as jnp
from jax import lax
from jax.experimental import pallas as pl
from jax.experimental.pallas import tpu as pltpu
from jax.sharding import PartitionSpec as P

F32 = jnp.float32
BF16 = jnp.bfloat16
NN = ((1,), (0,))
NT = ((1,), (1,))


COST = dict(project=10**6, join=10**6, term=10**10, core_sum=10**6, sum=10**6, stack=3 * 10**9, finish=10**10, gram=10**6, pieces=10**6, unpack=10**6)


def tree_sum(parts):
    while len(parts) > 1:
        paired = [a + b for a, b in zip(parts[::2], parts[1::2])]
        parts = paired + parts[2 * len(paired) :]
    return parts[0]


def split2(a):
    hi = a.astype(BF16)
    return hi, (a - hi.astype(F32)).astype(BF16)


def split3(a):
    hi = a.astype(BF16)
    rest = a - hi.astype(F32)
    mid = rest.astype(BF16)
    return hi, mid, (rest - mid.astype(F32)).astype(BF16)


def sided(s, n_row):
    if n_row != 4 or s in (0, 3):
        return s
    return jnp.where(lax.axis_index("col") % 2 == 1, 3 - s, s)


def mm(a, b, dims):
    return lax.dot_general(a, b, (dims, ((), ())), preferred_element_type=F32)


def mm3(a, b, dims):
    return mm(a[1], b[0], dims) + mm(a[0], b[1], dims) + mm(a[0], b[0], dims)


def mm4(a, b):
    left = jnp.concatenate([a[0], a[0], a[1], a[1]], 1)
    return mm(left, jnp.concatenate([b[0], b[1], b[0], b[1]], 0), NN)


def gram6(a):
    n = a[0].shape[0]
    s = jnp.concatenate(a, 0)
    g = mm(s, s, NT)

    def at(i, j):
        return g[i * n : (i + 1) * n, j * n : (j + 1) * n]

    return at(0, 0) + ((at(0, 1) + at(1, 0)) + (at(1, 1) + (at(0, 2) + at(2, 0))))


COST = dict(project=10**6, join=10**6, term=10**10, core_sum=10**6, sum=10**6, stack=3 * 10**9, finish=10**10, gram=10**6, pieces=10**6, unpack=10**6)


def tree_sum(parts):
    while len(parts) > 1:
        paired = [a + b for a, b in zip(parts[::2], parts[1::2])]
        parts = paired + parts[2 * len(paired) :]
    return parts[0]


def split2(a):
    hi = a.astype(BF16)
    return hi, (a - hi.astype(F32)).astype(BF16)


def split3(a):
    hi = a.astype(BF16)
    rest = a - hi.astype(F32)
    mid = rest.astype(BF16)
    return hi, mid, (rest - mid.astype(F32)).astype(BF16)


def mm(a, b, dims):
    return lax.dot_general(a, b, (dims, ((), ())), preferred_element_type=F32)


def mm3(a, b, dims):
    return mm(a[1], b[0], dims) + mm(a[0], b[1], dims) + mm(a[0], b[0], dims)


def mm6(a, b, dims):
    low = mm(a[1], b[1], dims) + (mm(a[2], b[0], dims) + mm(a[0], b[2], dims))
    return (low + (mm(a[1], b[0], dims) + mm(a[0], b[1], dims))) + mm(a[0], b[0], dims)


def call(kernel, out_shape, *args, after=(), scratch=(), work=1000, name=None):
    n = len(args)

    def run(*refs):
        kernel(*refs[:n], *refs[n + len(after) :])

    return pl.pallas_call(
        run,
        out_shape=out_shape,
        in_specs=[pl.BlockSpec(memory_space=pltpu.VMEM)] * n + [pl.BlockSpec(memory_space=pl.ANY)] * len(after),
        out_specs=jax.tree.map(lambda _: pl.BlockSpec(memory_space=pltpu.VMEM), out_shape),
        scratch_shapes=list(scratch),
        compiler_params=pltpu.CompilerParams(vmem_limit_bytes=48 * 2**20),
        cost_estimate=pl.CostEstimate(flops=work, bytes_accessed=0, transcendentals=0),
        name=name,
    )(*args, *after)


def project_kernel(rows_here, factor_ref, x_ref, y_ref, *copies):
    row = lax.axis_index("row")
    n_row = factor_ref.shape[1] // rows_here
    mine = factor_ref[:, :rows_here]
    for r in range(1, n_row):
        mine = jnp.where(row == r, factor_ref[:, r * rows_here : (r + 1) * rows_here], mine)
    y_ref[...] = mm3(split2(mine), split2(x_ref[...]), NN)
    for i, ref in enumerate(copies):
        ref[...] = x_ref[i * ref.shape[0] : (i + 1) * ref.shape[0], :]


def join_kernel(mine_ref, got_ref, x_ref, y_ref, copy_ref):
    y_ref[...] = mine_ref[...] + got_ref[...]
    copy_ref[...] = x_ref[...]


def term_kernel(scale, x_ref, mine_ref, got_ref, kept_ref, given_ref):
    core = lax.axis_index("col") % 2
    y = mine_ref[...] + got_ref[...]
    term = mm3(split2(y), split2(x_ref[...]), NT) * scale
    hr = term.shape[0] // 2
    kept_ref[...] = jnp.where(core == 0, term[:hr], term[hr:])
    given_ref[...] = jnp.where(core == 0, term[hr:], term[:hr])


def sum_kernel(mine_ref, got_ref, out_ref):
    out_ref[...] = mine_ref[...] + got_ref[...]


def stack_kernel(mine_ref, got_ref, both_ref):
    n = mine_ref.shape[0]
    both_ref[:n] = mine_ref[...]
    both_ref[n:] = got_ref[...]


def inverse_factor(inner):
    n = inner.shape[0]
    wide = -(-2 * n // 128) * 128
    r = lax.broadcasted_iota(jnp.int32, (n, wide), 0)
    c = lax.broadcasted_iota(jnp.int32, (n, wide), 1)
    w = jnp.where(c == r + n, F32(1.0), F32(0.0))
    w = w + jnp.concatenate([inner, jnp.zeros((n, wide - n), F32)], 1)
    w = [w[8 * i : 8 * i + 8] for i in range(n // 8)]
    sub = lax.broadcasted_iota(jnp.int32, (8, wide), 0)
    done = []
    for b in range(n // 8):
        cols = {
            j: [jnp.broadcast_to(w[i][:, 8 * b + j : 8 * b + j + 1], (8, wide)) for i in range(b, n // 8)]
            for j in range(8)
        }
        for k in range(8):
            pivot = jnp.broadcast_to(cols[k][0][k : k + 1], (8, wide))
            rs = lax.rsqrt(pivot)
            inv = rs * rs
            rs = rs * (1.5 - 0.5 * (pivot * inv))
            inv = inv * (2.0 - pivot * inv)
            row = jnp.broadcast_to(w[b][k : k + 1], (8, wide))
            done.append(row[:1] * rs[:1])
            below = [jnp.where(sub > k, cols[k][0], F32(0.0))] + cols[k][1:]
            m = [a * inv for a in below]
            for j in range(k + 1, 8):
                at = jnp.broadcast_to(cols[j][0][k : k + 1], (8, wide))
                if j == k + 1:
                    cols[j] = [a - (f * at) * inv for a, f in zip(cols[j], below)]
                else:
                    cols[j] = [a - f * at for a, f in zip(cols[j], m)]
            for i in range(b, n // 8):
                w[i] = w[i] - m[i - b] * row
    return jnp.concatenate(done, 0)[:, n : 2 * n]


def finish_kernel(n_row, counts, mine_ref, other_ref, *refs):
    total = sum(counts)
    pieces, (nf_ref, core_ref, rows_ref) = refs[:total], refs[total:]
    row = lax.axis_index("row")
    core = lax.axis_index("col") % 2
    _, hr, rows_here = mine_ref.shape
    rank = 2 * hr
    mode = rows_here * n_row
    blocks = []
    for s in range(n_row):
        mine, other = mine_ref[s], other_ref[s]
        first, second = jnp.where(core == 0, mine, other), jnp.where(core == 0, other, mine)
        blocks.append(jnp.concatenate([first, second], 0))
    split = [split3(b) for b in blocks]
    inner = tree_sum([gram6(s) for s in split]) * (1.0 / mode)
    inv = inverse_factor(inner)
    z, at = [], 0
    for s in range(n_row):
        start = 0
        for _ in range(counts[s]):
            x = pieces[at][...]
            hi, lo = split[s][0], split[s][1]
            if n_row == 4 and s in (1, 2):
                hi, lo = (jnp.where(core == 1, b, a) for a, b in zip((hi, lo), split[3 - s][:2]))
            stop = start + x.shape[0]
            z.append(mm3((hi[:, start:stop], lo[:, start:stop]), split2(x), NN))
            start, at = stop, at + 1
    z = tree_sum(z)
    rank_here = rank // n_row
    for i in range(n_row):
        rows_ref[i] = inv[i * rank_here : (i + 1) * rank_here]
    core_ref[...] = mm4(split2(rows_ref[row]), split2(z)) * (1.0 / math.sqrt(mode))
    inv2 = split2(inv)
    for s in range(n_row):
        block = mm4(inv2, split[s])
        if len(nf_ref.shape) == 3:
            nf_ref[row ^ s] = block
        else:
            nf_ref[:, pl.ds(pl.multiple_of((row ^ s) * rows_here, rows_here), rows_here)] = block


def gram_kernel(n_row, n_col, scale, counts, *refs):
    total = sum(counts)
    pieces, (given_ref, kept_ref, hi_ref, lo_ref, part_ref) = refs[:total], refs[total:]
    row = lax.axis_index("row")
    core = lax.axis_index("col") % 2
    n_z = n_col // 2
    rows_here = hi_ref.shape[1] * 2
    group = rows_here // 2
    half = group // n_col
    at = 0
    for s in range(n_row):
        hi, lo = [], []
        for _ in range(counts[s]):
            h, l = split2(pieces[at][...])
            hi.append(h)
            lo.append(l)
            at += 1
        hi, lo = jnp.concatenate(hi, 0), jnp.concatenate(lo, 0)
        owner = row ^ sided(s, n_row)
        for i in range(2):
            hi_ref[2 * owner + i] = hi[i * group : (i + 1) * group]
            lo_ref[2 * owner + i] = lo[i * group : (i + 1) * group]
    high = 2 * n_row - 1 - row
    left = (
        jnp.concatenate([hi_ref[high], hi_ref[row]], 0),
        jnp.concatenate([lo_ref[high], lo_ref[row]], 0),
    )
    for r in range(n_row):
        right = (
            jnp.concatenate([hi_ref[2 * r], hi_ref[2 * r + 1]], 0),
            jnp.concatenate([lo_ref[2 * r], lo_ref[2 * r + 1]], 0),
        )
        g = mm3(left, right, NT) * scale
        for i in range(2):
            for h in range(2):
                for p in range(n_col):
                    start = h * group + p * half
                    part_ref[h, 2 * r + i, p] = g[start : start + half, i * group : (i + 1) * group]
    n_high = 2 * n_row - row
    for b in range(2 * n_row + 1):
        is_low = (b >= n_high).astype(jnp.int32)
        block = b - is_low * n_high
        for zz in range(n_z):
            for ref, k in ((given_ref, 1 - core), (kept_ref, core)):
                owner = 2 * zz + k
                piece = jnp.where(is_low == 1, owner, n_col - 1 - owner)
                ref[zz, :, b * group : (b + 1) * group] = part_ref[is_low, block, piece]


def pieces_kernel(n_z, kept_ref, got_ref, keep_ref, give_ref):
    z = lax.axis_index("col") // 2
    for t in range(n_z):
        ref = give_ref if t % 2 else keep_ref
        ref[t // 2] = kept_ref[z ^ t] + got_ref[z ^ t]


def unpack_kernel(n_row, n_col, *refs):
    out_ref = refs[-1]
    row = lax.axis_index("row")
    owner = row * n_col + lax.axis_index("col")
    total = tree_sum([r[0] for r in refs[:-1]])
    half, width = total.shape
    mode = out_ref.shape[1]
    group = width - mode
    r = lax.broadcasted_iota(jnp.int32, (half, mode), 0)
    c = lax.broadcasted_iota(jnp.int32, (half, mode), 1)
    out_ref[half:, :] = jnp.where(c <= mode - (owner + 1) * half + r, total[:, :mode], F32(0.0))
    out_ref[:half, :] = jnp.zeros((half, mode), F32)
    for k in range(n_row):

        @pl.when(row == k)
        def _():
            start, stop = mode - k * group, mode + group
            keep = c[:, : stop - start] <= owner * half + r[:, : stop - start]
            out_ref[:half, : stop - start] = jnp.where(keep, total[:, start:stop], F32(0.0))


def body(unfolding, factor):
    n_row = lax.axis_size("row")
    n_col = lax.axis_size("col")
    n_z = n_col // 2
    rows_here, cols_here = unfolding.shape
    mode = rows_here * n_row
    rank = factor.shape[1]
    hr = rank // 2
    scale = 1.0 / (cols_here * n_col)
    group = rows_here // 2
    half = group // n_col
    width = mode + group

    def over_row(x, s):
        return lax.ppermute(x, "row", [(i, i ^ s) for i in range(n_row)])

    def over_side(x, s):
        pairs = [((r, c), (r ^ (3 - s if c % 2 else s), c)) for r in range(n_row) for c in range(n_col)]
        return lax.ppermute(x, ("row", "col"), [(a * n_col + b, p * n_col + q) for (a, b), (p, q) in pairs])

    def over_col(x, s):
        return lax.ppermute(x, "col", [(i, i ^ s) for i in range(n_col)])

    def steps(n):
        return [1 << k for k in range(n.bit_length() - 1)]

    y_shape = jax.ShapeDtypeStruct((rank, cols_here), F32)
    part_shape = jax.ShapeDtypeStruct((group, cols_here), F32)
    project = functools.partial(project_kernel, rows_here)
    if n_row == 4:
        two_low = over_side(unfolding[group:], 2)
        y, upper, lower = call(
            project,
            (y_shape, part_shape, part_shape),
            factor.T,
            unfolding,
            work=COST["project"],
            name="project",
        )
        got = over_side(y, 1)
        one_up = over_side(upper, 1)
        one_low = over_side(lower, 1)
        y, upper = call(
            join_kernel, (y_shape, part_shape), y, got, upper, work=COST["join"], name="join"
        )
        y_got = over_side(y, 2)
        two_up = over_side(upper, 2)
        three = [over_side(one_up, 2), over_side(two_low, 1)]
        blocks = [[unfolding], [one_up, one_low], [two_up, two_low], three]
    else:
        (y,) = call(project, (y_shape,), factor.T, unfolding, work=COST["project"], name="project")
        for s in steps(n_row)[:-1]:
            y = y + over_row(y, s)
        y_got = over_row(y, n_row // 2)
        blocks = [[unfolding]] + [[over_row(unfolding, s)] for s in range(1, n_row)]
    counts = tuple(len(b) for b in blocks)
    blocks = [p for b in blocks for p in b]

    kept, given = call(
        functools.partial(term_kernel, scale),
        (jax.ShapeDtypeStruct((hr, rows_here), F32),) * 2,
        unfolding,
        y,
        y_got,
        work=COST["term"],
        name="term",
    )
    image = call(
        sum_kernel,
        jax.ShapeDtypeStruct((hr, rows_here), F32),
        kept,
        over_col(given, 1),
        work=COST["core_sum"],
        name="core_sum",
    )

    def z_sum(image, s, after):
        return call(
            sum_kernel,
            jax.ShapeDtypeStruct((hr, rows_here), F32),
            image,
            over_col(image, 2 * s),
            after=after,
            work=COST["sum"],
            name="z_sum",
        )

    for s in steps(n_z):
        image = z_sum(image, s, [])

    given, kept = call(
        functools.partial(gram_kernel, n_row, n_col, scale, counts),
        (jax.ShapeDtypeStruct((n_z, half, width), F32),) * 2,
        *blocks,
        scratch=[
            pltpu.VMEM((2 * n_row, group, cols_here), BF16),
            pltpu.VMEM((2 * n_row, group, cols_here), BF16),
            pltpu.VMEM((2, 2 * n_row, n_col, half, group), F32),
        ],
        after=[image],
        work=COST["gram"],
        name="gram",
    )
    mine = image[None]
    for s in steps(n_row):
        mine = call(
            stack_kernel,
            jax.ShapeDtypeStruct((2 * s, hr, rows_here), F32),
            mine,
            over_row(mine, s),
            after=[given] if s == 1 else [],
            work=COST["stack"],
            name="stack",
        )
    other = over_col(mine, 1)

    rank_here = rank // n_row
    whole = rows_here % 128 == 0
    nf, core_out = call(
        functools.partial(finish_kernel, n_row, counts),
        (
            jax.ShapeDtypeStruct((rank, mode) if whole else (n_row, rank, rows_here), F32),
            jax.ShapeDtypeStruct((rank_here, cols_here), F32),
        ),
        mine,
        other,
        *blocks,
        scratch=[pltpu.VMEM((n_row, rank_here, rank), F32)],
        work=COST["finish"],
        name="finish",
    )
    new_factor = nf.T if whole else nf.transpose(0, 2, 1).reshape(mode, rank)

    keep, give = call(
        functools.partial(pieces_kernel, n_z),
        (jax.ShapeDtypeStruct((n_z // 2, half, width), F32),) * 2,
        kept,
        over_col(given, 1),
        work=COST["pieces"],
        name="pieces",
    )
    got = over_col(give, 2)
    for s in steps(n_z)[1:]:
        keep, give = keep[0::2] + got[0::2], keep[1::2] + got[1::2]
        got = over_col(give, 2 * s)
    gram_lower = call(
        functools.partial(unpack_kernel, n_row, n_col),
        jax.ShapeDtypeStruct((2 * half, mode), F32),
        keep,
        got,
        work=COST["unpack"],
        name="unpack",
    )
    return gram_lower, new_factor, core_out


def solution(mesh):
    in_specs = (P("row", "col"), P())
    out_specs = (P(("row", "col"), None), P(), P("row", "col"))
    return jax.shard_map(body, mesh=mesh, in_specs=in_specs, out_specs=out_specs, check_vma=False)
```

```python
import functools
import math

import jax
import jax.numpy as jnp
from jax import lax
from jax.experimental import pallas as pl
from jax.experimental.pallas import tpu as pltpu
from jax.sharding import PartitionSpec as P

F32 = jnp.float32
BF16 = jnp.bfloat16
NN = ((1,), (0,))
NT = ((1,), (1,))


COST = dict(project=10**6, join=10**6, term=10**10, core_sum=10**6, sum=10**6, stack=3 * 10**9, finish=10**10, gram=10**6, pieces=10**6, unpack=10**6)


def tree_sum(parts):
    while len(parts) > 1:
        paired = [a + b for a, b in zip(parts[::2], parts[1::2])]
        parts = paired + parts[2 * len(paired) :]
    return parts[0]


def split2(a):
    hi = a.astype(BF16)
    return hi, (a - hi.astype(F32)).astype(BF16)


def split3(a):
    hi = a.astype(BF16)
    rest = a - hi.astype(F32)
    mid = rest.astype(BF16)
    return hi, mid, (rest - mid.astype(F32)).astype(BF16)


def sided(s, n):
    if n != 4 or s in (0, 3):
        return s
    return jnp.where(lax.axis_index("col") % 2 == 1, 3 - s, s)


def mm(a, b, dims):
    return lax.dot_general(a, b, (dims, ((), ())), preferred_element_type=F32)


def mm3(a, b, dims):
    return mm(a[1], b[0], dims) + mm(a[0], b[1], dims) + mm(a[0], b[0], dims)


def mm4(a, b):
    left = jnp.concatenate([a[0], a[0], a[1], a[1]], 1)
    return mm(left, jnp.concatenate([b[0], b[1], b[0], b[1]], 0), NN)


def gram6(a):
    n = a[0].shape[0]
    s = jnp.concatenate(a, 0)
    g = mm(s, s, NT)

    def at(i, j):
        return g[i * n : (i + 1) * n, j * n : (j + 1) * n]

    return at(0, 0) + ((at(0, 1) + at(1, 0)) + (at(1, 1) + (at(0, 2) + at(2, 0))))


COST = dict(project=10**6, join=10**6, term=10**10, core_sum=10**6, sum=10**6, stack=3 * 10**9, finish=10**10, gram=10**6, pieces=10**6, unpack=10**6)


def tree_sum(parts):
    while len(parts) > 1:
        paired = [a + b for a, b in zip(parts[::2], parts[1::2])]
        parts = paired + parts[2 * len(paired) :]
    return parts[0]


def split2(a):
    hi = a.astype(BF16)
    return hi, (a - hi.astype(F32)).astype(BF16)


def split3(a):
    hi = a.astype(BF16)
    rest = a - hi.astype(F32)
    mid = rest.astype(BF16)
    return hi, mid, (rest - mid.astype(F32)).astype(BF16)


def mm(a, b, dims):
    return lax.dot_general(a, b, (dims, ((), ())), preferred_element_type=F32)


def mm3(a, b, dims):
    return mm(a[1], b[0], dims) + mm(a[0], b[1], dims) + mm(a[0], b[0], dims)


def mm6(a, b, dims):
    low = mm(a[1], b[1], dims) + (mm(a[2], b[0], dims) + mm(a[0], b[2], dims))
    return (low + (mm(a[1], b[0], dims) + mm(a[0], b[1], dims))) + mm(a[0], b[0], dims)


def call(kernel, out_shape, *args, after=(), scratch=(), work=1000, name=None):
    n = len(args)

    def run(*refs):
        kernel(*refs[:n], *refs[n + len(after) :])

    return pl.pallas_call(
        run,
        out_shape=out_shape,
        in_specs=[pl.BlockSpec(memory_space=pltpu.VMEM)] * n + [pl.BlockSpec(memory_space=pl.ANY)] * len(after),
        out_specs=jax.tree.map(lambda _: pl.BlockSpec(memory_space=pltpu.VMEM), out_shape),
        scratch_shapes=list(scratch),
        compiler_params=pltpu.CompilerParams(vmem_limit_bytes=48 * 2**20),
        cost_estimate=pl.CostEstimate(flops=work, bytes_accessed=0, transcendentals=0),
        name=name,
    )(*args, *after)


def project_kernel(rows_here, factor_ref, x_ref, y_ref, *copies):
    row = lax.axis_index("row")
    n_row = factor_ref.shape[1] // rows_here
    mine = factor_ref[:, :rows_here]
    for r in range(1, n_row):
        mine = jnp.where(row == r, factor_ref[:, r * rows_here : (r + 1) * rows_here], mine)
    y_ref[...] = mm3(split2(mine), split2(x_ref[...]), NN)
    for i, ref in enumerate(copies):
        ref[...] = x_ref[i * ref.shape[0] : (i + 1) * ref.shape[0], :]


def join_kernel(mine_ref, got_ref, x_ref, y_ref, copy_ref):
    y_ref[...] = mine_ref[...] + got_ref[...]
    copy_ref[...] = x_ref[...]


def term_kernel(scale, x_ref, mine_ref, got_ref, kept_ref, given_ref):
    core = lax.axis_index("col") % 2
    y = mine_ref[...] + got_ref[...]
    term = mm3(split2(y), split2(x_ref[...]), NT) * scale
    hr = term.shape[0] // 2
    kept_ref[...] = jnp.where(core == 0, term[:hr], term[hr:])
    given_ref[...] = jnp.where(core == 0, term[hr:], term[:hr])


def sum_kernel(mine_ref, got_ref, out_ref):
    out_ref[...] = mine_ref[...] + got_ref[...]


def stack_kernel(mine_ref, got_ref, both_ref):
    n = mine_ref.shape[0]
    both_ref[:n] = mine_ref[...]
    both_ref[n:] = got_ref[...]


def inverse_factor(inner):
    n = inner.shape[0]
    wide = -(-2 * n // 128) * 128
    r = lax.broadcasted_iota(jnp.int32, (n, wide), 0)
    c = lax.broadcasted_iota(jnp.int32, (n, wide), 1)
    w = jnp.where(c == r + n, F32(1.0), F32(0.0))
    w = w + jnp.concatenate([inner, jnp.zeros((n, wide - n), F32)], 1)
    w = [w[8 * i : 8 * i + 8] for i in range(n // 8)]
    sub = lax.broadcasted_iota(jnp.int32, (8, wide), 0)
    done = []
    for b in range(n // 8):
        cols = {
            j: [jnp.broadcast_to(w[i][:, 8 * b + j : 8 * b + j + 1], (8, wide)) for i in range(b, n // 8)]
            for j in range(8)
        }
        for k in range(8):
            pivot = jnp.broadcast_to(cols[k][0][k : k + 1], (8, wide))
            rs = lax.rsqrt(pivot)
            inv = rs * rs
            rs = rs * (1.5 - 0.5 * (pivot * inv))
            inv = inv * (2.0 - pivot * inv)
            row = jnp.broadcast_to(w[b][k : k + 1], (8, wide))
            done.append(row[:1] * rs[:1])
            below = [jnp.where(sub > k, cols[k][0], F32(0.0))] + cols[k][1:]
            m = [a * inv for a in below]
            for j in range(k + 1, 8):
                at = jnp.broadcast_to(cols[j][0][k : k + 1], (8, wide))
                if j == k + 1:
                    cols[j] = [a - (f * at) * inv for a, f in zip(cols[j], below)]
                else:
                    cols[j] = [a - f * at for a, f in zip(cols[j], m)]
            for i in range(b, n // 8):
                w[i] = w[i] - m[i - b] * row
    return jnp.concatenate(done, 0)[:, n : 2 * n]


def finish_kernel(n_row, counts, mine_ref, other_ref, *refs):
    total = sum(counts)
    pieces, (nf_ref, core_ref, rows_ref) = refs[:total], refs[total:]
    row = lax.axis_index("row")
    core = lax.axis_index("col") % 2
    _, hr, rows_here = mine_ref.shape
    rank = 2 * hr
    mode = rows_here * n_row
    blocks = []
    for s in range(n_row):
        mine, other = mine_ref[s], other_ref[s]
        first, second = jnp.where(core == 0, mine, other), jnp.where(core == 0, other, mine)
        blocks.append(jnp.concatenate([first, second], 0))
    split = [split3(b) for b in blocks]
    inner = tree_sum([gram6(s) for s in split]) * (1.0 / mode)
    inv = inverse_factor(inner)
    z, at = [], 0
    for s in range(n_row):
        start = 0
        for _ in range(counts[s]):
            x = pieces[at][...]
            hi, lo = split[s][0], split[s][1]
            if n_row == 4 and s in (1, 2):
                hi, lo = (jnp.where(core == 1, b, a) for a, b in zip((hi, lo), split[3 - s][:2]))
            stop = start + x.shape[0]
            z.append(mm3((hi[:, start:stop], lo[:, start:stop]), split2(x), NN))
            start, at = stop, at + 1
    z = tree_sum(z)
    rank_here = rank // n_row
    for i in range(n_row):
        rows_ref[i] = inv[i * rank_here : (i + 1) * rank_here]
    core_ref[...] = mm4(split2(rows_ref[row]), split2(z)) * (1.0 / math.sqrt(mode))
    inv2 = split2(inv)
    for s in range(n_row):
        block = mm4(inv2, split[s])
        if len(nf_ref.shape) == 3:
            nf_ref[row ^ s] = block
        else:
            nf_ref[:, pl.ds(pl.multiple_of((row ^ s) * rows_here, rows_here), rows_here)] = block


def gram_kernel(n_row, n_col, scale, counts, *refs):
    total = sum(counts)
    pieces, (given_ref, kept_ref, hi_ref, lo_ref, part_ref) = refs[:total], refs[total:]
    row = lax.axis_index("row")
    core = lax.axis_index("col") % 2
    n_z = n_col // 2
    rows_here = hi_ref.shape[1] * 2
    group = rows_here // 2
    half = group // n_col
    at = 0
    for s in range(n_row):
        hi, lo = [], []
        for _ in range(counts[s]):
            h, l = split2(pieces[at][...])
            hi.append(h)
            lo.append(l)
            at += 1
        hi, lo = jnp.concatenate(hi, 0), jnp.concatenate(lo, 0)
        owner = row ^ sided(s, n_row)
        for i in range(2):
            hi_ref[2 * owner + i] = hi[i * group : (i + 1) * group]
            lo_ref[2 * owner + i] = lo[i * group : (i + 1) * group]
    high = 2 * n_row - 1 - row
    left = (
        jnp.concatenate([hi_ref[high], hi_ref[row]], 0),
        jnp.concatenate([lo_ref[high], lo_ref[row]], 0),
    )
    for r in range(n_row):
        right = (
            jnp.concatenate([hi_ref[2 * r], hi_ref[2 * r + 1]], 0),
            jnp.concatenate([lo_ref[2 * r], lo_ref[2 * r + 1]], 0),
        )
        g = mm3(left, right, NT) * scale
        for i in range(2):
            for h in range(2):
                for p in range(n_col):
                    start = h * group + p * half
                    part_ref[h, 2 * r + i, p] = g[start : start + half, i * group : (i + 1) * group]
    n_high = 2 * n_row - row
    for b in range(2 * n_row + 1):
        is_low = (b >= n_high).astype(jnp.int32)
        block = b - is_low * n_high
        for zz in range(n_z):
            for ref, k in ((given_ref, 1 - core), (kept_ref, core)):
                owner = 2 * zz + k
                piece = jnp.where(is_low == 1, owner, n_col - 1 - owner)
                ref[zz, :, b * group : (b + 1) * group] = part_ref[is_low, block, piece]


def pieces_kernel(n_z, kept_ref, got_ref, keep_ref, give_ref):
    z = lax.axis_index("col") // 2
    for t in range(n_z):
        ref = give_ref if t % 2 else keep_ref
        at = z ^ sided(t, n_z)
        ref[t // 2] = kept_ref[at] + got_ref[at]


def unpack_kernel(n_row, n_col, *refs):
    out_ref = refs[-1]
    row = lax.axis_index("row")
    owner = row * n_col + lax.axis_index("col")
    total = tree_sum([r[0] for r in refs[:-1]])
    half, width = total.shape
    mode = out_ref.shape[1]
    group = width - mode
    r = lax.broadcasted_iota(jnp.int32, (half, mode), 0)
    c = lax.broadcasted_iota(jnp.int32, (half, mode), 1)
    out_ref[half:, :] = jnp.where(c <= mode - (owner + 1) * half + r, total[:, :mode], F32(0.0))
    out_ref[:half, :] = jnp.zeros((half, mode), F32)
    for k in range(n_row):

        @pl.when(row == k)
        def _():
            start, stop = mode - k * group, mode + group
            keep = c[:, : stop - start] <= owner * half + r[:, : stop - start]
            out_ref[:half, : stop - start] = jnp.where(keep, total[:, start:stop], F32(0.0))


def body(unfolding, factor):
    n_row = lax.axis_size("row")
    n_col = lax.axis_size("col")
    n_z = n_col // 2
    rows_here, cols_here = unfolding.shape
    mode = rows_here * n_row
    rank = factor.shape[1]
    hr = rank // 2
    scale = 1.0 / (cols_here * n_col)
    group = rows_here // 2
    half = group // n_col
    width = mode + group

    def over_row(x, s):
        return lax.ppermute(x, "row", [(i, i ^ s) for i in range(n_row)])

    def over_side(x, s):
        pairs = [((r, c), (r ^ (3 - s if c % 2 else s), c)) for r in range(n_row) for c in range(n_col)]
        return lax.ppermute(x, ("row", "col"), [(a * n_col + b, p * n_col + q) for (a, b), (p, q) in pairs])

    def over_col(x, s):
        return lax.ppermute(x, "col", [(i, i ^ s) for i in range(n_col)])

    def over_z(x, s):
        far = [2 * (3 - s if n_z == 4 and c % 2 else s) for c in range(n_col)]
        return lax.ppermute(x, "col", [(c, c ^ far[c]) for c in range(n_col)])

    def steps(n):
        return [1 << k for k in range(n.bit_length() - 1)]

    y_shape = jax.ShapeDtypeStruct((rank, cols_here), F32)
    part_shape = jax.ShapeDtypeStruct((group, cols_here), F32)
    project = functools.partial(project_kernel, rows_here)
    if n_row == 4:
        two_low = over_side(unfolding[group:], 2)
        y, upper, lower = call(
            project,
            (y_shape, part_shape, part_shape),
            factor.T,
            unfolding,
            work=COST["project"],
            name="project",
        )
        got = over_side(y, 1)
        one_up = over_side(upper, 1)
        one_low = over_side(lower, 1)
        y, upper = call(
            join_kernel, (y_shape, part_shape), y, got, upper, work=COST["join"], name="join"
        )
        y_got = over_side(y, 2)
        two_up = over_side(upper, 2)
        three = [over_side(one_up, 2), over_side(two_low, 1)]
        blocks = [[unfolding], [one_up, one_low], [two_up, two_low], three]
    else:
        (y,) = call(project, (y_shape,), factor.T, unfolding, work=COST["project"], name="project")
        for s in steps(n_row)[:-1]:
            y = y + over_row(y, s)
        y_got = over_row(y, n_row // 2)
        blocks = [[unfolding]] + [[over_row(unfolding, s)] for s in range(1, n_row)]
    counts = tuple(len(b) for b in blocks)
    blocks = [p for b in blocks for p in b]

    kept, given = call(
        functools.partial(term_kernel, scale),
        (jax.ShapeDtypeStruct((hr, rows_here), F32),) * 2,
        unfolding,
        y,
        y_got,
        work=COST["term"],
        name="term",
    )
    image = call(
        sum_kernel,
        jax.ShapeDtypeStruct((hr, rows_here), F32),
        kept,
        over_col(given, 1),
        work=COST["core_sum"],
        name="core_sum",
    )

    def z_sum(image, s, after):
        return call(
            sum_kernel,
            jax.ShapeDtypeStruct((hr, rows_here), F32),
            image,
            over_z(image, s),
            after=after,
            work=COST["sum"],
            name="z_sum",
        )

    for s in steps(n_z):
        image = z_sum(image, s, [])

    given, kept = call(
        functools.partial(gram_kernel, n_row, n_col, scale, counts),
        (jax.ShapeDtypeStruct((n_z, half, width), F32),) * 2,
        *blocks,
        scratch=[
            pltpu.VMEM((2 * n_row, group, cols_here), BF16),
            pltpu.VMEM((2 * n_row, group, cols_here), BF16),
            pltpu.VMEM((2, 2 * n_row, n_col, half, group), F32),
        ],
        after=[image],
        work=COST["gram"],
        name="gram",
    )
    mine = image[None]
    for s in steps(n_row):
        mine = call(
            stack_kernel,
            jax.ShapeDtypeStruct((2 * s, hr, rows_here), F32),
            mine,
            over_row(mine, s),
            after=[given] if s == 1 else [],
            work=COST["stack"],
            name="stack",
        )
    other = over_col(mine, 1)

    rank_here = rank // n_row
    whole = rows_here % 128 == 0
    nf, core_out = call(
        functools.partial(finish_kernel, n_row, counts),
        (
            jax.ShapeDtypeStruct((rank, mode) if whole else (n_row, rank, rows_here), F32),
            jax.ShapeDtypeStruct((rank_here, cols_here), F32),
        ),
        mine,
        other,
        *blocks,
        scratch=[pltpu.VMEM((n_row, rank_here, rank), F32)],
        work=COST["finish"],
        name="finish",
    )
    new_factor = nf.T if whole else nf.transpose(0, 2, 1).reshape(mode, rank)

    keep, give = call(
        functools.partial(pieces_kernel, n_z),
        (jax.ShapeDtypeStruct((n_z // 2, half, width), F32),) * 2,
        kept,
        over_col(given, 1),
        work=COST["pieces"],
        name="pieces",
    )
    got = over_z(give, 1)
    for s in steps(n_z)[1:]:
        keep, give = keep[0::2] + got[0::2], keep[1::2] + got[1::2]
        got = over_z(give, s)
    gram_lower = call(
        functools.partial(unpack_kernel, n_row, n_col),
        jax.ShapeDtypeStruct((2 * half, mode), F32),
        keep,
        got,
        work=COST["unpack"],
        name="unpack",
    )
    return gram_lower, new_factor, core_out


def solution(mesh):
    in_specs = (P("row", "col"), P())
    out_specs = (P(("row", "col"), None), P(), P("row", "col"))
    return jax.shard_map(body, mesh=mesh, in_specs=in_specs, out_specs=out_specs, check_vma=False)
```

```python
import functools
import math

import jax
import jax.numpy as jnp
from jax import lax
from jax.experimental import pallas as pl
from jax.experimental.pallas import tpu as pltpu
from jax.sharding import PartitionSpec as P

F32 = jnp.float32
BF16 = jnp.bfloat16
NN = ((1,), (0,))
NT = ((1,), (1,))


COST = dict(project=10**6, join=10**6, term=10**10, core_sum=10**6, sum=10**6, stack=3 * 10**9, finish=10**10, gram=10**6, pieces=10**6, unpack=10**6)


def tree_sum(parts):
    while len(parts) > 1:
        paired = [a + b for a, b in zip(parts[::2], parts[1::2])]
        parts = paired + parts[2 * len(paired) :]
    return parts[0]


def split2(a):
    hi = a.astype(BF16)
    return hi, (a - hi.astype(F32)).astype(BF16)


def split3(a):
    hi = a.astype(BF16)
    rest = a - hi.astype(F32)
    mid = rest.astype(BF16)
    return hi, mid, (rest - mid.astype(F32)).astype(BF16)


def sided(s, n):
    if n != 4 or s in (0, 3):
        return s
    return jnp.where(lax.axis_index("col") % 2 == 1, 3 - s, s)


def mm(a, b, dims):
    return lax.dot_general(a, b, (dims, ((), ())), preferred_element_type=F32)


def mm3(a, b, dims):
    return mm(a[1], b[0], dims) + mm(a[0], b[1], dims) + mm(a[0], b[0], dims)


def mm4(a, b):
    left = jnp.concatenate([a[0], a[0], a[1], a[1]], 1)
    return mm(left, jnp.concatenate([b[0], b[1], b[0], b[1]], 0), NN)


def gram6(a):
    n = a[0].shape[0]
    s = jnp.concatenate(a, 0)
    g = mm(s, s, NT)

    def at(i, j):
        return g[i * n : (i + 1) * n, j * n : (j + 1) * n]

    return at(0, 0) + ((at(0, 1) + at(1, 0)) + (at(1, 1) + (at(0, 2) + at(2, 0))))


COST = dict(project=10**6, join=10**6, term=10**10, core_sum=10**6, sum=10**6, stack=3 * 10**9, finish=10**10, gram=10**6, pieces=10**6, unpack=10**6)


def tree_sum(parts):
    while len(parts) > 1:
        paired = [a + b for a, b in zip(parts[::2], parts[1::2])]
        parts = paired + parts[2 * len(paired) :]
    return parts[0]


def split2(a):
    hi = a.astype(BF16)
    return hi, (a - hi.astype(F32)).astype(BF16)


def split3(a):
    hi = a.astype(BF16)
    rest = a - hi.astype(F32)
    mid = rest.astype(BF16)
    return hi, mid, (rest - mid.astype(F32)).astype(BF16)


def mm(a, b, dims):
    return lax.dot_general(a, b, (dims, ((), ())), preferred_element_type=F32)


def mm3(a, b, dims):
    return mm(a[1], b[0], dims) + mm(a[0], b[1], dims) + mm(a[0], b[0], dims)


def mm6(a, b, dims):
    low = mm(a[1], b[1], dims) + (mm(a[2], b[0], dims) + mm(a[0], b[2], dims))
    return (low + (mm(a[1], b[0], dims) + mm(a[0], b[1], dims))) + mm(a[0], b[0], dims)


def call(kernel, out_shape, *args, after=(), scratch=(), work=1000, name=None):
    n = len(args)

    def run(*refs):
        kernel(*refs[:n], *refs[n + len(after) :])

    return pl.pallas_call(
        run,
        out_shape=out_shape,
        in_specs=[pl.BlockSpec(memory_space=pltpu.VMEM)] * n + [pl.BlockSpec(memory_space=pl.ANY)] * len(after),
        out_specs=jax.tree.map(lambda _: pl.BlockSpec(memory_space=pltpu.VMEM), out_shape),
        scratch_shapes=list(scratch),
        compiler_params=pltpu.CompilerParams(vmem_limit_bytes=48 * 2**20),
        cost_estimate=pl.CostEstimate(flops=work, bytes_accessed=0, transcendentals=0),
        name=name,
    )(*args, *after)


def project_kernel(rows_here, factor_ref, x_ref, y_ref, *copies):
    row = lax.axis_index("row")
    n_row = factor_ref.shape[1] // rows_here
    mine = factor_ref[:, :rows_here]
    for r in range(1, n_row):
        mine = jnp.where(row == r, factor_ref[:, r * rows_here : (r + 1) * rows_here], mine)
    y_ref[...] = mm3(split2(mine), split2(x_ref[...]), NN)
    for i, ref in enumerate(copies):
        ref[...] = x_ref[i * ref.shape[0] : (i + 1) * ref.shape[0], :]


def join_kernel(mine_ref, got_ref, x_ref, y_ref, copy_ref):
    y_ref[...] = mine_ref[...] + got_ref[...]
    copy_ref[...] = x_ref[...]


def term_kernel(scale, x_ref, mine_ref, got_ref, kept_ref, given_ref):
    core = lax.axis_index("col") % 2
    y = mine_ref[...] + got_ref[...]
    term = mm3(split2(y), split2(x_ref[...]), NT) * scale
    hr = term.shape[0] // 2
    kept_ref[...] = jnp.where(core == 0, term[:hr], term[hr:])
    given_ref[...] = jnp.where(core == 0, term[hr:], term[:hr])


def sum_kernel(mine_ref, got_ref, out_ref):
    out_ref[...] = mine_ref[...] + got_ref[...]


def stack_kernel(mine_ref, got_ref, both_ref):
    n = mine_ref.shape[0]
    both_ref[:n] = mine_ref[...]
    both_ref[n:] = got_ref[...]


def inverse_factor(inner):
    n = inner.shape[0]
    wide = -(-2 * n // 128) * 128
    r = lax.broadcasted_iota(jnp.int32, (n, wide), 0)
    c = lax.broadcasted_iota(jnp.int32, (n, wide), 1)
    w = jnp.where(c == r + n, F32(1.0), F32(0.0))
    w = w + jnp.concatenate([inner, jnp.zeros((n, wide - n), F32)], 1)
    w = [w[8 * i : 8 * i + 8] for i in range(n // 8)]
    sub = lax.broadcasted_iota(jnp.int32, (8, wide), 0)
    done = []
    for b in range(n // 8):
        cols = {
            j: [jnp.broadcast_to(w[i][:, 8 * b + j : 8 * b + j + 1], (8, wide)) for i in range(b, n // 8)]
            for j in range(8)
        }
        for k in range(8):
            pivot = jnp.broadcast_to(cols[k][0][k : k + 1], (8, wide))
            rs = lax.rsqrt(pivot)
            inv = rs * rs
            rs = rs * (1.5 - 0.5 * (pivot * inv))
            inv = inv * (2.0 - pivot * inv)
            row = jnp.broadcast_to(w[b][k : k + 1], (8, wide))
            done.append(row[:1] * rs[:1])
            below = [jnp.where(sub > k, cols[k][0], F32(0.0))] + cols[k][1:]
            m = [a * inv for a in below]
            for j in range(k + 1, 8):
                at = jnp.broadcast_to(cols[j][0][k : k + 1], (8, wide))
                if j == k + 1:
                    cols[j] = [a - (f * at) * inv for a, f in zip(cols[j], below)]
                else:
                    cols[j] = [a - f * at for a, f in zip(cols[j], m)]
            for i in range(b, n // 8):
                w[i] = w[i] - m[i - b] * row
    return jnp.concatenate(done, 0)[:, n : 2 * n]


def finish_kernel(n_row, counts, mine_ref, other_ref, *refs):
    total = sum(counts)
    pieces, (nf_ref, core_ref, rows_ref) = refs[:total], refs[total:]
    row = lax.axis_index("row")
    core = lax.axis_index("col") % 2
    _, hr, rows_here = mine_ref.shape
    rank = 2 * hr
    mode = rows_here * n_row
    blocks = []
    for s in range(n_row):
        mine, other = mine_ref[s], other_ref[s]
        first, second = jnp.where(core == 0, mine, other), jnp.where(core == 0, other, mine)
        blocks.append(jnp.concatenate([first, second], 0))
    split = [split3(b) for b in blocks]
    inner = tree_sum([gram6(s) for s in split]) * (1.0 / mode)
    inv = inverse_factor(inner)
    z, at = [], 0
    for s in range(n_row):
        start = 0
        for _ in range(counts[s]):
            x = pieces[at][...]
            hi, lo = split[s][0], split[s][1]
            if n_row == 4 and s in (1, 2):
                hi, lo = (jnp.where(core == 1, b, a) for a, b in zip((hi, lo), split[3 - s][:2]))
            stop = start + x.shape[0]
            z.append(mm3((hi[:, start:stop], lo[:, start:stop]), split2(x), NN))
            start, at = stop, at + 1
    z = tree_sum(z)
    rank_here = rank // n_row
    for i in range(n_row):
        rows_ref[i] = inv[i * rank_here : (i + 1) * rank_here]
    core_ref[...] = mm4(split2(rows_ref[row]), split2(z)) * (1.0 / math.sqrt(mode))
    inv2 = split2(inv)
    for s in range(n_row):
        block = mm4(inv2, split[s])
        if len(nf_ref.shape) == 3:
            nf_ref[row ^ s] = block
        else:
            nf_ref[:, pl.ds(pl.multiple_of((row ^ s) * rows_here, rows_here), rows_here)] = block


def gram_kernel(n_row, n_col, scale, counts, *refs):
    total = sum(counts)
    pieces, (given_ref, kept_ref, hi_ref, lo_ref, part_ref) = refs[:total], refs[total:]
    row = lax.axis_index("row")
    core = lax.axis_index("col") % 2
    n_z = n_col // 2
    rows_here = hi_ref.shape[1] * 2
    group = rows_here // 2
    half = group // n_col
    at = 0
    for s in range(n_row):
        hi, lo = [], []
        for _ in range(counts[s]):
            h, l = split2(pieces[at][...])
            hi.append(h)
            lo.append(l)
            at += 1
        hi, lo = jnp.concatenate(hi, 0), jnp.concatenate(lo, 0)
        owner = row ^ sided(s, n_row)
        for i in range(2):
            hi_ref[2 * owner + i] = hi[i * group : (i + 1) * group]
            lo_ref[2 * owner + i] = lo[i * group : (i + 1) * group]
    high = 2 * n_row - 1 - row
    left = (
        jnp.concatenate([hi_ref[high], hi_ref[row]], 0),
        jnp.concatenate([lo_ref[high], lo_ref[row]], 0),
    )
    for r in range(n_row):
        right = (
            jnp.concatenate([hi_ref[2 * r], hi_ref[2 * r + 1]], 0),
            jnp.concatenate([lo_ref[2 * r], lo_ref[2 * r + 1]], 0),
        )
        g = mm3(left, right, NT) * scale
        for i in range(2):
            for h in range(2):
                for p in range(n_col):
                    start = h * group + p * half
                    part_ref[h, 2 * r + i, p] = g[start : start + half, i * group : (i + 1) * group]
    n_high = 2 * n_row - row
    for b in range(2 * n_row + 1):
        is_low = (b >= n_high).astype(jnp.int32)
        block = b - is_low * n_high
        for zz in range(n_z):
            for ref, k in ((given_ref, 1 - core), (kept_ref, core)):
                owner = 2 * zz + k
                piece = jnp.where(is_low == 1, owner, n_col - 1 - owner)
                ref[zz, :, b * group : (b + 1) * group] = part_ref[is_low, block, piece]


def pieces_kernel(n_z, kept_ref, got_ref, keep_ref, give_ref):
    z = lax.axis_index("col") // 2
    for t in range(n_z):
        ref = give_ref if t % 2 else keep_ref
        at = z ^ sided(t, n_z)
        ref[t // 2] = kept_ref[at] + got_ref[at]


def unpack_kernel(n_row, n_col, *refs):
    out_ref = refs[-1]
    row = lax.axis_index("row")
    owner = row * n_col + lax.axis_index("col")
    total = tree_sum([r[0] for r in refs[:-1]])
    half, width = total.shape
    mode = out_ref.shape[1]
    group = width - mode
    r = lax.broadcasted_iota(jnp.int32, (half, mode), 0)
    c = lax.broadcasted_iota(jnp.int32, (half, mode), 1)
    out_ref[half:, :] = jnp.where(c <= mode - (owner + 1) * half + r, total[:, :mode], F32(0.0))
    out_ref[:half, :] = jnp.zeros((half, mode), F32)
    for k in range(n_row):

        @pl.when(row == k)
        def _():
            start, stop = mode - k * group, mode + group
            keep = c[:, : stop - start] <= owner * half + r[:, : stop - start]
            out_ref[:half, : stop - start] = jnp.where(keep, total[:, start:stop], F32(0.0))


def body(unfolding, factor):
    n_row = lax.axis_size("row")
    n_col = lax.axis_size("col")
    n_z = n_col // 2
    rows_here, cols_here = unfolding.shape
    mode = rows_here * n_row
    rank = factor.shape[1]
    hr = rank // 2
    scale = 1.0 / (cols_here * n_col)
    group = rows_here // 2
    half = group // n_col
    width = mode + group

    def over_row(x, s):
        return lax.ppermute(x, "row", [(i, i ^ s) for i in range(n_row)])

    def over_side(x, s):
        pairs = [((r, c), (r ^ (3 - s if c % 2 else s), c)) for r in range(n_row) for c in range(n_col)]
        return lax.ppermute(x, ("row", "col"), [(a * n_col + b, p * n_col + q) for (a, b), (p, q) in pairs])

    def over_col(x, s):
        return lax.ppermute(x, "col", [(i, i ^ s) for i in range(n_col)])

    def over_z(x, s):
        far = [2 * (3 - s if n_z == 4 and c % 2 else s) for c in range(n_col)]
        return lax.ppermute(x, "col", [(c, c ^ far[c]) for c in range(n_col)])

    def steps(n):
        return [1 << k for k in range(n.bit_length() - 1)]

    y_shape = jax.ShapeDtypeStruct((rank, cols_here), F32)
    part_shape = jax.ShapeDtypeStruct((group, cols_here), F32)
    project = functools.partial(project_kernel, rows_here)
    if n_row == 4:
        two_low = over_side(unfolding[group:], 2)
        y, upper, lower = call(
            project,
            (y_shape, part_shape, part_shape),
            factor.T,
            unfolding,
            work=COST["project"],
            name="project",
        )
        got = over_side(y, 1)
        one_up = over_side(upper, 1)
        one_low = over_side(lower, 1)
        y, upper = call(
            join_kernel, (y_shape, part_shape), y, got, upper, work=COST["join"], name="join"
        )
        y_got = over_side(y, 2)
        two_up = over_side(upper, 2)
        three = [over_side(one_up, 2), over_side(two_low, 1)]
        blocks = [[unfolding], [one_up, one_low], [two_up, two_low], three]
    else:
        (y,) = call(project, (y_shape,), factor.T, unfolding, work=COST["project"], name="project")
        for s in steps(n_row)[:-1]:
            y = y + over_row(y, s)
        y_got = over_row(y, n_row // 2)
        blocks = [[unfolding]] + [[over_row(unfolding, s)] for s in range(1, n_row)]
    counts = tuple(len(b) for b in blocks)
    blocks = [p for b in blocks for p in b]

    kept, given = call(
        functools.partial(term_kernel, scale),
        (jax.ShapeDtypeStruct((hr, rows_here), F32),) * 2,
        unfolding,
        y,
        y_got,
        work=COST["term"],
        name="term",
    )
    image = call(
        sum_kernel,
        jax.ShapeDtypeStruct((hr, rows_here), F32),
        kept,
        over_col(given, 1),
        work=COST["core_sum"],
        name="core_sum",
    )

    def z_sum(image, s, after, work):
        return call(
            sum_kernel,
            jax.ShapeDtypeStruct((hr, rows_here), F32),
            image,
            over_z(image, s),
            after=after,
            work=work,
            name="z_sum",
        )

    for s in steps(n_z)[:-1]:
        image = z_sum(image, s, [], COST["sum"])

    given, kept = call(
        functools.partial(gram_kernel, n_row, n_col, scale, counts),
        (jax.ShapeDtypeStruct((n_z, half, width), F32),) * 2,
        *blocks,
        scratch=[
            pltpu.VMEM((2 * n_row, group, cols_here), BF16),
            pltpu.VMEM((2 * n_row, group, cols_here), BF16),
            pltpu.VMEM((2, 2 * n_row, n_col, half, group), F32),
        ],
        after=[image],
        work=COST["gram"],
        name="gram",
    )
    image = z_sum(image, n_z // 2, [given], COST["stack"])
    mine = image[None]
    for s in steps(n_row):
        mine = call(
            stack_kernel,
            jax.ShapeDtypeStruct((2 * s, hr, rows_here), F32),
            mine,
            over_row(mine, s),
            work=COST["stack"],
            name="stack",
        )
    other = over_col(mine, 1)

    rank_here = rank // n_row
    whole = rows_here % 128 == 0
    nf, core_out = call(
        functools.partial(finish_kernel, n_row, counts),
        (
            jax.ShapeDtypeStruct((rank, mode) if whole else (n_row, rank, rows_here), F32),
            jax.ShapeDtypeStruct((rank_here, cols_here), F32),
        ),
        mine,
        other,
        *blocks,
        scratch=[pltpu.VMEM((n_row, rank_here, rank), F32)],
        work=COST["finish"],
        name="finish",
    )
    new_factor = nf.T if whole else nf.transpose(0, 2, 1).reshape(mode, rank)

    keep, give = call(
        functools.partial(pieces_kernel, n_z),
        (jax.ShapeDtypeStruct((n_z // 2, half, width), F32),) * 2,
        kept,
        over_col(given, 1),
        work=COST["pieces"],
        name="pieces",
    )
    got = over_z(give, 1)
    for s in steps(n_z)[1:]:
        keep, give = keep[0::2] + got[0::2], keep[1::2] + got[1::2]
        got = over_z(give, s)
    gram_lower = call(
        functools.partial(unpack_kernel, n_row, n_col),
        jax.ShapeDtypeStruct((2 * half, mode), F32),
        keep,
        got,
        work=COST["unpack"],
        name="unpack",
    )
    return gram_lower, new_factor, core_out


def solution(mesh):
    in_specs = (P("row", "col"), P())
    out_specs = (P(("row", "col"), None), P(), P("row", "col"))
    return jax.shard_map(body, mesh=mesh, in_specs=in_specs, out_specs=out_specs, check_vma=False)
```

```python
import functools
import math

import jax
import jax.numpy as jnp
from jax import lax
from jax.experimental import pallas as pl
from jax.experimental.pallas import tpu as pltpu
from jax.sharding import PartitionSpec as P

F32 = jnp.float32
BF16 = jnp.bfloat16
NN = ((1,), (0,))
NT = ((1,), (1,))


COST = dict(project=10**6, join=10**6, term=10**10, core_sum=10**6, sum=10**6, stack=3 * 10**9, finish=10**10, gram=10**6, pieces=10**6, unpack=10**6)


def tree_sum(parts):
    while len(parts) > 1:
        paired = [a + b for a, b in zip(parts[::2], parts[1::2])]
        parts = paired + parts[2 * len(paired) :]
    return parts[0]


def split2(a):
    hi = a.astype(BF16)
    return hi, (a - hi.astype(F32)).astype(BF16)


def split3(a):
    hi = a.astype(BF16)
    rest = a - hi.astype(F32)
    mid = rest.astype(BF16)
    return hi, mid, (rest - mid.astype(F32)).astype(BF16)


def sided(s, n_row):
    if n_row != 4 or s in (0, 3):
        return s
    return jnp.where(lax.axis_index("col") % 2 == 1, 3 - s, s)


def mm(a, b, dims):
    return lax.dot_general(a, b, (dims, ((), ())), preferred_element_type=F32)


def mm3(a, b, dims):
    return mm(a[1], b[0], dims) + mm(a[0], b[1], dims) + mm(a[0], b[0], dims)


def mm4(a, b):
    left = jnp.concatenate([a[0], a[0], a[1], a[1]], 1)
    return mm(left, jnp.concatenate([b[0], b[1], b[0], b[1]], 0), NN)


def gram6(a):
    n = a[0].shape[0]
    s = jnp.concatenate(a, 0)
    g = mm(s, s, NT)

    def at(i, j):
        return g[i * n : (i + 1) * n, j * n : (j + 1) * n]

    return at(0, 0) + ((at(0, 1) + at(1, 0)) + (at(1, 1) + (at(0, 2) + at(2, 0))))


COST = dict(project=10**6, join=10**6, term=10**10, core_sum=10**6, sum=10**6, stack=3 * 10**9, finish=10**10, gram=10**6, pieces=10**6, unpack=10**6)


def tree_sum(parts):
    while len(parts) > 1:
        paired = [a + b for a, b in zip(parts[::2], parts[1::2])]
        parts = paired + parts[2 * len(paired) :]
    return parts[0]


def split2(a):
    hi = a.astype(BF16)
    return hi, (a - hi.astype(F32)).astype(BF16)


def split3(a):
    hi = a.astype(BF16)
    rest = a - hi.astype(F32)
    mid = rest.astype(BF16)
    return hi, mid, (rest - mid.astype(F32)).astype(BF16)


def mm(a, b, dims):
    return lax.dot_general(a, b, (dims, ((), ())), preferred_element_type=F32)


def mm3(a, b, dims):
    return mm(a[1], b[0], dims) + mm(a[0], b[1], dims) + mm(a[0], b[0], dims)


def mm6(a, b, dims):
    low = mm(a[1], b[1], dims) + (mm(a[2], b[0], dims) + mm(a[0], b[2], dims))
    return (low + (mm(a[1], b[0], dims) + mm(a[0], b[1], dims))) + mm(a[0], b[0], dims)


def call(kernel, out_shape, *args, after=(), scratch=(), work=1000, name=None):
    n = len(args)

    def run(*refs):
        kernel(*refs[:n], *refs[n + len(after) :])

    return pl.pallas_call(
        run,
        out_shape=out_shape,
        in_specs=[pl.BlockSpec(memory_space=pltpu.VMEM)] * n + [pl.BlockSpec(memory_space=pl.ANY)] * len(after),
        out_specs=jax.tree.map(lambda _: pl.BlockSpec(memory_space=pltpu.VMEM), out_shape),
        scratch_shapes=list(scratch),
        compiler_params=pltpu.CompilerParams(vmem_limit_bytes=48 * 2**20),
        cost_estimate=pl.CostEstimate(flops=work, bytes_accessed=0, transcendentals=0),
        name=name,
    )(*args, *after)


def project_kernel(rows_here, factor_ref, x_ref, y_ref, *copies):
    row = lax.axis_index("row")
    n_row = factor_ref.shape[1] // rows_here
    mine = factor_ref[:, :rows_here]
    for r in range(1, n_row):
        mine = jnp.where(row == r, factor_ref[:, r * rows_here : (r + 1) * rows_here], mine)
    y_ref[...] = mm3(split2(mine), split2(x_ref[...]), NN)
    for i, ref in enumerate(copies):
        ref[...] = x_ref[i * ref.shape[0] : (i + 1) * ref.shape[0], :]


def join_kernel(mine_ref, got_ref, x_ref, y_ref, copy_ref):
    y_ref[...] = mine_ref[...] + got_ref[...]
    copy_ref[...] = x_ref[...]


def term_kernel(scale, x_ref, mine_ref, got_ref, kept_ref, given_ref):
    core = lax.axis_index("col") % 2
    y = mine_ref[...] + got_ref[...]
    term = mm3(split2(y), split2(x_ref[...]), NT) * scale
    hr = term.shape[0] // 2
    kept_ref[...] = jnp.where(core == 0, term[:hr], term[hr:])
    given_ref[...] = jnp.where(core == 0, term[hr:], term[:hr])


def sum_kernel(mine_ref, got_ref, out_ref):
    out_ref[...] = mine_ref[...] + got_ref[...]


def stack_kernel(mine_ref, got_ref, both_ref):
    n = mine_ref.shape[0]
    both_ref[:n] = mine_ref[...]
    both_ref[n:] = got_ref[...]


def inverse_factor(inner):
    n = inner.shape[0]
    wide = -(-2 * n // 128) * 128
    r = lax.broadcasted_iota(jnp.int32, (n, wide), 0)
    c = lax.broadcasted_iota(jnp.int32, (n, wide), 1)
    w = jnp.where(c == r + n, F32(1.0), F32(0.0))
    w = w + jnp.concatenate([inner, jnp.zeros((n, wide - n), F32)], 1)
    w = [w[8 * i : 8 * i + 8] for i in range(n // 8)]
    sub = lax.broadcasted_iota(jnp.int32, (8, wide), 0)
    done = []
    for b in range(n // 8):
        cols = {
            j: [jnp.broadcast_to(w[i][:, 8 * b + j : 8 * b + j + 1], (8, wide)) for i in range(b, n // 8)]
            for j in range(8)
        }
        for k in range(8):
            pivot = jnp.broadcast_to(cols[k][0][k : k + 1], (8, wide))
            rs = lax.rsqrt(pivot)
            inv = rs * rs
            rs = rs * (1.5 - 0.5 * (pivot * inv))
            inv = inv * (2.0 - pivot * inv)
            row = jnp.broadcast_to(w[b][k : k + 1], (8, wide))
            done.append(row[:1] * rs[:1])
            below = [jnp.where(sub > k, cols[k][0], F32(0.0))] + cols[k][1:]
            m = [a * inv for a in below]
            for j in range(k + 1, 8):
                at = jnp.broadcast_to(cols[j][0][k : k + 1], (8, wide))
                if j == k + 1:
                    cols[j] = [a - (f * at) * inv for a, f in zip(cols[j], below)]
                else:
                    cols[j] = [a - f * at for a, f in zip(cols[j], m)]
            for i in range(b, n // 8):
                w[i] = w[i] - m[i - b] * row
    return jnp.concatenate(done, 0)[:, n : 2 * n]


def finish_kernel(n_row, counts, mine_ref, other_ref, *refs):
    total = sum(counts)
    pieces, (nf_ref, core_ref, rows_ref) = refs[:total], refs[total:]
    row = lax.axis_index("row")
    core = lax.axis_index("col") % 2
    _, hr, rows_here = mine_ref.shape
    rank = 2 * hr
    mode = rows_here * n_row
    blocks = []
    for s in range(n_row):
        mine, other = mine_ref[s], other_ref[s]
        first, second = jnp.where(core == 0, mine, other), jnp.where(core == 0, other, mine)
        blocks.append(jnp.concatenate([first, second], 0))
    split = [split3(b) for b in blocks]
    inner = tree_sum([gram6(s) for s in split]) * (1.0 / mode)
    inv = inverse_factor(inner)
    z, at = [], 0
    for s in range(n_row):
        start = 0
        for _ in range(counts[s]):
            x = pieces[at][...]
            hi, lo = split[s][0], split[s][1]
            if n_row == 4 and s in (1, 2):
                hi, lo = (jnp.where(core == 1, b, a) for a, b in zip((hi, lo), split[3 - s][:2]))
            stop = start + x.shape[0]
            z.append(mm3((hi[:, start:stop], lo[:, start:stop]), split2(x), NN))
            start, at = stop, at + 1
    z = tree_sum(z)
    rank_here = rank // n_row
    for i in range(n_row):
        rows_ref[i] = inv[i * rank_here : (i + 1) * rank_here]
    core_ref[...] = mm4(split2(rows_ref[row]), split2(z)) * (1.0 / math.sqrt(mode))
    inv2 = split2(inv)
    for s in range(n_row):
        block = mm4(inv2, split[s])
        if len(nf_ref.shape) == 3:
            nf_ref[row ^ s] = block
        else:
            nf_ref[:, pl.ds(pl.multiple_of((row ^ s) * rows_here, rows_here), rows_here)] = block


def gram_kernel(n_row, n_col, scale, counts, *refs):
    total = sum(counts)
    pieces, (given_ref, kept_ref, hi_ref, lo_ref, part_ref) = refs[:total], refs[total:]
    row = lax.axis_index("row")
    core = lax.axis_index("col") % 2
    n_z = n_col // 2
    rows_here = hi_ref.shape[1] * 2
    group = rows_here // 2
    half = group // n_col
    at = 0
    for s in range(n_row):
        hi, lo = [], []
        for _ in range(counts[s]):
            h, l = split2(pieces[at][...])
            hi.append(h)
            lo.append(l)
            at += 1
        hi, lo = jnp.concatenate(hi, 0), jnp.concatenate(lo, 0)
        owner = row ^ sided(s, n_row)
        for i in range(2):
            hi_ref[2 * owner + i] = hi[i * group : (i + 1) * group]
            lo_ref[2 * owner + i] = lo[i * group : (i + 1) * group]
    high = 2 * n_row - 1 - row
    left = (
        jnp.concatenate([hi_ref[high], hi_ref[row]], 0),
        jnp.concatenate([lo_ref[high], lo_ref[row]], 0),
    )
    for r in range(n_row):
        right = (
            jnp.concatenate([hi_ref[2 * r], hi_ref[2 * r + 1]], 0),
            jnp.concatenate([lo_ref[2 * r], lo_ref[2 * r + 1]], 0),
        )
        g = mm3(left, right, NT) * scale
        for i in range(2):
            for h in range(2):
                for p in range(n_col):
                    start = h * group + p * half
                    part_ref[h, 2 * r + i, p] = g[start : start + half, i * group : (i + 1) * group]
    n_high = 2 * n_row - row
    for b in range(2 * n_row + 1):
        is_low = (b >= n_high).astype(jnp.int32)
        block = b - is_low * n_high
        for zz in range(n_z):
            for ref, k in ((given_ref, 1 - core), (kept_ref, core)):
                owner = 2 * zz + k
                piece = jnp.where(is_low == 1, owner, n_col - 1 - owner)
                ref[zz, :, b * group : (b + 1) * group] = part_ref[is_low, block, piece]


def pieces_kernel(n_z, kept_ref, got_ref, keep_ref, give_ref):
    z = lax.axis_index("col") // 2
    for t in range(n_z):
        ref = give_ref if t % 2 else keep_ref
        ref[t // 2] = kept_ref[z ^ t] + got_ref[z ^ t]


def unpack_kernel(n_row, n_col, *refs):
    out_ref = refs[-1]
    row = lax.axis_index("row")
    owner = row * n_col + lax.axis_index("col")
    total = tree_sum([r[0] for r in refs[:-1]])
    half, width = total.shape
    mode = out_ref.shape[1]
    group = width - mode
    r = lax.broadcasted_iota(jnp.int32, (half, mode), 0)
    c = lax.broadcasted_iota(jnp.int32, (half, mode), 1)
    out_ref[half:, :] = jnp.where(c <= mode - (owner + 1) * half + r, total[:, :mode], F32(0.0))
    out_ref[:half, :] = jnp.zeros((half, mode), F32)
    for k in range(n_row):

        @pl.when(row == k)
        def _():
            start, stop = mode - k * group, mode + group
            keep = c[:, : stop - start] <= owner * half + r[:, : stop - start]
            out_ref[:half, : stop - start] = jnp.where(keep, total[:, start:stop], F32(0.0))


def body(unfolding, factor):
    n_row = lax.axis_size("row")
    n_col = lax.axis_size("col")
    n_z = n_col // 2
    rows_here, cols_here = unfolding.shape
    mode = rows_here * n_row
    rank = factor.shape[1]
    hr = rank // 2
    scale = 1.0 / (cols_here * n_col)
    group = rows_here // 2
    half = group // n_col
    width = mode + group

    def over_row(x, s):
        return lax.ppermute(x, "row", [(i, i ^ s) for i in range(n_row)])

    def over_side(x, s):
        pairs = [((r, c), (r ^ (3 - s if c % 2 else s), c)) for r in range(n_row) for c in range(n_col)]
        return lax.ppermute(x, ("row", "col"), [(a * n_col + b, p * n_col + q) for (a, b), (p, q) in pairs])

    def over_col(x, s):
        return lax.ppermute(x, "col", [(i, i ^ s) for i in range(n_col)])

    def steps(n):
        return [1 << k for k in range(n.bit_length() - 1)]

    y_shape = jax.ShapeDtypeStruct((rank, cols_here), F32)
    part_shape = jax.ShapeDtypeStruct((group, cols_here), F32)
    project = functools.partial(project_kernel, rows_here)
    if n_row == 4:
        y, upper, lower = call(
            project,
            (y_shape, part_shape, part_shape),
            factor.T,
            unfolding,
            work=COST["project"],
            name="project",
        )
        got = over_side(y, 1)
        two_low = over_side(lower, 2)
        one_up = over_side(upper, 1)
        one_low = over_side(lower, 1)
        y, upper = call(
            join_kernel, (y_shape, part_shape), y, got, upper, work=COST["join"], name="join"
        )
        y_got = over_side(y, 2)
        two_up = over_side(upper, 2)
        three = [over_side(one_up, 2), over_side(two_low, 1)]
        blocks = [[unfolding], [one_up, one_low], [two_up, two_low], three]
    else:
        (y,) = call(project, (y_shape,), factor.T, unfolding, work=COST["project"], name="project")
        for s in steps(n_row)[:-1]:
            y = y + over_row(y, s)
        y_got = over_row(y, n_row // 2)
        blocks = [[unfolding]] + [[over_row(unfolding, s)] for s in range(1, n_row)]
    counts = tuple(len(b) for b in blocks)
    blocks = [p for b in blocks for p in b]

    kept, given = call(
        functools.partial(term_kernel, scale),
        (jax.ShapeDtypeStruct((hr, rows_here), F32),) * 2,
        unfolding,
        y,
        y_got,
        work=COST["term"],
        name="term",
    )
    image = call(
        sum_kernel,
        jax.ShapeDtypeStruct((hr, rows_here), F32),
        kept,
        over_col(given, 1),
        work=COST["core_sum"],
        name="core_sum",
    )

    def z_sum(image, s, after):
        return call(
            sum_kernel,
            jax.ShapeDtypeStruct((hr, rows_here), F32),
            image,
            over_col(image, 2 * s),
            after=after,
            work=COST["sum"],
            name="z_sum",
        )

    for s in steps(n_z):
        image = z_sum(image, s, [])

    given, kept = call(
        functools.partial(gram_kernel, n_row, n_col, scale, counts),
        (jax.ShapeDtypeStruct((n_z, half, width), F32),) * 2,
        *blocks,
        scratch=[
            pltpu.VMEM((2 * n_row, group, cols_here), BF16),
            pltpu.VMEM((2 * n_row, group, cols_here), BF16),
            pltpu.VMEM((2, 2 * n_row, n_col, half, group), F32),
        ],
        after=[image],
        work=COST["gram"],
        name="gram",
    )
    mine = image[None]
    for s in steps(n_row):
        mine = call(
            stack_kernel,
            jax.ShapeDtypeStruct((2 * s, hr, rows_here), F32),
            mine,
            over_row(mine, s),
            after=[given] if s == 1 else [],
            work=COST["stack"],
            name="stack",
        )
    other = over_col(mine, 1)

    rank_here = rank // n_row
    whole = rows_here % 128 == 0
    nf, core_out = call(
        functools.partial(finish_kernel, n_row, counts),
        (
            jax.ShapeDtypeStruct((rank, mode) if whole else (n_row, rank, rows_here), F32),
            jax.ShapeDtypeStruct((rank_here, cols_here), F32),
        ),
        mine,
        other,
        *blocks,
        scratch=[pltpu.VMEM((n_row, rank_here, rank), F32)],
        work=COST["finish"],
        name="finish",
    )
    new_factor = nf.T if whole else nf.transpose(0, 2, 1).reshape(mode, rank)

    keep, give = call(
        functools.partial(pieces_kernel, n_z),
        (jax.ShapeDtypeStruct((n_z // 2, half, width), F32),) * 2,
        kept,
        over_col(given, 1),
        work=COST["pieces"],
        name="pieces",
    )
    got = over_col(give, 2)
    for s in steps(n_z)[1:]:
        keep, give = keep[0::2] + got[0::2], keep[1::2] + got[1::2]
        got = over_col(give, 2 * s)
    gram_lower = call(
        functools.partial(unpack_kernel, n_row, n_col),
        jax.ShapeDtypeStruct((2 * half, mode), F32),
        keep,
        got,
        work=COST["unpack"],
        name="unpack",
    )
    return gram_lower, new_factor, core_out


def solution(mesh):
    in_specs = (P("row", "col"), P())
    out_specs = (P(("row", "col"), None), P(), P("row", "col"))
    return jax.shard_map(body, mesh=mesh, in_specs=in_specs, out_specs=out_specs, check_vma=False)
```
